32 devices in a mesh: corpus: 8 (over z, y), blk: 4 (over x, core).
Axes of the slice: x: 2, y: 2, z: 4, core: 2. Of those that a mesh axis runs over, the one named last changes fastest.
Arguments:
- queries: bfloat16 [512, 32, 128], P(('corpus', 'blk')), may hold values from -0.0625 to 0.0625
- index: bfloat16 [4096, 128, 128], P('corpus'), may hold values from -6 to 6
- cand_owner: int32 [512, 64, 1], P(('corpus', 'blk')), may hold values from 0 to 7; in each aligned block of 1024 rows (0 to 1023, 1024 to 2047, ..., all dimensions but the last counted through in order) at most 256 rows name the same one
- cand_row: int32 [512, 64], P(('corpus', 'blk')), may hold values from 0 to 511
- neg_row: int32 [32, 24], P(('corpus', 'blk')), may hold values from 0 to 511
- teacher: float32 [512, 64], P(('corpus', 'blk')), may hold values from -16 to 16
Outputs:
- losses: float32 [512], P(('corpus', 'blk'))
- query_grads: float32 [512, 32, 128], P(('corpus', 'blk'))
The draws below stay inside these ranges and needn't reach their ends.
Inputs may be any that keep to these rules, and one draw needn't show every extreme that they name: `cand_owner`: among the 1024 candidates of one device, no owner shard is named more than 256 times, and some owner shard is named exactly 256 times.
All inputs are finite; a program needn't handle non-finite values.
Results may differ from the reference program's by a relative error of at most 0.007.
Values may be sent and summed in bfloat16 or wider, within the bound.
No kernel may reach another device: no remote copies, remote signals or barrier semaphores. Data moves between devices by JAX's collectives and lax.ppermute only.
A program may use at most 256 MiB of HBM per device.

```python
import math
import jax
import jax.numpy as jnp
import numpy as np
from jax import lax

DIM = 128
QT = 32
PT = 128
NCAND = 64
NEG = 24
QDEV = 16
PASS_DEV = 512
NQ = 512
PASSAGES = 4096
CAP = 256
N_CORPUS = 8
N_BLK = 4
DEVICES = 32


def place_ends(values, rng, least, high):
    longest = values.shape.index(max(values.shape))
    spots = []
    for shift in (0, 1):
        where = [jax.random.randint(jax.random.fold_in(rng, axis), (), 0, length) for axis, length in enumerate(values.shape)]
        where[longest] = (where[longest] + shift) % values.shape[longest]
        spots.append(tuple(where))
    return values.at[spots[0]].set(least).at[spots[1]].set(high)


def shard_levels(key, dims, split, least, high):
    loudness = 1.0
    for dim, shards_of in split:
        steps = jax.random.uniform(jax.random.fold_in(jax.random.fold_in(key, 6), dim), (shards_of,), jnp.float32, least / len(split), high / len(split))
        loudness = loudness * jnp.repeat(jnp.exp(steps), dims[dim] // shards_of).reshape((-1,) + (1,) * (len(dims) - 1 - dim))
    return loudness


def assign_block(rng, own, number, rows, number_of, top, reach, slope):
    ranking = jax.random.permutation(rng, number_of)
    crowded, common = shares(number_of, rows * top, reach, slope, True), shares(number_of, rows * top, reach, slope, False)
    places = jnp.arange(number_of)

    def named(lengths, offset_by):
        used = int((lengths > 0).sum())
        fixed = max(1, used // 4)
        moved = fixed + (places - fixed + offset_by * (used - fixed)) % max(1, number_of - fixed)
        return jnp.zeros((number_of,), jnp.int32).at[ranking[jnp.where(places < fixed, places, moved)]].set(jnp.asarray(lengths, jnp.int32))

    lengths = jnp.where(number % 4 == 0, named(crowded, number // 4), named(common, number - number // 4 - 1))
    mixed = jax.random.permutation(jax.random.fold_in(own, 3), number_of)
    donor, sink = mixed[0:number_of // 2 * 2:2], mixed[1:number_of // 2 * 2:2]
    slack = jnp.minimum(lengths[donor] - 1, reach - lengths[sink]) // 2
    slack = jnp.where((donor == ranking[0]) | (sink == ranking[0]) | (lengths[sink] == 0), 0, jnp.maximum(slack, 0))
    moved = jax.random.randint(jax.random.fold_in(own, 4), (number_of // 2,), 0, 1 << 20) % (slack + 1)
    lengths = lengths.at[donor].add(-moved).at[sink].add(moved)
    items = jnp.searchsorted(jnp.cumsum(lengths), jnp.arange(rows * top), side="right").astype(jnp.int32)
    grid = items.reshape(top, rows).T
    grid = grid[jax.random.permutation(jax.random.fold_in(own, 1), rows)]
    offset_by = jax.random.randint(jax.random.fold_in(own, 2), (rows, 1), 0, top)
    return jnp.take_along_axis(grid, (jnp.arange(top)[None, :] + offset_by) % top, axis=1)


def shares(amount, total, most, skew, full):
    portions = [(1 << 20) // math.isqrt(grade ** skew) + 1 for grade in range(1, amount + 1)]
    largest = most if full else min(most, max(-(-total // amount), total * portions[0] // sum(portions)))
    least = 1 if total - largest >= amount - 1 else 0
    holding, spare = [largest] + [least] * (amount - 1), total - largest - least * (amount - 1)
    while spare > 0:
        free = [i for i in range(1, amount) if holding[i] < largest] or [i for i in range(1, amount) if holding[i] < most]
        pool, left = sum([portions[i] for i in free]), spare
        for i in free:
            more = min(most - holding[i], max(1, left * portions[i] // pool), spare)
            holding[i] = holding[i] + more
            spare = spare - more
    return np.array(holding)


def centred(rng, dims, scale, reach, shards=(), kind=jnp.bfloat16):
    level = shard_levels(rng, dims, shards, -0.22, 0.18) if shards else 1.0
    entries = jax.random.normal(rng, dims, jnp.float32) * scale * level
    return jnp.minimum(jnp.maximum(entries, -reach), reach).astype(kind)


def setup_inputs(seed: int = 0) -> dict:
    arg_keys = jax.random.split(jax.random.key(seed), 7)
    queries = centred(arg_keys[0], (NQ, QT, DIM), 0.01, 0.0625, ((0, 32),))
    index = centred(arg_keys[1], (PASSAGES, PT, DIM), 1.0, 6.0, ((0, 8),))
    cand_owner_keys = jax.random.split(jax.random.fold_in(arg_keys[2], 1), NQ * NCAND // (QDEV * NCAND))
    cand_owner_turns = jax.random.permutation(jax.random.fold_in(arg_keys[2], 3), NQ * NCAND // (QDEV * NCAND))
    cand_owner = jax.vmap(lambda own, number: assign_block(jax.random.fold_in(arg_keys[2], 2), own, number, QDEV * NCAND, N_CORPUS, 1, CAP, 2))(cand_owner_keys, cand_owner_turns).reshape((NQ, NCAND, 1))
    cand_row = place_ends(jax.random.randint(arg_keys[3], (NQ, NCAND), 0, PASS_DEV), jax.random.fold_in(arg_keys[3], 1), 0, PASS_DEV - 1).astype(jnp.int32)
    neg_row = place_ends(jax.random.randint(arg_keys[4], (DEVICES, NEG), 0, PASS_DEV), jax.random.fold_in(arg_keys[4], 1), 0, PASS_DEV - 1).astype(jnp.int32)
    teacher = centred(arg_keys[5], (NQ, NCAND), 3.0, 16.0, ((0, 32),), jnp.float32)
    return dict(queries=queries, index=index, cand_owner=cand_owner, cand_row=cand_row, neg_row=neg_row, teacher=teacher)


inner_temp = 0.1
epsilon = 1e-06

def soft_terms(raw, inverse):
    scaled = raw * inverse
    expo = jnp.exp(scaled / inner_temp)
    totals = lax.optimization_barrier(jnp.sum(expo, axis=-1, keepdims=True))
    score = inner_temp * lax.optimization_barrier(jnp.sum(jnp.log(totals[..., 0]), axis=-1))
    weights = (expo / totals * inverse).astype(jnp.bfloat16)
    return (score, weights)

def tile_inverse(tiles):
    wide = tiles.astype(jnp.float32)
    return lax.rsqrt(lax.optimization_barrier(jnp.sum(wide * wide, axis=-1)) + epsilon)

def one_query(query, tiles, teacher_row):
    widened = query.astype(jnp.float32)
    radius = jnp.sqrt(lax.optimization_barrier(jnp.sum(widened * widened, axis=-1, keepdims=True)) + epsilon)
    unit = widened / radius
    rounded = unit.astype(jnp.bfloat16)
    wide_tiles = tiles.astype(jnp.float32)
    raw = jnp.einsum('id,pjd->pij', rounded.astype(jnp.float32), wide_tiles)
    inverse = tile_inverse(tiles)[:, None, :]
    score, weights = soft_terms(raw, inverse)
    back = jnp.einsum('pij,pjd->pid', weights.astype(jnp.float32), wide_tiles)
    cands = score[:NCAND]
    negs = score[NCAND:]
    total = jnp.sum(jnp.exp(cands)) + jnp.sum(jnp.exp(negs))
    spread = jnp.log(total)
    log_target = teacher_row - jnp.log(jnp.sum(jnp.exp(teacher_row)))
    target = jnp.exp(log_target)
    loss = jnp.sum(target * (log_target - cands + spread))
    grads_score = jnp.concatenate([jnp.exp(cands - spread) - target, jnp.exp(negs - spread)])
    pulled = lax.optimization_barrier(jnp.sum(grads_score[:, None, None] * back, axis=0))
    result = (pulled - unit * lax.optimization_barrier(jnp.sum(unit * pulled, axis=-1, keepdims=True))) / radius
    return (loss, result)

def reference(queries, index, cand_owner, cand_row, neg_row, teacher):
    numbers = jnp.arange(NQ, dtype=jnp.int32)

    def handle(number):
        shard = (number // QDEV // N_BLK).astype(jnp.int32)
        listed = cand_owner[number, :, 0] * PASS_DEV + cand_row[number]
        sampled = lax.dynamic_slice_in_dim(neg_row, (shard * N_BLK).astype(jnp.int32), N_BLK, 0).reshape(-1) + shard * PASS_DEV
        tiles = index[jnp.concatenate([listed, sampled]).astype(jnp.int32)]
        return one_query(queries[number], tiles, teacher[number])
    losses, grads = lax.map(handle, numbers)
    return (losses, grads)
```

```python
import functools

import jax
import jax.numpy as jnp
from jax import lax
from jax.experimental import pallas as pl
from jax.experimental.pallas import tpu as pltpu
from jax.sharding import PartitionSpec as P

inner_temp = 0.1
epsilon = 1e-06
LOG2E = 1.4426950408889634
GROUP = 4
UNITS = 4
SLOTS = 3
NEG_STEP = 2
VMEM_LIMIT = 48 * 1024 * 1024
LAST = (((1,), (1,)), ((), ()))


def dot_last(a, b):
    return lax.dot_general(a, b, LAST, preferred_element_type=jnp.float32)


def dot(a, b):
    return jnp.dot(a, b, preferred_element_type=jnp.float32)


def split3(x):
    high = x.astype(jnp.bfloat16)
    rest = x - high.astype(jnp.float32)
    mid = rest.astype(jnp.bfloat16)
    low = (rest - mid.astype(jnp.float32)).astype(jnp.bfloat16)
    return high, mid, low


def rounded_queries(raw):
    wide = raw.astype(jnp.float32)
    radius = jnp.sqrt(jnp.sum(wide * wide, axis=-1, keepdims=True) + epsilon)
    return (wide / radius).astype(jnp.bfloat16)


def norm_kernel(tiles_ref, out_ref):
    count, tokens, _ = tiles_ref.shape
    sub = lax.broadcasted_iota(jnp.int32, (8, tokens), 0)
    lane = lax.broadcasted_iota(jnp.int32, (8, tokens), 1)
    block = lane // 8
    chosen = sub == lane % 8

    def body(step, carry):
        rows = []
        for k in range(8):
            tile = tiles_ref[step * 8 + k]
            gram = dot_last(tile, tile)
            acc = gram[0:8]
            for r in range(1, tokens // 8):
                acc = jnp.where(block == r, gram[8 * r : 8 * r + 8], acc)
            rows.append(jnp.sum(jnp.where(chosen, acc, 0.0), axis=0, keepdims=True))
        squares = jnp.concatenate(rows, axis=0)
        out_ref[pl.ds(pl.multiple_of(step * 8, 8), 8), :] = lax.rsqrt(squares + epsilon)
        return carry

    lax.fori_loop(0, count // 8, body, 0)


def norms(index):
    count, tokens, dim = index.shape
    block = min(count, 64)
    return pl.pallas_call(
        norm_kernel,
        grid=(count // block,),
        in_specs=[pl.BlockSpec((block, tokens, dim), lambda i: (i, 0, 0))],
        out_specs=pl.BlockSpec((block, tokens), lambda i: (i, 0)),
        out_shape=jax.ShapeDtypeStruct((count, tokens), jnp.float32),
        compiler_params=pltpu.CompilerParams(vmem_limit_bytes=VMEM_LIMIT),
        cost_estimate=pl.CostEstimate(
            flops=2 * count * tokens * tokens * dim,
            bytes_accessed=2 * count * tokens * dim,
            transcendentals=count * tokens,
        ),
        name="norms",
    )(index)


def prep_kernel(me_ref, meta_ref, rows_ref, target_ref, value_ref, place_ref, result_ref, *, shard, cands):
    count = meta_ref.shape[0]
    code = meta_ref[:, :cands]
    owner = jnp.floor((code + 0.5) * (1.0 / shard))
    row = code - owner * shard
    teacher = meta_ref[:, cands:]
    log_target = teacher - jnp.log(jnp.sum(jnp.exp(teacher), axis=-1, keepdims=True))
    target = jnp.exp(log_target)
    mine = (owner == me_ref[0].astype(jnp.float32)).astype(jnp.float32)
    before = lax.broadcasted_iota(jnp.int32, (cands, cands), 0) < lax.broadcasted_iota(
        jnp.int32, (cands, cands), 1
    )
    place = dot(mine.astype(jnp.bfloat16), before.astype(jnp.float32).astype(jnp.bfloat16))
    wide = value_ref.shape[1]
    pad = jnp.zeros((count, wide - cands), jnp.float32)
    place_ref[...] = jnp.concatenate([jnp.where(mine > 0, place, -1.0), pad - 1.0], axis=1)
    row_high = jnp.floor(row * (1.0 / 16))
    first, second, third = split3(target)
    values = [row_high, row - 16 * row_high, first, second, third]
    for v in range(8):
        value = values[v].astype(jnp.float32) if v < len(values) else jnp.zeros_like(row)
        value_ref[pl.ds(v, count, stride=8), :] = jnp.concatenate([value, pad], axis=1)
    spots = lax.broadcasted_iota(jnp.int32, (wide, wide), 0).astype(jnp.float32)

    def body(step, carry):
        for k in range(8):
            q = step * 8 + k
            hot = jnp.where(place_ref[pl.ds(q, 1), :] == spots, 1.0, 0.0).astype(jnp.bfloat16)
            at = pl.ds(pl.multiple_of(q * 8, 8), 8)
            result_ref[at, :] = dot_last(value_ref[at, :].astype(jnp.bfloat16), hot)
        return carry

    lax.fori_loop(0, count // 8, body, 0)
    result = [result_ref[pl.ds(v, count, stride=8), :] for v in range(5)]
    found = jnp.sum(mine, axis=-1, keepdims=True)
    lane = lax.broadcasted_iota(jnp.int32, (count, wide), 1)
    rows = 16 * result[0] + result[1]
    rows_ref[...] = jnp.where(lane < cands, rows, found).astype(jnp.int32)
    target_ref[...] = result[2] + result[3] + result[4]


def prep(me, meta, shard, cands):
    count = meta.shape[0]
    wide = 128
    return pl.pallas_call(
        functools.partial(prep_kernel, shard=shard, cands=cands),
        in_specs=[
            pl.BlockSpec(memory_space=pltpu.SMEM),
            pl.BlockSpec(memory_space=pltpu.VMEM),
        ],
        out_specs=[pl.BlockSpec(memory_space=pltpu.VMEM)] * 2,
        out_shape=[
            jax.ShapeDtypeStruct((count, wide), jnp.int32),
            jax.ShapeDtypeStruct((count, wide), jnp.float32),
        ],
        scratch_shapes=[
            pltpu.VMEM((count * 8, wide), jnp.float32),
            pltpu.VMEM((count, wide), jnp.float32),
            pltpu.VMEM((count * 8, wide), jnp.float32),
        ],
        compiler_params=pltpu.CompilerParams(vmem_limit_bytes=VMEM_LIMIT),
        name="prep",
    )(me, meta)


def score_terms(totals):
    product = (totals[0:8] * totals[8:16]) * (totals[16:24] * totals[24:32])
    return inner_temp * jnp.sum(jnp.log(product), axis=0, keepdims=True)


def pair_kernel(source_ref, rows_ref, target_ref, queries_ref, inverse_ref, index_ref, out_ref,
                units_ref, unit_ref, acc_ref, score_ref, buffer_ref, sems, *, cands):
    count, tokens = queries_ref.shape[0], queries_ref.shape[1]
    wide = rows_ref.shape[1]
    step_pairs = UNITS * GROUP
    for q in range(count):
        unit_ref[q] = rounded_queries(queries_ref[q])
    acc_ref[...] = jnp.zeros_like(acc_ref)
    score_ref[...] = jnp.zeros_like(score_ref)
    total = jnp.int32(0)
    for q in range(count):
        for t in range(cands // GROUP):
            units_ref[total + t] = jnp.int32(q * wide + t * GROUP)
        total = total + (rows_ref[q, cands] + (GROUP - 1)) // GROUP
    for t in range(UNITS):
        units_ref[total + t] = jnp.int32(0)
    steps = (total + (UNITS - 1)) // UNITS

    def entry(u):
        code = units_ref[u]
        return code // wide, code % wide

    def start(step):
        slot = lax.rem(step, SLOTS)
        for u in range(UNITS):
            q, base = entry(step * UNITS + u)
            for g in range(GROUP):
                row = rows_ref[q, base + g]
                pltpu.make_async_copy(
                    index_ref.at[row], buffer_ref.at[slot, u * GROUP + g], sems.at[slot]
                ).start()

    for ahead in range(SLOTS - 1):
        @pl.when(ahead < steps)
        def _():
            start(jnp.int32(ahead))

    lane = lax.broadcasted_iota(jnp.int32, (1, wide), 1)

    def body(step, carry):
        @pl.when(step + (SLOTS - 1) < steps)
        def _():
            start(step + (SLOTS - 1))

        slot = lax.rem(step, SLOTS)
        pltpu.make_async_copy(
            index_ref.at[pl.ds(0, step_pairs)], buffer_ref.at[slot], sems.at[slot]
        ).wait()
        for u in range(UNITS):
            number = step * UNITS + u
            q, base = entry(number)
            found = jnp.where(number < total, rows_ref[q, cands], 0)
            tiles = buffer_ref[slot, u * GROUP : (u + 1) * GROUP].reshape(GROUP * wide, wide)
            raw = dot_last(unit_ref[q], tiles)
            left, right = [], []
            sums = jnp.zeros((1, wide), jnp.float32)
            for g in range(GROUP):
                row = rows_ref[q, base + g]
                valid = jnp.where(base + g < found, 1.0, 0.0).astype(jnp.float32)
                target = target_ref[q, base + g] * valid
                inverse = inverse_ref[pl.ds(row, 1), :]
                expo = jnp.exp2(raw[:, g * wide : (g + 1) * wide] * (inverse * (LOG2E / inner_temp)))
                totals = jnp.sum(expo, axis=-1, keepdims=True)
                score = score_terms(totals)
                lift = jnp.exp(score) * valid
                weights = expo * inverse
                recip = 1.0 / totals
                left.append((weights * (recip * lift)).astype(jnp.bfloat16))
                right.append((weights * (recip * target)).astype(jnp.bfloat16))
                sums = sums + jnp.where(lane < wide // 2, lift, score * target)
            both = jnp.concatenate(
                [jnp.concatenate(left, axis=1), jnp.concatenate(right, axis=1)], axis=0
            )
            acc_ref[q] += dot(both, tiles)
            score_ref[pl.ds(q, 1), :] += sums
        return carry

    lax.fori_loop(0, steps, body, 0)
    for q in range(count):
        out_ref[pl.ds(q * 2 * tokens, 2 * tokens), :] = acc_ref[q].astype(jnp.bfloat16)
    for k, part in enumerate(split3(score_ref[...])):
        out_ref[pl.ds(count * 2 * tokens + k * count, count), :] = part


def pairs(source, rows, targets, queries, inverse, index, count, cands, room):
    tokens, dim = queries.shape[1:]
    wide = rows.shape[1]
    height = count * 2 * tokens + 3 * count
    return pl.pallas_call(
        functools.partial(pair_kernel, cands=cands),
        grid_spec=pltpu.PrefetchScalarGridSpec(
            num_scalar_prefetch=1,
            grid=(1,),
            in_specs=[
                pl.BlockSpec((count, wide), lambda i, s: (s[0], 0), memory_space=pltpu.SMEM),
                pl.BlockSpec((count, wide), lambda i, s: (s[0], 0), memory_space=pltpu.SMEM),
                pl.BlockSpec((count, tokens, dim), lambda i, s: (s[0], 0, 0)),
                pl.BlockSpec(memory_space=pltpu.VMEM),
                pl.BlockSpec(memory_space=pl.ANY),
            ],
            out_specs=pl.BlockSpec((height, dim), lambda i, s: (0, 0)),
            scratch_shapes=[
                pltpu.SMEM((count * (cands // GROUP) + cands + UNITS,), jnp.int32),
                pltpu.VMEM((count, tokens, dim), jnp.bfloat16),
                pltpu.VMEM((count, 2 * tokens, dim), jnp.float32),
                pltpu.VMEM((count, wide), jnp.float32),
                pltpu.VMEM((SLOTS, UNITS * GROUP) + index.shape[1:], jnp.bfloat16),
                pltpu.SemaphoreType.DMA((SLOTS,)),
            ],
        ),
        out_shape=jax.ShapeDtypeStruct((height, dim), jnp.bfloat16),
        compiler_params=pltpu.CompilerParams(vmem_limit_bytes=VMEM_LIMIT),
        cost_estimate=pl.CostEstimate(
            flops=6 * room * tokens * wide * dim,
            bytes_accessed=2 * room * wide * dim,
            transcendentals=room * tokens * wide,
        ),
        name="pairs",
    )(source, rows, targets, queries, inverse, index)


def neg_kernel(rows_ref, queries_ref, inverse_ref, index_ref, acc_ref, score_ref, unit_ref, buffer_ref, sem):
    total = rows_ref.shape[0]
    height, dim = queries_ref.shape
    tokens = 32
    chunk = min(height, 128)
    for k in range(total):
        pltpu.make_async_copy(index_ref.at[rows_ref[k]], buffer_ref.at[k], sem).start()
    unit_ref[...] = rounded_queries(queries_ref[...])
    acc_ref[...] = jnp.zeros_like(acc_ref)
    score_ref[...] = jnp.zeros_like(score_ref)
    pltpu.make_async_copy(index_ref.at[pl.ds(0, total)], buffer_ref, sem).wait()
    wide = buffer_ref.shape[1]

    def body(step, carry):
        tiles = buffer_ref[pl.ds(step * NEG_STEP, NEG_STEP)].reshape(NEG_STEP * wide, dim)
        inverses = [
            inverse_ref[pl.ds(rows_ref[step * NEG_STEP + g], 1), :] for g in range(NEG_STEP)
        ]
        for c in range(height // chunk):
            raw = dot_last(unit_ref[c * chunk : (c + 1) * chunk], tiles)
            left = []
            lifts = [0.0] * (chunk // tokens)
            for g in range(NEG_STEP):
                inverse = inverses[g]
                expo = jnp.exp2(raw[:, g * wide : (g + 1) * wide] * (inverse * (LOG2E / inner_temp)))
                totals = jnp.sum(expo, axis=-1, keepdims=True)
                recip = 1.0 / totals
                weights = expo * inverse
                for q in range(chunk // tokens):
                    part = slice(q * tokens, (q + 1) * tokens)
                    lift = jnp.exp(score_terms(totals[part]))
                    lifts[q] = lifts[q] + lift
                    left.append((weights[part] * (recip[part] * lift)).astype(jnp.bfloat16))
            half = chunk // tokens
            both = jnp.concatenate(
                [jnp.concatenate(left[g * half : (g + 1) * half], axis=0) for g in range(NEG_STEP)],
                axis=1,
            )
            acc_ref[c * chunk : (c + 1) * chunk] += dot(both, tiles)
            for q in range(chunk // tokens):
                at = pl.ds(c * (chunk // tokens) + q, 1)
                score_ref[at, :] += jnp.broadcast_to(lifts[q], (1, wide))
        return carry

    lax.fori_loop(0, total // NEG_STEP, body, 0)


def negatives(rows, queries, inverse, index):
    total = rows.shape[0]
    count, tokens, dim = queries.shape
    wide = index.shape[1]
    return pl.pallas_call(
        neg_kernel,
        in_specs=[
            pl.BlockSpec(memory_space=pltpu.SMEM),
            pl.BlockSpec(memory_space=pltpu.VMEM),
            pl.BlockSpec(memory_space=pltpu.VMEM),
            pl.BlockSpec(memory_space=pl.ANY),
        ],
        out_specs=[pl.BlockSpec(memory_space=pltpu.VMEM)] * 2,
        out_shape=[
            jax.ShapeDtypeStruct((count * tokens, dim), jnp.float32),
            jax.ShapeDtypeStruct((count, wide), jnp.float32),
        ],
        scratch_shapes=[
            pltpu.VMEM((count * tokens, dim), jnp.bfloat16),
            pltpu.VMEM((total, wide, dim), jnp.bfloat16),
            pltpu.SemaphoreType.DMA,
        ],
        compiler_params=pltpu.CompilerParams(vmem_limit_bytes=VMEM_LIMIT),
        cost_estimate=pl.CostEstimate(
            flops=4 * total * count * tokens * wide * dim,
            bytes_accessed=2 * total * wide * dim,
            transcendentals=total * count * tokens * wide,
        ),
        name="negatives",
    )(rows, queries.reshape(count * tokens, dim), inverse, index)


def on_device(queries, index, cand_owner, cand_row, neg_row, teacher):
    count, tokens, dim = queries.shape
    cands = cand_row.shape[1]
    shard = index.shape[0]
    owners = lax.axis_size("corpus")
    room = (2 * count * cands + owners - 1) // owners
    me = lax.axis_index("corpus").astype(jnp.int32)
    code = (cand_owner[..., 0] * shard + cand_row).astype(jnp.float32)
    meta = jnp.concatenate([code, teacher], axis=1)
    all_meta = lax.all_gather(meta, "corpus", axis=0, tiled=True)
    all_queries = lax.all_gather(queries, "corpus", axis=0, tiled=True)
    all_neg = lax.all_gather(neg_row, "blk", axis=0, tiled=True).reshape(-1)
    inverse = norms(index)
    neg_acc, neg_sum = negatives(all_neg, queries, inverse, index)
    rows, targets = prep(me.reshape(1), all_meta, shard, cands)
    messages = []
    for step in reversed(range(owners)):
        source = lax.rem(me + step, owners)
        message = pairs(
            source.reshape(1), rows, targets, all_queries, inverse, index, count, cands, room
        )
        if step:
            message = lax.ppermute(
                message, "corpus", [(i, (i + step) % owners) for i in range(owners)]
            )
        messages.append(message)
    cut = count * 2 * tokens
    both = sum(m[:cut].astype(jnp.float32) for m in messages).reshape(count, 2, tokens, dim)
    scores = sum(m[cut:].astype(jnp.float32) for m in messages).reshape(3, count, dim).sum(axis=0)
    total = scores[:, 0] + neg_sum[:, 0]
    spread = jnp.log(total)
    log_target = teacher - jnp.log(jnp.sum(jnp.exp(teacher), axis=1, keepdims=True))
    target = jnp.exp(log_target)
    losses = jnp.sum(target * (log_target + spread[:, None]), axis=1) - scores[:, dim // 2]
    pulled = (both[:, 0] + neg_acc.reshape(count, tokens, dim)) / total[:, None, None] - both[:, 1]
    widened = queries.astype(jnp.float32)
    radius = jnp.sqrt(jnp.sum(widened * widened, axis=-1, keepdims=True) + epsilon)
    unit = widened / radius
    query_grads = (pulled - unit * jnp.sum(unit * pulled, axis=-1, keepdims=True)) / radius
    return (losses, query_grads)


def solution(mesh):
    placed = (
        P(("corpus", "blk"), None, None),
        P("corpus", None, None),
        P(("corpus", "blk"), None, None),
        P(("corpus", "blk"), None),
        P(("corpus", "blk"), None),
        P(("corpus", "blk"), None),
    )
    return jax.shard_map(
        on_device,
        mesh=mesh,
        in_specs=placed,
        out_specs=(P(("corpus", "blk")), P(("corpus", "blk"), None, None)),
        check_vma=False,
    )
```

```python
import functools
import math

import jax
import jax.numpy as jnp
from jax import lax
from jax.experimental import pallas as pl
from jax.experimental.pallas import tpu as pltpu
from jax.sharding import PartitionSpec as P

inner_temp = 0.1
epsilon = 1e-06
LOG2E = 1.4426950408889634
GROUP = 4
UNITS = 8
NEG_STEP = 8
NEG_CHUNK = 96
MIB = 1024 * 1024
LAST = (((1,), (1,)), ((), ()))


def dot_last(a, b):
    return lax.dot_general(a, b, LAST, preferred_element_type=jnp.float32)


def dot(a, b):
    return jnp.dot(a, b, preferred_element_type=jnp.float32)


def split3(x):
    high = x.astype(jnp.bfloat16)
    rest = x - high.astype(jnp.float32)
    mid = rest.astype(jnp.bfloat16)
    low = (rest - mid.astype(jnp.float32)).astype(jnp.bfloat16)
    return high, mid, low


def rounded_queries(raw):
    wide = raw.astype(jnp.float32)
    radius = jnp.sqrt(jnp.sum(wide * wide, axis=-1, keepdims=True) + epsilon)
    return (wide / radius).astype(jnp.bfloat16)


def norm_kernel(index_ref, out_ref):
    count, tokens, dim = index_ref.shape
    ones = jnp.ones((8, dim), jnp.bfloat16)
    sub = lax.broadcasted_iota(jnp.int32, (8, tokens), 0)

    def body(step, carry):
        squares = jnp.zeros((8, tokens), jnp.float32)
        for k in range(8):
            tile = index_ref[step * 8 + k].astype(jnp.float32)
            tile = tile * tile
            high = tile.astype(jnp.bfloat16)
            low = (tile - high.astype(jnp.float32)).astype(jnp.bfloat16)
            squares = jnp.where(sub == k, dot_last(ones, high) + dot_last(ones, low), squares)
        out_ref[pl.ds(pl.multiple_of(step * 8, 8), 8), :] = lax.rsqrt(squares + epsilon)
        return carry

    lax.fori_loop(0, count // 8, body, 0, unroll=2)


def norms(index):
    count, tokens, dim = index.shape
    return pl.pallas_call(
        norm_kernel,
        in_specs=[pl.BlockSpec(memory_space=pltpu.VMEM)],
        out_specs=pl.BlockSpec(memory_space=pltpu.VMEM),
        out_shape=jax.ShapeDtypeStruct((count, tokens), jnp.float32),
        compiler_params=pltpu.CompilerParams(vmem_limit_bytes=8 * MIB),
        cost_estimate=pl.CostEstimate(
            flops=32 * count * tokens * dim,
            bytes_accessed=2 * count * tokens * dim,
            transcendentals=count * tokens,
        ),
        name="norms",
    )(index)


def prep_kernel(me_ref, meta_ref, rows_ref, target_ref, value_ref, place_ref, result_ref, *, shard, cands):
    count = meta_ref.shape[0]
    code = meta_ref[:, :cands]
    owner = jnp.floor((code + 0.5) * (1.0 / shard))
    row = code - owner * shard
    teacher = meta_ref[:, cands:]
    log_target = teacher - jnp.log(jnp.sum(jnp.exp(teacher), axis=-1, keepdims=True))
    target = jnp.exp(log_target)
    mine = (owner == me_ref[0].astype(jnp.float32)).astype(jnp.float32)
    before = lax.broadcasted_iota(jnp.int32, (cands, cands), 0) < lax.broadcasted_iota(
        jnp.int32, (cands, cands), 1
    )
    place = dot(mine.astype(jnp.bfloat16), before.astype(jnp.float32).astype(jnp.bfloat16))
    wide = value_ref.shape[1]
    pad = jnp.zeros((count, wide - cands), jnp.float32)
    place_ref[...] = jnp.concatenate([jnp.where(mine > 0, place, -1.0), pad - 1.0], axis=1)
    row_high = jnp.floor(row * (1.0 / 16))
    first, second, third = split3(target)
    values = [row_high, row - 16 * row_high, first, second, third]
    for v in range(8):
        value = values[v].astype(jnp.float32) if v < len(values) else jnp.zeros_like(row)
        value_ref[pl.ds(v, count, stride=8), :] = jnp.concatenate([value, pad], axis=1)
    spots = lax.broadcasted_iota(jnp.int32, (wide, wide), 0).astype(jnp.float32)

    def body(step, carry):
        for k in range(8):
            q = step * 8 + k
            hot = jnp.where(place_ref[pl.ds(q, 1), :] == spots, 1.0, 0.0).astype(jnp.bfloat16)
            at = pl.ds(pl.multiple_of(q * 8, 8), 8)
            result_ref[at, :] = dot_last(value_ref[at, :].astype(jnp.bfloat16), hot)
        return carry

    lax.fori_loop(0, count // 8, body, 0)
    result = [result_ref[pl.ds(v, count, stride=8), :] for v in range(5)]
    found = jnp.sum(mine, axis=-1, keepdims=True)
    lane = lax.broadcasted_iota(jnp.int32, (count, wide), 1)
    rows = 16 * result[0] + result[1]
    rows_ref[...] = jnp.where(lane < cands, rows, found).astype(jnp.int32)
    listed = jnp.where(lane.astype(jnp.float32) < found, result[2] + result[3] + result[4], -1.0)
    stacked = jnp.concatenate(split3(listed), axis=0)
    steps = cands // GROUP
    source = lax.broadcasted_iota(jnp.int32, (wide, wide), 0)
    block = lax.broadcasted_iota(jnp.int32, (wide, wide), 1) // (wide // GROUP)
    for t in range(steps):
        pick = jnp.where(source == block + t * GROUP, 1.0, 0.0).astype(jnp.bfloat16)
        spread = dot(stacked, pick)
        target_ref[pl.ds(t, count, stride=steps), :] = (
            spread[:count] + spread[count : 2 * count] + spread[2 * count :]
        )


def prep(me, meta, shard, cands):
    count = meta.shape[0]
    wide = 128
    return pl.pallas_call(
        functools.partial(prep_kernel, shard=shard, cands=cands),
        in_specs=[
            pl.BlockSpec(memory_space=pltpu.SMEM),
            pl.BlockSpec(memory_space=pltpu.VMEM),
        ],
        out_specs=[pl.BlockSpec(memory_space=pltpu.VMEM)] * 2,
        out_shape=[
            jax.ShapeDtypeStruct((count, wide), jnp.int32),
            jax.ShapeDtypeStruct((count * (cands // GROUP), wide), jnp.float32),
        ],
        scratch_shapes=[
            pltpu.VMEM((count * 8, wide), jnp.float32),
            pltpu.VMEM((count, wide), jnp.float32),
            pltpu.VMEM((count * 8, wide), jnp.float32),
        ],
        compiler_params=pltpu.CompilerParams(vmem_limit_bytes=12 * MIB),
        name="prep",
    )(me, meta)


def pair_kernel(source_ref, rows_ref, target_ref, queries_ref, inverse_ref, index_ref, out_ref,
                units_ref, unit_ref, acc_ref, total_ref, left_ref, right_ref, back_ref, *, cands):
    count, tokens, dim = queries_ref.shape
    wide = rows_ref.shape[1]
    per_query = cands // GROUP
    slots = count * per_query
    bits = per_query.bit_length() - 1
    total = jnp.int32(0)
    for q in range(count):
        for t in range(per_query):
            units_ref[total + t] = jnp.int32(q * per_query + t)
        total = total + lax.div(rows_ref[q, cands] + (GROUP - 1), GROUP)
    for t in range(UNITS):
        units_ref[total + t] = jnp.int32(slots)
    steps = lax.div(total + (UNITS - 1), UNITS)

    def entry(number):
        slot = units_ref[number]
        q = jnp.minimum(lax.shift_right_logical(slot, bits), count - 1)
        return slot, q, jnp.bitwise_and(slot, per_query - 1) * GROUP

    for q in range(count):
        unit_ref[q] = rounded_queries(queries_ref[q])
    acc_ref[...] = jnp.zeros_like(acc_ref)
    ones = jnp.ones((8, wide), jnp.bfloat16)

    def forward(step, carry):
        done = []
        for u in range(UNITS):
            slot, q, base = entry(step * UNITS + u)
            rows = [rows_ref[q, base + g] for g in range(GROUP)]
            tiles = jnp.concatenate([index_ref[row] for row in rows], axis=0)
            raw = dot_last(unit_ref[q], tiles)
            expos, backs = [], []
            for g in range(GROUP):
                inverse = inverse_ref[pl.ds(rows[g], 1), :]
                expo = jnp.exp2(raw[:, g * wide : (g + 1) * wide] * (inverse * (LOG2E / inner_temp)))
                expos.append(expo.astype(jnp.bfloat16))
                backs.append(
                    dot((expo * inverse).astype(jnp.bfloat16), tiles[g * wide : (g + 1) * wide]).astype(
                        jnp.bfloat16
                    )
                )
            totals = dot_last(ones, jnp.concatenate(expos, axis=0))
            done.append((slot, totals, jnp.concatenate(backs, axis=0)))
        for u, (slot, totals, back) in enumerate(done):
            total_ref[pl.ds(slot, 1), :] = totals[0:1]
            back_ref[step * UNITS + u] = back
        return carry

    lax.fori_loop(0, steps, forward, 0)

    target = target_ref[...]
    held = target >= 0.0
    totals = jnp.where(held, total_ref[0:slots, :], 1.0)
    target = jnp.where(held, target, 0.0)
    same = lax.broadcasted_iota(jnp.int32, (wide, wide), 0) // tokens == lax.broadcasted_iota(
        jnp.int32, (wide, wide), 1
    ) // tokens
    same = jnp.where(same, 1.0, 0.0).astype(jnp.bfloat16)
    parts = [dot(part, same) for part in split3(jnp.log(totals))]
    score = inner_temp * (parts[0] + parts[1] + parts[2])
    lift = jnp.where(held, jnp.exp(score), 0.0)
    recip = 1.0 / totals
    left_ref[0:slots, :] = lift * recip
    right_ref[0:slots, :] = target * recip
    left_ref[slots:, :] = jnp.zeros_like(left_ref[slots:, :])
    right_ref[slots:, :] = jnp.zeros_like(right_ref[slots:, :])

    def per_source(values):
        rows = jnp.sum(values.reshape(count, per_query, wide), axis=1)
        return jnp.sum(rows, axis=-1, keepdims=True) * (1.0 / tokens)

    lane = lax.broadcasted_iota(jnp.int32, (count, wide), 1)
    sums = jnp.where(lane < wide // 2, per_source(lift), per_source(target * score))
    diagonal = lax.broadcasted_iota(jnp.int32, (tokens, wide), 0) == lax.broadcasted_iota(
        jnp.int32, (tokens, wide), 1
    ) % tokens

    def backward(step, carry):
        done = []
        for u in range(UNITS):
            slot, q, _ = entry(step * UNITS + u)
            left = jnp.where(diagonal, left_ref[pl.ds(slot, 1), :], 0.0)
            right = jnp.where(diagonal, right_ref[pl.ds(slot, 1), :], 0.0)
            both = jnp.concatenate([left, right], axis=0)
            high = both.astype(jnp.bfloat16)
            low = (both - high.astype(jnp.float32)).astype(jnp.bfloat16)
            part = dot(jnp.concatenate([high, low], axis=0), back_ref[step * UNITS + u])
            done.append((q, part[: 2 * tokens] + part[2 * tokens :]))
        for q, part in done:
            acc_ref[q] += part
        return carry

    lax.fori_loop(0, steps, backward, 0)
    for q in range(count):
        out_ref[pl.ds(q * 2 * tokens, 2 * tokens), :] = acc_ref[q].astype(jnp.bfloat16)
    for k, part in enumerate(split3(sums)):
        out_ref[pl.ds(count * 2 * tokens + k * count, count), :] = part


def pairs(source, rows, targets, queries, inverse, index, cands, room):
    count, tokens, dim = queries.shape
    wide = rows.shape[1]
    per_query = cands // GROUP
    slots = count * per_query
    most = (room + (GROUP - 1) * count) // GROUP + UNITS
    height = count * 2 * tokens + 3 * count
    return pl.pallas_call(
        functools.partial(pair_kernel, cands=cands),
        grid_spec=pltpu.PrefetchScalarGridSpec(
            num_scalar_prefetch=1,
            grid=(1,),
            in_specs=[
                pl.BlockSpec((count, wide), lambda i, s: (s[0], 0), memory_space=pltpu.SMEM),
                pl.BlockSpec((slots, wide), lambda i, s: (s[0], 0)),
                pl.BlockSpec(memory_space=pltpu.VMEM),
                pl.BlockSpec(memory_space=pltpu.VMEM),
                pl.BlockSpec(memory_space=pltpu.VMEM),
            ],
            out_specs=pl.BlockSpec((height, dim), lambda i, s: (0, 0)),
            scratch_shapes=[
                pltpu.SMEM((slots + per_query + UNITS,), jnp.int32),
                pltpu.VMEM((count, tokens, dim), jnp.bfloat16),
                pltpu.VMEM((count, 2 * tokens, dim), jnp.float32),
                pltpu.VMEM((slots + 8, wide), jnp.float32),
                pltpu.VMEM((slots + 8, wide), jnp.float32),
                pltpu.VMEM((slots + 8, wide), jnp.float32),
                pltpu.VMEM((most, GROUP * tokens, dim), jnp.bfloat16),
            ],
        ),
        out_shape=jax.ShapeDtypeStruct((height, dim), jnp.bfloat16),
        compiler_params=pltpu.CompilerParams(vmem_limit_bytes=12 * MIB),
        cost_estimate=pl.CostEstimate(
            flops=6 * room * tokens * wide * dim,
            bytes_accessed=2 * room * wide * dim,
            transcendentals=room * tokens * wide,
        ),
        name="pairs",
    )(source, rows, targets, queries, inverse, index)


def neg_kernel(rows_ref, queries_ref, index_ref, acc_ref, sums_ref,
               unit_ref, turned_ref, expo_ref, total_ref, left_ref, back_ref, *, tokens):
    total = rows_ref.shape[0]
    chunk = expo_ref.shape[0]
    height, dim = queries_ref.shape
    wide = index_ref.shape[1]
    lanes = 128
    half = min(height, 256)
    unit_ref[...] = rounded_queries(queries_ref[...])
    back_ref[...] = jnp.zeros_like(back_ref)
    sums_ref[...] = jnp.zeros_like(sums_ref)
    same = lax.broadcasted_iota(jnp.int32, (lanes, lanes), 0) // tokens == lax.broadcasted_iota(
        jnp.int32, (lanes, lanes), 1
    ) // tokens
    same = jnp.where(same, 1.0, 0.0).astype(jnp.bfloat16)

    def block(number, carry):
        def forward(step, carry):
            first = step * NEG_STEP
            tiles = jnp.concatenate(
                [index_ref[rows_ref[number * chunk + first + g]] for g in range(NEG_STEP)], axis=0
            )
            raw = dot_last(tiles, unit_ref[...])
            broad = tiles.astype(jnp.float32)
            inverse = lax.rsqrt(jnp.sum(broad * broad, axis=-1, keepdims=True) + epsilon)
            flat = (broad * inverse).astype(jnp.bfloat16)
            expo = jnp.exp2(raw * (inverse * (LOG2E / inner_temp)))
            for g in range(NEG_STEP):
                part = slice(g * wide, (g + 1) * wide)
                turned_ref[first + g] = flat[part].T
                expo_ref[first + g] = expo[part].astype(jnp.bfloat16)
                total_ref[pl.ds(first + g, 1), :] = jnp.sum(expo[part], axis=0, keepdims=True)
            return carry

        lax.fori_loop(0, chunk // NEG_STEP, forward, 0)
        for c in range(height // lanes):
            part = slice(c * lanes, (c + 1) * lanes)
            totals = total_ref[:, part]
            pieces = [dot(piece, same) for piece in split3(jnp.log(totals))]
            lift = jnp.exp(inner_temp * (pieces[0] + pieces[1] + pieces[2]))
            left_ref[:, part] = lift / totals
            sums_ref[:, part] += jnp.broadcast_to(jnp.sum(lift, axis=0, keepdims=True), (8, lanes))
        for c in range(height // half):
            part = slice(c * half, (c + 1) * half)

            def backward(step, acc):
                for g in range(NEG_STEP):
                    k = step * NEG_STEP + g
                    acc = acc + dot(turned_ref[k], expo_ref[k, :, part]) * left_ref[pl.ds(k, 1), part]
                return acc

            back_ref[:, part] = lax.fori_loop(0, chunk // NEG_STEP, backward, back_ref[:, part])
        return carry

    lax.fori_loop(0, total // chunk, block, 0)
    for c in range(height // lanes):
        part = slice(c * lanes, (c + 1) * lanes)
        acc_ref[part, :] = back_ref[:, part].T


def negatives(rows, queries, index):
    total = rows.shape[0]
    count, tokens, dim = queries.shape
    wide = index.shape[1]
    height = count * tokens
    chunk = math.gcd(total, NEG_CHUNK)
    return pl.pallas_call(
        functools.partial(neg_kernel, tokens=tokens),
        in_specs=[
            pl.BlockSpec(memory_space=pltpu.SMEM),
            pl.BlockSpec(memory_space=pltpu.VMEM),
            pl.BlockSpec(memory_space=pltpu.VMEM),
        ],
        out_specs=[pl.BlockSpec(memory_space=pltpu.VMEM)] * 2,
        out_shape=[
            jax.ShapeDtypeStruct((height, dim), jnp.float32),
            jax.ShapeDtypeStruct((8, height), jnp.float32),
        ],
        scratch_shapes=[
            pltpu.VMEM((height, dim), jnp.bfloat16),
            pltpu.VMEM((chunk, dim, wide), jnp.bfloat16),
            pltpu.VMEM((chunk, wide, height), jnp.bfloat16),
            pltpu.VMEM((chunk, height), jnp.float32),
            pltpu.VMEM((chunk, height), jnp.float32),
            pltpu.VMEM((dim, height), jnp.float32),
        ],
        compiler_params=pltpu.CompilerParams(vmem_limit_bytes=28 * MIB),
        cost_estimate=pl.CostEstimate(
            flops=4 * total * height * wide * dim,
            bytes_accessed=2 * total * wide * dim,
            transcendentals=total * height * wide,
        ),
        name="negatives",
    )(rows, queries.reshape(height, dim), index)


def on_device(queries, index, cand_owner, cand_row, neg_row, teacher):
    count, tokens, dim = queries.shape
    cands = cand_row.shape[1]
    shard = index.shape[0]
    owners = lax.axis_size("corpus")
    room = (2 * count * cands + owners - 1) // owners
    me = lax.axis_index("corpus").astype(jnp.int32)
    group = lax.axis_size("blk")

    def from_step(value, axis, size, step):
        return lax.ppermute(value, axis, [((i + step) % size, i) for i in range(size)])

    def gathered(value, axis, size):
        return [value] + [from_step(value, axis, size, step) for step in range(1, size)]

    code = (cand_owner[..., 0] * shard + cand_row).astype(jnp.float32)
    meta = jnp.concatenate([code, teacher], axis=1)
    all_neg = jnp.concatenate(gathered(neg_row, "blk", group), axis=0).reshape(-1)
    all_meta = lax.all_gather(meta, "corpus", axis=0, tiled=True)
    all_queries = gathered(queries, "corpus", owners)
    index = pltpu.with_memory_space_constraint(index, pltpu.VMEM)
    inverse = norms(index)
    neg_acc, neg_sum = negatives(all_neg, queries, index)
    rows, targets = prep(me.reshape(1), all_meta, shard, cands)
    rows, neg_acc = lax.optimization_barrier((rows, neg_acc))
    messages = []
    for step in list(range(1, owners)) + [0]:
        source = lax.rem(me + step, owners)
        message = pairs(
            source.reshape(1), rows, targets, all_queries[step], inverse, index, cands, room
        )
        if step:
            message = lax.ppermute(
                message, "corpus", [(i, (i + step) % owners) for i in range(owners)]
            )
        messages.append(message)
    cut = count * 2 * tokens
    both = sum(m[:cut].astype(jnp.float32) for m in messages).reshape(count, 2, tokens, dim)
    scores = sum(m[cut:].astype(jnp.float32) for m in messages).reshape(3, count, dim).sum(axis=0)
    total = scores[:, 0] + neg_sum[0].reshape(count, tokens)[:, 0]
    spread = jnp.log(total)
    log_target = teacher - jnp.log(jnp.sum(jnp.exp(teacher), axis=1, keepdims=True))
    target = jnp.exp(log_target)
    losses = jnp.sum(target * (log_target + spread[:, None]), axis=1) - scores[:, dim // 2]
    pulled = (both[:, 0] + neg_acc.reshape(count, tokens, dim)) / total[:, None, None] - both[:, 1]
    widened = queries.astype(jnp.float32)
    radius = jnp.sqrt(jnp.sum(widened * widened, axis=-1, keepdims=True) + epsilon)
    unit = widened / radius
    query_grads = (pulled - unit * jnp.sum(unit * pulled, axis=-1, keepdims=True)) / radius
    return (losses, query_grads)


def solution(mesh):
    placed = (
        P(("corpus", "blk"), None, None),
        P("corpus", None, None),
        P(("corpus", "blk"), None, None),
        P(("corpus", "blk"), None),
        P(("corpus", "blk"), None),
        P(("corpus", "blk"), None),
    )
    return jax.shard_map(
        on_device,
        mesh=mesh,
        in_specs=placed,
        out_specs=(P(("corpus", "blk")), P(("corpus", "blk"), None, None)),
        check_vma=False,
    )
```

```python
import functools
import math

import jax
import jax.numpy as jnp
from jax import lax
from jax.experimental import pallas as pl
from jax.experimental.pallas import tpu as pltpu
from jax.sharding import PartitionSpec as P

inner_temp = 0.1
epsilon = 1e-06
LOG2E = 1.4426950408889634
GROUP = 4
UNITS = 8
NEG_STEP = 8
NEG_CHUNK = 96
MIB = 1024 * 1024
LAST = (((1,), (1,)), ((), ()))


def dot_last(a, b):
    return lax.dot_general(a, b, LAST, preferred_element_type=jnp.float32)


def dot(a, b):
    return jnp.dot(a, b, preferred_element_type=jnp.float32)


def split3(x):
    high = x.astype(jnp.bfloat16)
    rest = x - high.astype(jnp.float32)
    mid = rest.astype(jnp.bfloat16)
    low = (rest - mid.astype(jnp.float32)).astype(jnp.bfloat16)
    return high, mid, low


def rounded_queries(raw):
    wide = raw.astype(jnp.float32)
    radius = jnp.sqrt(jnp.sum(wide * wide, axis=-1, keepdims=True) + epsilon)
    return (wide / radius).astype(jnp.bfloat16)


def norm_kernel(part_ref, index_ref, out_ref):
    count, tokens = out_ref.shape
    dim = index_ref.shape[2]
    base = part_ref[0] * count
    ones = jnp.ones((8, dim), jnp.bfloat16)
    sub = lax.broadcasted_iota(jnp.int32, (8, tokens), 0)

    def body(step, carry):
        squares = jnp.zeros((8, tokens), jnp.float32)
        for k in range(8):
            tile = index_ref[base + step * 8 + k].astype(jnp.float32)
            tile = tile * tile
            high = tile.astype(jnp.bfloat16)
            low = (tile - high.astype(jnp.float32)).astype(jnp.bfloat16)
            squares = jnp.where(sub == k, dot_last(ones, high) + dot_last(ones, low), squares)
        out_ref[pl.ds(pl.multiple_of(step * 8, 8), 8), :] = lax.rsqrt(squares + epsilon)
        return carry

    lax.fori_loop(0, count // 8, body, 0, unroll=2)


def norms(part, index, parts):
    tokens, dim = index.shape[1:]
    count = index.shape[0] // parts
    return pl.pallas_call(
        norm_kernel,
        in_specs=[pl.BlockSpec(memory_space=pltpu.SMEM), pl.BlockSpec(memory_space=pltpu.VMEM)],
        out_specs=pl.BlockSpec(memory_space=pltpu.VMEM),
        out_shape=jax.ShapeDtypeStruct((count, tokens), jnp.float32),
        compiler_params=pltpu.CompilerParams(vmem_limit_bytes=8 * MIB),
        cost_estimate=pl.CostEstimate(
            flops=32 * count * tokens * dim,
            bytes_accessed=2 * count * tokens * dim,
            transcendentals=count * tokens,
        ),
        name="norms",
    )(part, index)


def prep_kernel(me_ref, meta_ref, rows_ref, target_ref, value_ref, place_ref, result_ref, *, shard, cands):
    count = meta_ref.shape[0]
    code = meta_ref[:, :cands]
    owner = jnp.floor((code + 0.5) * (1.0 / shard))
    row = code - owner * shard
    teacher = meta_ref[:, cands:]
    log_target = teacher - jnp.log(jnp.sum(jnp.exp(teacher), axis=-1, keepdims=True))
    target = jnp.exp(log_target)
    mine = (owner == me_ref[0].astype(jnp.float32)).astype(jnp.float32)
    before = lax.broadcasted_iota(jnp.int32, (cands, cands), 0) < lax.broadcasted_iota(
        jnp.int32, (cands, cands), 1
    )
    place = dot(mine.astype(jnp.bfloat16), before.astype(jnp.float32).astype(jnp.bfloat16))
    wide = value_ref.shape[1]
    pad = jnp.zeros((count, wide - cands), jnp.float32)
    place_ref[...] = jnp.concatenate([jnp.where(mine > 0, place, -1.0), pad - 1.0], axis=1)
    row_high = jnp.floor(row * (1.0 / 16))
    first, second, third = split3(target)
    values = [row_high, row - 16 * row_high, first, second, third]
    for v in range(8):
        value = values[v].astype(jnp.float32) if v < len(values) else jnp.zeros_like(row)
        value_ref[pl.ds(v, count, stride=8), :] = jnp.concatenate([value, pad], axis=1)
    spots = lax.broadcasted_iota(jnp.int32, (wide, wide), 0).astype(jnp.float32)

    def body(step, carry):
        for k in range(8):
            q = step * 8 + k
            hot = jnp.where(place_ref[pl.ds(q, 1), :] == spots, 1.0, 0.0).astype(jnp.bfloat16)
            at = pl.ds(pl.multiple_of(q * 8, 8), 8)
            result_ref[at, :] = dot_last(value_ref[at, :].astype(jnp.bfloat16), hot)
        return carry

    lax.fori_loop(0, count // 8, body, 0)
    result = [result_ref[pl.ds(v, count, stride=8), :] for v in range(5)]
    found = jnp.sum(mine, axis=-1, keepdims=True)
    lane = lax.broadcasted_iota(jnp.int32, (count, wide), 1)
    rows = 16 * result[0] + result[1]
    rows_ref[...] = jnp.where(lane < cands, rows, found).astype(jnp.int32)
    listed = jnp.where(lane.astype(jnp.float32) < found, result[2] + result[3] + result[4], -1.0)
    stacked = jnp.concatenate(split3(listed), axis=0)
    steps = cands // GROUP
    source = lax.broadcasted_iota(jnp.int32, (wide, wide), 0)
    block = lax.broadcasted_iota(jnp.int32, (wide, wide), 1) // (wide // GROUP)
    for t in range(steps):
        pick = jnp.where(source == block + t * GROUP, 1.0, 0.0).astype(jnp.bfloat16)
        spread = dot(stacked, pick)
        target_ref[pl.ds(t, count, stride=steps), :] = (
            spread[:count] + spread[count : 2 * count] + spread[2 * count :]
        )


def prep(me, meta, shard, cands):
    count = meta.shape[0]
    wide = 128
    return pl.pallas_call(
        functools.partial(prep_kernel, shard=shard, cands=cands),
        in_specs=[
            pl.BlockSpec(memory_space=pltpu.SMEM),
            pl.BlockSpec(memory_space=pltpu.VMEM),
        ],
        out_specs=[pl.BlockSpec(memory_space=pltpu.VMEM)] * 2,
        out_shape=[
            jax.ShapeDtypeStruct((count, wide), jnp.int32),
            jax.ShapeDtypeStruct((count * (cands // GROUP), wide), jnp.float32),
        ],
        scratch_shapes=[
            pltpu.VMEM((count * 8, wide), jnp.float32),
            pltpu.VMEM((count, wide), jnp.float32),
            pltpu.VMEM((count * 8, wide), jnp.float32),
        ],
        compiler_params=pltpu.CompilerParams(vmem_limit_bytes=12 * MIB),
        name="prep",
    )(me, meta)


def pair_kernel(source_ref, rows_ref, target_ref, queries_ref, inverse_ref, index_ref, out_ref,
                units_ref, unit_ref, acc_ref, total_ref, left_ref, right_ref, back_ref, raw_ref, *, cands):
    count, tokens, dim = queries_ref.shape
    wide = rows_ref.shape[1]
    per_query = cands // GROUP
    slots = count * per_query
    bits = per_query.bit_length() - 1
    total = jnp.int32(0)
    for q in range(count):
        for t in range(per_query):
            units_ref[total + t] = jnp.int32(q * per_query + t)
        total = total + lax.div(rows_ref[q, cands] + (GROUP - 1), GROUP)
    for t in range(2 * UNITS):
        units_ref[total + t] = jnp.int32(slots)
    steps = lax.div(total + (UNITS - 1), UNITS)

    def entry(number):
        slot = units_ref[number]
        q = jnp.minimum(lax.shift_right_logical(slot, bits), count - 1)
        return slot, q, jnp.bitwise_and(slot, per_query - 1) * GROUP

    for q in range(count):
        unit_ref[q] = rounded_queries(queries_ref[q])
    acc_ref[...] = jnp.zeros_like(acc_ref)
    ones = jnp.ones((8, wide), jnp.bfloat16)

    def tiles_of(number):
        _, q, base = entry(number)
        rows = [rows_ref[q, base + g] for g in range(GROUP)]
        return q, rows, [index_ref[row] for row in rows]

    def multiply(step):
        found = []
        for u in range(UNITS):
            q, _, tiles = tiles_of(step * UNITS + u)
            found.append(dot_last(unit_ref[q], jnp.concatenate(tiles, axis=0)))
        return found

    def forward(step, carry):
        expos, weights = [], []
        for u in range(UNITS):
            _, q, base = entry(step * UNITS + u)
            for g in range(GROUP):
                row = rows_ref[q, base + g] - source_ref[1]
                row = row + jnp.where(row < 0, index_ref.shape[0], 0)
                inverse = inverse_ref[pl.ds(row, 1), :]
                raw = raw_ref[u, :, g * wide : (g + 1) * wide]
                expo = jnp.exp2(raw * (inverse * (LOG2E / inner_temp)))
                expos.append(expo.astype(jnp.bfloat16))
                weights.append((expo * inverse).astype(jnp.bfloat16))
        following = multiply(step + 1)
        done = []
        for u in range(UNITS):
            slot = units_ref[step * UNITS + u]
            part = slice(u * GROUP, (u + 1) * GROUP)
            _, _, tiles = tiles_of(step * UNITS + u)
            backs = [dot(w, tile).astype(jnp.bfloat16) for w, tile in zip(weights[part], tiles)]
            totals = dot_last(ones, jnp.concatenate(expos[part], axis=0))
            done.append((slot, totals, jnp.concatenate(backs, axis=0)))
        for u in range(UNITS):
            raw_ref[u] = following[u]
        for u, (slot, totals, back) in enumerate(done):
            total_ref[pl.ds(slot, 1), :] = totals[0:1]
            back_ref[step * UNITS + u] = back
        return carry

    for u, raw in enumerate(multiply(0)):
        raw_ref[u] = raw
    lax.fori_loop(0, steps, forward, 0)

    target = target_ref[...]
    held = target >= 0.0
    totals = jnp.where(held, total_ref[0:slots, :], 1.0)
    target = jnp.where(held, target, 0.0)
    same = lax.broadcasted_iota(jnp.int32, (wide, wide), 0) // tokens == lax.broadcasted_iota(
        jnp.int32, (wide, wide), 1
    ) // tokens
    same = jnp.where(same, 1.0, 0.0).astype(jnp.bfloat16)
    parts = [dot(part, same) for part in split3(jnp.log(totals))]
    score = inner_temp * (parts[0] + parts[1] + parts[2])
    lift = jnp.where(held, jnp.exp(score), 0.0)
    recip = 1.0 / totals
    left_ref[0:slots, :] = lift * recip
    right_ref[0:slots, :] = target * recip
    left_ref[slots:, :] = jnp.zeros_like(left_ref[slots:, :])
    right_ref[slots:, :] = jnp.zeros_like(right_ref[slots:, :])

    def per_source(values):
        rows = jnp.sum(values.reshape(count, per_query, wide), axis=1)
        return jnp.sum(rows, axis=-1, keepdims=True) * (1.0 / tokens)

    lane = lax.broadcasted_iota(jnp.int32, (count, wide), 1)
    sums = jnp.where(lane < wide // 2, per_source(lift), per_source(target * score))
    diagonal = lax.broadcasted_iota(jnp.int32, (tokens, wide), 0) == lax.broadcasted_iota(
        jnp.int32, (tokens, wide), 1
    ) % tokens

    def backward(step, carry):
        done = []
        for u in range(UNITS):
            slot, q, _ = entry(step * UNITS + u)
            left = jnp.where(diagonal, left_ref[pl.ds(slot, 1), :], 0.0)
            right = jnp.where(diagonal, right_ref[pl.ds(slot, 1), :], 0.0)
            both = jnp.concatenate([left, right], axis=0)
            high = both.astype(jnp.bfloat16)
            low = (both - high.astype(jnp.float32)).astype(jnp.bfloat16)
            part = dot(jnp.concatenate([high, low], axis=0), back_ref[step * UNITS + u])
            done.append((q, part[: 2 * tokens] + part[2 * tokens :]))
        for q, part in done:
            acc_ref[q] += part
        return carry

    lax.fori_loop(0, steps, backward, 0)
    for q in range(count):
        out_ref[pl.ds(q * 2 * tokens, 2 * tokens), :] = acc_ref[q].astype(jnp.bfloat16)
    for k, part in enumerate(split3(sums)):
        out_ref[pl.ds(count * 2 * tokens + k * count, count), :] = part


def pairs(source, rows, targets, queries, inverse, index, cands, room):
    count, tokens, dim = queries.shape
    wide = rows.shape[1]
    per_query = cands // GROUP
    slots = count * per_query
    most = (room + (GROUP - 1) * count) // GROUP + UNITS
    height = count * 2 * tokens + 3 * count
    return pl.pallas_call(
        functools.partial(pair_kernel, cands=cands),
        grid_spec=pltpu.PrefetchScalarGridSpec(
            num_scalar_prefetch=1,
            grid=(1,),
            in_specs=[
                pl.BlockSpec((count, wide), lambda i, s: (s[0], 0), memory_space=pltpu.SMEM),
                pl.BlockSpec((slots, wide), lambda i, s: (s[0], 0)),
                pl.BlockSpec(memory_space=pltpu.VMEM),
                pl.BlockSpec(memory_space=pltpu.VMEM),
                pl.BlockSpec(memory_space=pltpu.VMEM),
            ],
            out_specs=pl.BlockSpec((height, dim), lambda i, s: (0, 0)),
            scratch_shapes=[
                pltpu.SMEM((slots + per_query + 2 * UNITS,), jnp.int32),
                pltpu.VMEM((count, tokens, dim), jnp.bfloat16),
                pltpu.VMEM((count, 2 * tokens, dim), jnp.float32),
                pltpu.VMEM((slots + 8, wide), jnp.float32),
                pltpu.VMEM((slots + 8, wide), jnp.float32),
                pltpu.VMEM((slots + 8, wide), jnp.float32),
                pltpu.VMEM((most, GROUP * tokens, dim), jnp.bfloat16),
                pltpu.VMEM((UNITS, tokens, GROUP * wide), jnp.float32),
            ],
        ),
        out_shape=jax.ShapeDtypeStruct((height, dim), jnp.bfloat16),
        compiler_params=pltpu.CompilerParams(vmem_limit_bytes=12 * MIB),
        cost_estimate=pl.CostEstimate(
            flops=6 * room * tokens * wide * dim,
            bytes_accessed=2 * room * wide * dim,
            transcendentals=room * tokens * wide,
        ),
        name="pairs",
    )(source, rows, targets, queries, inverse, index)


def neg_kernel(rows_ref, queries_ref, index_ref, acc_ref, sums_ref,
               unit_ref, turned_ref, expo_ref, total_ref, left_ref, back_ref, *, tokens):
    total = rows_ref.shape[0]
    chunk = expo_ref.shape[0]
    height, dim = queries_ref.shape
    wide = index_ref.shape[1]
    lanes = 128
    half = min(height, 256)
    unit_ref[...] = rounded_queries(queries_ref[...])
    back_ref[...] = jnp.zeros_like(back_ref)
    sums_ref[...] = jnp.zeros_like(sums_ref)
    same = lax.broadcasted_iota(jnp.int32, (lanes, lanes), 0) // tokens == lax.broadcasted_iota(
        jnp.int32, (lanes, lanes), 1
    ) // tokens
    same = jnp.where(same, 1.0, 0.0).astype(jnp.bfloat16)

    def block(number, carry):
        def forward(step, carry):
            first = step * NEG_STEP
            tiles = jnp.concatenate(
                [index_ref[rows_ref[number * chunk + first + g]] for g in range(NEG_STEP)], axis=0
            )
            raw = dot_last(tiles, unit_ref[...])
            broad = tiles.astype(jnp.float32)
            inverse = lax.rsqrt(jnp.sum(broad * broad, axis=-1, keepdims=True) + epsilon)
            flat = (broad * inverse).astype(jnp.bfloat16)
            expo = jnp.exp2(raw * (inverse * (LOG2E / inner_temp)))
            for g in range(NEG_STEP):
                part = slice(g * wide, (g + 1) * wide)
                turned_ref[first + g] = flat[part].T
                expo_ref[first + g] = expo[part].astype(jnp.bfloat16)
                total_ref[pl.ds(first + g, 1), :] = jnp.sum(expo[part], axis=0, keepdims=True)
            return carry

        lax.fori_loop(0, chunk // NEG_STEP, forward, 0)
        for c in range(height // lanes):
            part = slice(c * lanes, (c + 1) * lanes)
            totals = total_ref[:, part]
            pieces = [dot(piece, same) for piece in split3(jnp.log(totals))]
            lift = jnp.exp(inner_temp * (pieces[0] + pieces[1] + pieces[2]))
            left_ref[:, part] = lift / totals
            sums_ref[:, part] += jnp.broadcast_to(jnp.sum(lift, axis=0, keepdims=True), (8, lanes))
        for c in range(height // half):
            part = slice(c * half, (c + 1) * half)

            def backward(step, acc):
                for g in range(NEG_STEP):
                    k = step * NEG_STEP + g
                    acc = acc + dot(turned_ref[k], expo_ref[k, :, part]) * left_ref[pl.ds(k, 1), part]
                return acc

            back_ref[:, part] = lax.fori_loop(0, chunk // NEG_STEP, backward, back_ref[:, part])
        return carry

    lax.fori_loop(0, total // chunk, block, 0)
    for c in range(height // lanes):
        part = slice(c * lanes, (c + 1) * lanes)
        acc_ref[part, :] = back_ref[:, part].T


def negatives(rows, queries, index):
    total = rows.shape[0]
    count, tokens, dim = queries.shape
    wide = index.shape[1]
    height = count * tokens
    chunk = math.gcd(total, NEG_CHUNK)
    return pl.pallas_call(
        functools.partial(neg_kernel, tokens=tokens),
        in_specs=[
            pl.BlockSpec(memory_space=pltpu.SMEM),
            pl.BlockSpec(memory_space=pltpu.VMEM),
            pl.BlockSpec(memory_space=pltpu.VMEM),
        ],
        out_specs=[pl.BlockSpec(memory_space=pltpu.VMEM)] * 2,
        out_shape=[
            jax.ShapeDtypeStruct((height, dim), jnp.float32),
            jax.ShapeDtypeStruct((8, height), jnp.float32),
        ],
        scratch_shapes=[
            pltpu.VMEM((height, dim), jnp.bfloat16),
            pltpu.VMEM((chunk, dim, wide), jnp.bfloat16),
            pltpu.VMEM((chunk, wide, height), jnp.bfloat16),
            pltpu.VMEM((chunk, height), jnp.float32),
            pltpu.VMEM((chunk, height), jnp.float32),
            pltpu.VMEM((dim, height), jnp.float32),
        ],
        compiler_params=pltpu.CompilerParams(vmem_limit_bytes=28 * MIB),
        cost_estimate=pl.CostEstimate(
            flops=4 * total * height * wide * dim,
            bytes_accessed=2 * total * wide * dim,
            transcendentals=total * height * wide,
        ),
        name="negatives",
    )(rows, queries.reshape(height, dim), index)


def on_device(queries, index, cand_owner, cand_row, neg_row, teacher):
    count, tokens, dim = queries.shape
    cands = cand_row.shape[1]
    shard = index.shape[0]
    owners = lax.axis_size("corpus")
    room = (2 * count * cands + owners - 1) // owners
    me = lax.axis_index("corpus").astype(jnp.int32)
    group = lax.axis_size("blk")

    def from_step(value, axis, size, step):
        return lax.ppermute(value, axis, [((i + step) % size, i) for i in range(size)])

    def gathered(value, axis, size):
        return [value] + [from_step(value, axis, size, step) for step in range(1, size)]

    code = (cand_owner[..., 0] * shard + cand_row).astype(jnp.float32)
    meta = jnp.concatenate([code, teacher], axis=1)
    all_neg = jnp.concatenate(gathered(neg_row, "blk", group), axis=0).reshape(-1)
    all_meta = lax.all_gather(meta, "corpus", axis=0, tiled=True)
    all_meta, sent = lax.optimization_barrier((all_meta, queries))
    all_queries = gathered(sent, "corpus", owners)
    index = pltpu.with_memory_space_constraint(index, pltpu.VMEM)
    part = lax.axis_index("blk").astype(jnp.int32)
    pieces = gathered(norms(part.reshape(1), index, group), "blk", group)
    inverse = jnp.concatenate(pieces, axis=0)
    turn = part * pieces[0].shape[0]
    neg_acc, neg_sum = negatives(all_neg, queries, index)
    rows, targets = prep(me.reshape(1), all_meta, shard, cands)
    rows, neg_acc = lax.optimization_barrier((rows, neg_acc))
    messages = []
    for step in list(range(1, owners)) + [0]:
        source = lax.rem(me + step, owners)
        message = pairs(
            jnp.stack([source, turn]), rows, targets, all_queries[step], inverse, index, cands, room
        )
        if step:
            message = lax.ppermute(
                message, "corpus", [(i, (i + step) % owners) for i in range(owners)]
            )
        messages.append(message)
    cut = count * 2 * tokens
    both = sum(m[:cut].astype(jnp.float32) for m in messages).reshape(count, 2, tokens, dim)
    scores = sum(m[cut:].astype(jnp.float32) for m in messages).reshape(3, count, dim).sum(axis=0)
    total = scores[:, 0] + neg_sum[0].reshape(count, tokens)[:, 0]
    spread = jnp.log(total)
    log_target = teacher - jnp.log(jnp.sum(jnp.exp(teacher), axis=1, keepdims=True))
    target = jnp.exp(log_target)
    losses = jnp.sum(target * (log_target + spread[:, None]), axis=1) - scores[:, dim // 2]
    pulled = (both[:, 0] + neg_acc.reshape(count, tokens, dim)) / total[:, None, None] - both[:, 1]
    widened = queries.astype(jnp.float32)
    radius = jnp.sqrt(jnp.sum(widened * widened, axis=-1, keepdims=True) + epsilon)
    unit = widened / radius
    query_grads = (pulled - unit * jnp.sum(unit * pulled, axis=-1, keepdims=True)) / radius
    return (losses, query_grads)


def solution(mesh):
    placed = (
        P(("corpus", "blk"), None, None),
        P("corpus", None, None),
        P(("corpus", "blk"), None, None),
        P(("corpus", "blk"), None),
        P(("corpus", "blk"), None),
        P(("corpus", "blk"), None),
    )
    return jax.shard_map(
        on_device,
        mesh=mesh,
        in_specs=placed,
        out_specs=(P(("corpus", "blk")), P(("corpus", "blk"), None, None)),
        check_vma=False,
    )
```

```python
import functools
import math

import jax
import jax.numpy as jnp
from jax import lax
from jax.experimental import pallas as pl
from jax.experimental.pallas import tpu as pltpu
from jax.sharding import PartitionSpec as P

inner_temp = 0.1
epsilon = 1e-06
LOG2E = 1.4426950408889634
GROUP = 4
UNITS = 8
LOADS = 8
LOAD_STEP = 16
NEG_STEP = 8
NEG_CHUNK = 24
SOURCES = 2
VMEM_LIMIT = 12 * 1024 * 1024
LAST = (((1,), (1,)), ((), ()))


def dot_last(a, b):
    return lax.dot_general(a, b, LAST, preferred_element_type=jnp.float32)


def dot(a, b):
    return jnp.dot(a, b, preferred_element_type=jnp.float32)


def split3(x):
    high = x.astype(jnp.bfloat16)
    rest = x - high.astype(jnp.float32)
    mid = rest.astype(jnp.bfloat16)
    low = (rest - mid.astype(jnp.float32)).astype(jnp.bfloat16)
    return high, mid, low


def rounded_queries(raw):
    wide = raw.astype(jnp.float32)
    radius = jnp.sqrt(jnp.sum(wide * wide, axis=-1, keepdims=True) + epsilon)
    return (wide / radius).astype(jnp.bfloat16)


def load_shard(index_ref, tiles_ref, turned_ref, inverse_ref, sems):
    count = index_ref.shape[0]
    chunk = count // LOADS

    def copy(part):
        at = pl.ds(part * chunk, chunk)
        return pltpu.make_async_copy(index_ref.at[at], tiles_ref.at[at], sems.at[part])

    for part in range(LOADS):
        copy(part).start()

    for part in range(LOADS):
        copy(part).wait()

        def body(step, carry):
            first = part * chunk + step * LOAD_STEP
            squares = []
            turned = []
            for k in range(LOAD_STEP):
                tile = tiles_ref[first + k].T
                turned.append(tile)
                wide = tile.astype(jnp.float32)
                squares.append(jnp.sum(wide * wide, axis=0, keepdims=True))
            for k in range(LOAD_STEP):
                turned_ref[first + k] = turned[k]
            at = pl.ds(pl.multiple_of(first, LOAD_STEP), LOAD_STEP)
            inverse_ref[at, :] = lax.rsqrt(jnp.concatenate(squares, axis=0) + epsilon)
            return carry

        lax.fori_loop(0, chunk // LOAD_STEP, body, 0)


def prep_kernel(me_ref, meta_ref, index_ref, turned_ref, rows_ref, target_ref, value_ref, place_ref, result_ref, *, shard, cands):
    count = meta_ref.shape[0]
    code = meta_ref[:, :cands]
    owner = jnp.floor((code + 0.5) * (1.0 / shard))
    row = code - owner * shard
    teacher = meta_ref[:, cands:]
    log_target = teacher - jnp.log(jnp.sum(jnp.exp(teacher), axis=-1, keepdims=True))
    target = jnp.exp(log_target)
    mine = (owner == me_ref[0].astype(jnp.float32)).astype(jnp.float32)
    before = lax.broadcasted_iota(jnp.int32, (cands, cands), 0) < lax.broadcasted_iota(
        jnp.int32, (cands, cands), 1
    )
    place = dot(mine.astype(jnp.bfloat16), before.astype(jnp.float32).astype(jnp.bfloat16))
    wide = value_ref.shape[1]
    pad = jnp.zeros((count, wide - cands), jnp.float32)
    place_ref[...] = jnp.concatenate([jnp.where(mine > 0, place, -1.0), pad - 1.0], axis=1)
    row_high = jnp.floor(row * (1.0 / 16))
    first, second, third = split3(target)
    values = [row_high, row - 16 * row_high, first, second, third]
    for v in range(8):
        value = values[v].astype(jnp.float32) if v < len(values) else jnp.zeros_like(row)
        value_ref[pl.ds(v, count, stride=8), :] = jnp.concatenate([value, pad], axis=1)
    spots = lax.broadcasted_iota(jnp.int32, (wide, wide), 0).astype(jnp.float32)

    def body(step, carry):
        for k in range(8):
            q = step * 8 + k
            hot = jnp.where(place_ref[pl.ds(q, 1), :] == spots, 1.0, 0.0).astype(jnp.bfloat16)
            at = pl.ds(pl.multiple_of(q * 8, 8), 8)
            result_ref[at, :] = dot_last(value_ref[at, :].astype(jnp.bfloat16), hot)
        return carry

    lax.fori_loop(0, count // 8, body, 0)
    result = [result_ref[pl.ds(v, count, stride=8), :] for v in range(5)]
    found = jnp.sum(mine, axis=-1, keepdims=True)
    lane = lax.broadcasted_iota(jnp.int32, (count, wide), 1)
    rows = 16 * result[0] + result[1]
    rows_ref[...] = jnp.where(lane < cands, rows, found).astype(jnp.int32)
    listed = jnp.where(lane.astype(jnp.float32) < found, result[2] + result[3] + result[4], -1.0)
    stacked = jnp.concatenate(split3(listed), axis=0)
    steps = cands // GROUP
    source = lax.broadcasted_iota(jnp.int32, (wide, wide), 0)
    block = lax.broadcasted_iota(jnp.int32, (wide, wide), 1) // (wide // GROUP)
    for t in range(steps):
        pick = jnp.where(source == block + t * GROUP, 1.0, 0.0).astype(jnp.bfloat16)
        spread = dot(stacked, pick)
        target_ref[pl.ds(t, count, stride=steps), :] = (
            spread[:count] + spread[count : 2 * count] + spread[2 * count :]
        )


def prep(me, meta, index, turned, shard, cands):
    count = meta.shape[0]
    wide = 128
    return pl.pallas_call(
        functools.partial(prep_kernel, shard=shard, cands=cands),
        in_specs=[
            pl.BlockSpec(memory_space=pltpu.SMEM),
            pl.BlockSpec(memory_space=pltpu.VMEM),
            pl.BlockSpec(memory_space=pltpu.VMEM),
            pl.BlockSpec(memory_space=pltpu.VMEM),
        ],
        out_specs=[pl.BlockSpec(memory_space=pltpu.VMEM)] * 2,
        out_shape=[
            jax.ShapeDtypeStruct((count, wide), jnp.int32),
            jax.ShapeDtypeStruct((count * (cands // GROUP), wide), jnp.float32),
        ],
        scratch_shapes=[
            pltpu.VMEM((count * 8, wide), jnp.float32),
            pltpu.VMEM((count, wide), jnp.float32),
            pltpu.VMEM((count * 8, wide), jnp.float32),
        ],
        compiler_params=pltpu.CompilerParams(vmem_limit_bytes=VMEM_LIMIT),
        cost_estimate=pl.CostEstimate(flops=count * wide, bytes_accessed=count * wide, transcendentals=0),
        name="prep",
    )(me, meta, index, turned)


def pair_kernel(source_ref, rows_ref, target_ref, queries_ref, inverse_ref, index_ref, turned_ref, *refs, cands, sources):
    out_refs = refs[:sources]
    (units_ref, unit_ref, acc_ref, total_ref, left_ref, right_ref, back_ref, raw_ref) = refs[sources:]
    count, tokens, dim = unit_ref.shape
    wide = rows_ref.shape[1]
    per_query = cands // GROUP
    slots = count * per_query
    bits = per_query.bit_length() - 1
    total = jnp.int32(0)
    for q in range(count):
        for t in range(per_query):
            units_ref[total + t] = jnp.int32(q * per_query + t)
        total = total + lax.div(rows_ref[q, cands] + (GROUP - 1), GROUP)
    for t in range(2 * UNITS):
        units_ref[total + t] = jnp.int32(slots)
    steps = lax.div(total + (UNITS - 1), UNITS)

    def entry(number):
        slot = units_ref[number]
        q = jnp.minimum(lax.shift_right_logical(slot, bits), count - 1)
        return slot, q, jnp.bitwise_and(slot, per_query - 1) * GROUP

    for q in range(count):
        unit_ref[q] = rounded_queries(queries_ref[0, q])
    acc_ref[...] = jnp.zeros_like(acc_ref)
    ones = jnp.ones((8, wide), jnp.bfloat16)

    def tiles_of(number, ref):
        _, q, base = entry(number)
        return q, [ref[rows_ref[q, base + g]] for g in range(GROUP)]

    def multiply(step):
        found = []
        for u in range(UNITS):
            q, tiles = tiles_of(step * UNITS + u, turned_ref)
            found.append(dot(unit_ref[q], jnp.concatenate(tiles, axis=1)))
        return found

    def forward(step, carry):
        expos, weights = [], []
        for u in range(UNITS):
            _, q, base = entry(step * UNITS + u)
            for g in range(GROUP):
                inverse = inverse_ref[pl.ds(rows_ref[q, base + g], 1), :]
                raw = raw_ref[u, :, g * wide : (g + 1) * wide]
                expo = jnp.exp2(raw * (inverse * (LOG2E / inner_temp)))
                expos.append(expo.astype(jnp.bfloat16))
                weights.append((expo * inverse).astype(jnp.bfloat16))
        following = multiply(step + 1)
        done = []
        for u in range(UNITS):
            slot = units_ref[step * UNITS + u]
            part = slice(u * GROUP, (u + 1) * GROUP)
            _, tiles = tiles_of(step * UNITS + u, index_ref)
            backs = [dot(w, tile).astype(jnp.bfloat16) for w, tile in zip(weights[part], tiles)]
            totals = dot_last(ones, jnp.concatenate(expos[part], axis=0))
            done.append((slot, totals, jnp.concatenate(backs, axis=0)))
        for u in range(UNITS):
            raw_ref[u] = following[u]
        for u, (slot, totals, back) in enumerate(done):
            total_ref[pl.ds(slot, 1), :] = totals[0:1]
            back_ref[step * UNITS + u] = back
        return carry

    for u, raw in enumerate(multiply(0)):
        raw_ref[u] = raw
    lax.fori_loop(0, steps, forward, 0)

    target = target_ref[...]
    held = target >= 0.0
    totals = jnp.where(held, total_ref[0:slots, :], 1.0)
    target = jnp.where(held, target, 0.0)
    same = lax.broadcasted_iota(jnp.int32, (wide, wide), 0) // tokens == lax.broadcasted_iota(
        jnp.int32, (wide, wide), 1
    ) // tokens
    same = jnp.where(same, 1.0, 0.0).astype(jnp.bfloat16)
    parts = [dot(part, same) for part in split3(jnp.log(totals))]
    score = inner_temp * (parts[0] + parts[1] + parts[2])
    lift = jnp.where(held, jnp.exp(score), 0.0)
    recip = 1.0 / totals
    left_ref[0:slots, :] = lift * recip
    right_ref[0:slots, :] = target * recip
    left_ref[slots:, :] = jnp.zeros_like(left_ref[slots:, :])
    right_ref[slots:, :] = jnp.zeros_like(right_ref[slots:, :])

    def per_source(values):
        rows = jnp.sum(values.reshape(count, per_query, wide), axis=1)
        return jnp.sum(rows, axis=-1, keepdims=True) * (1.0 / tokens)

    lane = lax.broadcasted_iota(jnp.int32, (count, wide), 1)
    sums = jnp.where(lane < wide // 2, per_source(lift), per_source(target * score))
    diagonal = lax.broadcasted_iota(jnp.int32, (tokens, wide), 0) == lax.broadcasted_iota(
        jnp.int32, (tokens, wide), 1
    ) % tokens

    def backward(step, carry):
        done = []
        for u in range(UNITS):
            slot, q, _ = entry(step * UNITS + u)
            left = jnp.where(diagonal, left_ref[pl.ds(slot, 1), :], 0.0)
            right = jnp.where(diagonal, right_ref[pl.ds(slot, 1), :], 0.0)
            both = jnp.concatenate([left, right], axis=0)
            high = both.astype(jnp.bfloat16)
            low = (both - high.astype(jnp.float32)).astype(jnp.bfloat16)
            part = dot(jnp.concatenate([high, low], axis=0), back_ref[step * UNITS + u])
            done.append((q, part[: 2 * tokens] + part[2 * tokens :]))
        for q, part in done:
            acc_ref[q] += part
        return carry

    lax.fori_loop(0, steps, backward, 0)
    for k, out_ref in enumerate(out_refs):
        @pl.when(pl.program_id(0) == k)
        def _():
            for q in range(count):
                out_ref[pl.ds(q * 2 * tokens, 2 * tokens), :] = acc_ref[q].astype(jnp.bfloat16)
            for j, part in enumerate(split3(sums)):
                out_ref[pl.ds(count * 2 * tokens + j * count, count), :] = part


def pairs(sources, rows, targets, queries, inverse, index, turned, cands, room):
    count, tokens, dim = queries.shape[1:]
    wide = rows.shape[1]
    per_query = cands // GROUP
    slots = count * per_query
    most = (room + (GROUP - 1) * count) // GROUP + UNITS
    height = count * 2 * tokens + 3 * count
    return pl.pallas_call(
        functools.partial(pair_kernel, cands=cands, sources=len(sources)),
        grid_spec=pltpu.PrefetchScalarGridSpec(
            num_scalar_prefetch=1,
            grid=(len(sources),),
            in_specs=[
                pl.BlockSpec((count, wide), lambda i, s: (s[i], 0), memory_space=pltpu.SMEM),
                pl.BlockSpec((slots, wide), lambda i, s: (s[i], 0)),
                pl.BlockSpec((1, count, tokens, dim), lambda i, s: (s[i], 0, 0, 0)),
                pl.BlockSpec(memory_space=pltpu.VMEM),
                pl.BlockSpec(memory_space=pltpu.VMEM),
                pl.BlockSpec(memory_space=pltpu.VMEM),
            ],
            out_specs=[pl.BlockSpec((height, dim), lambda i, s: (0, 0))] * len(sources),
            scratch_shapes=[
                pltpu.SMEM((slots + per_query + 2 * UNITS,), jnp.int32),
                pltpu.VMEM((count, tokens, dim), jnp.bfloat16),
                pltpu.VMEM((count, 2 * tokens, dim), jnp.float32),
                pltpu.VMEM((slots + 8, wide), jnp.float32),
                pltpu.VMEM((slots + 8, wide), jnp.float32),
                pltpu.VMEM((slots + 8, wide), jnp.float32),
                pltpu.VMEM((most, GROUP * tokens, dim), jnp.bfloat16),
                pltpu.VMEM((UNITS, tokens, GROUP * wide), jnp.float32),
            ],
        ),
        out_shape=[jax.ShapeDtypeStruct((height, dim), jnp.bfloat16)] * len(sources),
        compiler_params=pltpu.CompilerParams(vmem_limit_bytes=VMEM_LIMIT),
        cost_estimate=pl.CostEstimate(
            flops=6 * len(sources) * room * tokens * wide * dim,
            bytes_accessed=2 * len(sources) * room * wide * dim,
            transcendentals=len(sources) * room * tokens * wide,
        ),
        name="pairs",
    )(jnp.stack(sources), rows, targets, queries, inverse, index, turned)


def neg_kernel(rows_ref, queries_ref, shard_ref, index_ref, turned_ref, inverse_ref, acc_ref, sums_ref,
               sems, unit_ref, expo_ref, total_ref, left_ref, back_ref, *, tokens):
    total = rows_ref.shape[0]
    chunk = expo_ref.shape[0]
    height, dim = queries_ref.shape
    wide = index_ref.shape[1]
    lanes = 128
    half = min(height, 256)
    for c in range(height // lanes):
        part = slice(c * lanes, (c + 1) * lanes)
        unit_ref[:, part] = rounded_queries(queries_ref[part]).T
    load_shard(shard_ref, index_ref, turned_ref, inverse_ref, sems)
    back_ref[...] = jnp.zeros_like(back_ref)
    sums_ref[...] = jnp.zeros_like(sums_ref)
    same = lax.broadcasted_iota(jnp.int32, (lanes, lanes), 0) // tokens == lax.broadcasted_iota(
        jnp.int32, (lanes, lanes), 1
    ) // tokens
    same = jnp.where(same, 1.0, 0.0).astype(jnp.bfloat16)

    def block(number, carry):
        def forward(step, carry):
            first = step * NEG_STEP
            tiles = jnp.concatenate(
                [index_ref[rows_ref[number * chunk + first + g]] for g in range(NEG_STEP)], axis=0
            )
            raw = dot(tiles, unit_ref[...])
            broad = tiles.astype(jnp.float32)
            inverse = lax.rsqrt(jnp.sum(broad * broad, axis=-1, keepdims=True) + epsilon)
            expo = jnp.exp2(raw * (inverse * (LOG2E / inner_temp)))
            for g in range(NEG_STEP):
                part = slice(g * wide, (g + 1) * wide)
                expo_ref[first + g] = (expo[part] * inverse[part]).astype(jnp.bfloat16)
                total_ref[pl.ds(first + g, 1), :] = jnp.sum(expo[part], axis=0, keepdims=True)
            return carry

        lax.fori_loop(0, chunk // NEG_STEP, forward, 0)
        for c in range(height // lanes):
            part = slice(c * lanes, (c + 1) * lanes)
            totals = total_ref[:, part]
            pieces = [dot(piece, same) for piece in split3(jnp.log(totals))]
            lift = jnp.exp(inner_temp * (pieces[0] + pieces[1] + pieces[2]))
            left_ref[:, part] = lift / totals
            sums_ref[:, part] += jnp.broadcast_to(jnp.sum(lift, axis=0, keepdims=True), (8, lanes))
        for c in range(height // half):
            part = slice(c * half, (c + 1) * half)

            def backward(step, acc):
                for g in range(NEG_STEP):
                    k = step * NEG_STEP + g
                    tile = turned_ref[rows_ref[number * chunk + k]]
                    acc = acc + dot(tile, expo_ref[k, :, part]) * left_ref[pl.ds(k, 1), part]
                return acc

            back_ref[:, part] = lax.fori_loop(0, chunk // NEG_STEP, backward, back_ref[:, part])
        return carry

    lax.fori_loop(0, total // chunk, block, 0)
    for c in range(height // lanes):
        part = slice(c * lanes, (c + 1) * lanes)
        acc_ref[part, :] = back_ref[:, part].T


def negatives(rows, queries, index):
    total = rows.shape[0]
    count, tokens, dim = queries.shape
    wide = index.shape[1]
    height = count * tokens
    chunk = math.gcd(total, NEG_CHUNK)
    return pl.pallas_call(
        functools.partial(neg_kernel, tokens=tokens),
        in_specs=[
            pl.BlockSpec(memory_space=pltpu.SMEM),
            pl.BlockSpec(memory_space=pltpu.VMEM),
            pl.BlockSpec(memory_space=pltpu.HBM),
        ],
        out_specs=[pl.BlockSpec(memory_space=pltpu.VMEM)] * 5,
        out_shape=[
            pltpu.VMEM(index.shape, jnp.bfloat16),
            pltpu.VMEM((index.shape[0], dim, wide), jnp.bfloat16),
            pltpu.VMEM((index.shape[0], wide), jnp.float32),
            jax.ShapeDtypeStruct((height, dim), jnp.float32),
            jax.ShapeDtypeStruct((8, height), jnp.float32),
        ],
        scratch_shapes=[
            pltpu.SemaphoreType.DMA((LOADS,)),
            pltpu.VMEM((dim, height), jnp.bfloat16),
            pltpu.VMEM((chunk, wide, height), jnp.bfloat16),
            pltpu.VMEM((chunk, height), jnp.float32),
            pltpu.VMEM((chunk, height), jnp.float32),
            pltpu.VMEM((dim, height), jnp.float32),
        ],
        compiler_params=pltpu.CompilerParams(vmem_limit_bytes=VMEM_LIMIT),
        cost_estimate=pl.CostEstimate(
            flops=4 * total * height * wide * dim,
            bytes_accessed=2 * total * wide * dim,
            transcendentals=total * height * wide,
        ),
        name="negatives",
    )(rows, queries.reshape(height, dim), pltpu.with_memory_space_constraint(index, pltpu.HBM))


def finish_kernel(queries_ref, teacher_ref, back_ref, sums_ref, *refs, owners):
    messages, (loss_ref, grad_ref) = refs[:owners], refs[owners:]
    count, tokens, dim = grad_ref.shape
    cut = count * 2 * tokens
    scores = jnp.zeros((count, dim), jnp.float32)
    for message in messages:
        for k in range(3):
            scores = scores + message[cut + k * count : cut + (k + 1) * count, :].astype(jnp.float32)
    totals = []
    for q in range(count):
        total = scores[q : q + 1, 0:1] + sums_ref[0:1, q * tokens : q * tokens + 1]
        totals.append(total)
        pulled = back_ref[q * tokens : (q + 1) * tokens, :]
        right = jnp.zeros((tokens, dim), jnp.float32)
        for message in messages:
            pulled = pulled + message[q * 2 * tokens : (q * 2 + 1) * tokens, :].astype(jnp.float32)
            right = right + message[(q * 2 + 1) * tokens : (q + 1) * 2 * tokens, :].astype(jnp.float32)
        pulled = pulled / total - right
        wide = queries_ref[q].astype(jnp.float32)
        radius = jnp.sqrt(jnp.sum(wide * wide, axis=-1, keepdims=True) + epsilon)
        unit = wide / radius
        grad_ref[q] = (pulled - unit * jnp.sum(unit * pulled, axis=-1, keepdims=True)) / radius
    spread = jnp.log(jnp.concatenate(totals, axis=0))
    teacher = teacher_ref[...]
    log_target = teacher - jnp.log(jnp.sum(jnp.exp(teacher), axis=-1, keepdims=True))
    gain = jnp.sum(jnp.exp(log_target) * (log_target + spread), axis=-1, keepdims=True)
    loss_ref[...] = gain - scores[:, dim // 2 : dim // 2 + 1] + jnp.zeros_like(loss_ref)


def finish(queries, teacher, back, sums, messages):
    count, tokens, dim = queries.shape
    owners = len(messages)
    return pl.pallas_call(
        functools.partial(finish_kernel, owners=owners),
        in_specs=[pl.BlockSpec(memory_space=pltpu.VMEM)] * (4 + owners),
        out_specs=[pl.BlockSpec(memory_space=pltpu.VMEM)] * 2,
        out_shape=[
            jax.ShapeDtypeStruct((count, dim), jnp.float32),
            jax.ShapeDtypeStruct((count, tokens, dim), jnp.float32),
        ],
        compiler_params=pltpu.CompilerParams(vmem_limit_bytes=VMEM_LIMIT),
        name="finish",
    )(queries, teacher, back, sums, *messages)


def on_device(queries, index, cand_owner, cand_row, neg_row, teacher):
    count, tokens, dim = queries.shape
    cands = cand_row.shape[1]
    shard = index.shape[0]
    owners = lax.axis_size("corpus")
    room = (2 * count * cands + owners - 1) // owners
    me = lax.axis_index("corpus").astype(jnp.int32)
    group = lax.axis_size("blk")

    def from_step(value, axis, size, step):
        return lax.ppermute(value, axis, [((i + step) % size, i) for i in range(size)])

    def gathered(value, axis, size):
        return [value] + [from_step(value, axis, size, step) for step in range(1, size)]

    code = (cand_owner[..., 0] * shard + cand_row).astype(jnp.float32)
    meta = jnp.concatenate([code, teacher], axis=1)
    all_neg = jnp.concatenate(gathered(neg_row, "blk", group), axis=0).reshape(-1)
    def told(value):
        copies = jnp.broadcast_to(value[None], (owners,) + value.shape)
        return lax.all_to_all(copies, "corpus", split_axis=0, concat_axis=0, tiled=True)

    all_meta = told(meta).reshape(owners * count, -1)
    all_queries = told(queries)
    index, turned, inverse, neg_acc, neg_sum = negatives(all_neg, queries, index)
    rows, targets = prep(me.reshape(1), all_meta, index, turned, shard, cands)
    messages = []
    order = list(range(1, owners)) + [0]
    for first in range(0, owners, SOURCES):
        steps = order[first : first + SOURCES]
        sources = [lax.rem(me + step, owners) for step in steps]
        found = pairs(
            sources, rows, targets, all_queries, inverse, index, turned, cands, room
        )
        for step, message in zip(steps, found):
            if step:
                message = lax.ppermute(
                    message, "corpus", [(i, (i + step) % owners) for i in range(owners)]
                )
            messages.append(message)
    losses, query_grads = finish(queries, teacher, neg_acc, neg_sum, messages)
    return (losses[:, 0], query_grads)


def solution(mesh):
    placed = (
        P(("corpus", "blk"), None, None),
        P("corpus", None, None),
        P(("corpus", "blk"), None, None),
        P(("corpus", "blk"), None),
        P(("corpus", "blk"), None),
        P(("corpus", "blk"), None),
    )
    return jax.shard_map(
        on_device,
        mesh=mesh,
        in_specs=placed,
        out_specs=(P(("corpus", "blk")), P(("corpus", "blk"), None, None)),
        check_vma=False,
    )
```

```python
import functools
import math

import jax
import jax.numpy as jnp
from jax import lax
from jax.experimental import pallas as pl
from jax.experimental.pallas import tpu as pltpu
from jax.sharding import PartitionSpec as P

inner_temp = 0.1
epsilon = 1e-06
LOG2E = 1.4426950408889634
GROUP = 4
UNITS = 8
LOADS = 8
LOAD_STEP = 16
NEG_STEP = 8
NEG_CHUNK = 24
SOURCES = 2
VMEM_LIMIT = 12 * 1024 * 1024
LAST = (((1,), (1,)), ((), ()))


def dot_last(a, b):
    return lax.dot_general(a, b, LAST, preferred_element_type=jnp.float32)


def dot(a, b):
    return jnp.dot(a, b, preferred_element_type=jnp.float32)


def split3(x):
    high = x.astype(jnp.bfloat16)
    rest = x - high.astype(jnp.float32)
    mid = rest.astype(jnp.bfloat16)
    low = (rest - mid.astype(jnp.float32)).astype(jnp.bfloat16)
    return high, mid, low


def rounded_queries(raw):
    wide = raw.astype(jnp.float32)
    radius = jnp.sqrt(jnp.sum(wide * wide, axis=-1, keepdims=True) + epsilon)
    return (wide / radius).astype(jnp.bfloat16)


def load_shard(index_ref, tiles_ref, turned_ref, inverse_ref, sems):
    count = index_ref.shape[0]
    chunk = count // LOADS

    def copy(part):
        at = pl.ds(part * chunk, chunk)
        return pltpu.make_async_copy(index_ref.at[at], tiles_ref.at[at], sems.at[part])

    for part in range(LOADS):
        copy(part).start()

    for part in range(LOADS):
        copy(part).wait()

        def body(step, carry):
            first = part * chunk + step * LOAD_STEP
            squares = []
            turned = []
            for k in range(LOAD_STEP):
                tile = tiles_ref[first + k].T
                turned.append(tile)
                wide = tile.astype(jnp.float32)
                squares.append(jnp.sum(wide * wide, axis=0, keepdims=True))
            for k in range(LOAD_STEP):
                turned_ref[first + k] = turned[k]
            at = pl.ds(pl.multiple_of(first, LOAD_STEP), LOAD_STEP)
            inverse_ref[at, :] = lax.rsqrt(jnp.concatenate(squares, axis=0) + epsilon)
            return carry

        lax.fori_loop(0, chunk // LOAD_STEP, body, 0)


def prep_kernel(me_ref, meta_ref, rows_ref, target_ref, value_ref, place_ref, result_ref, *, shard, cands):
    count = meta_ref.shape[0]
    code = meta_ref[:, :cands]
    owner = jnp.floor((code + 0.5) * (1.0 / shard))
    row = code - owner * shard
    teacher = meta_ref[:, cands:]
    log_target = teacher - jnp.log(jnp.sum(jnp.exp(teacher), axis=-1, keepdims=True))
    target = jnp.exp(log_target)
    mine = (owner == me_ref[0].astype(jnp.float32)).astype(jnp.float32)
    before = lax.broadcasted_iota(jnp.int32, (cands, cands), 0) < lax.broadcasted_iota(
        jnp.int32, (cands, cands), 1
    )
    place = dot(mine.astype(jnp.bfloat16), before.astype(jnp.float32).astype(jnp.bfloat16))
    wide = value_ref.shape[1]
    pad = jnp.zeros((count, wide - cands), jnp.float32)
    place_ref[...] = jnp.concatenate([jnp.where(mine > 0, place, -1.0), pad - 1.0], axis=1)
    row_high = jnp.floor(row * (1.0 / 16))
    first, second, third = split3(target)
    values = [row_high, row - 16 * row_high, first, second, third]
    for v in range(8):
        value = values[v].astype(jnp.float32) if v < len(values) else jnp.zeros_like(row)
        value_ref[pl.ds(v, count, stride=8), :] = jnp.concatenate([value, pad], axis=1)
    spots = lax.broadcasted_iota(jnp.int32, (wide, wide), 0).astype(jnp.float32)

    def body(step, carry):
        for k in range(8):
            q = step * 8 + k
            hot = jnp.where(place_ref[pl.ds(q, 1), :] == spots, 1.0, 0.0).astype(jnp.bfloat16)
            at = pl.ds(pl.multiple_of(q * 8, 8), 8)
            result_ref[at, :] = dot_last(value_ref[at, :].astype(jnp.bfloat16), hot)
        return carry

    lax.fori_loop(0, count // 8, body, 0)
    result = [result_ref[pl.ds(v, count, stride=8), :] for v in range(5)]
    found = jnp.sum(mine, axis=-1, keepdims=True)
    lane = lax.broadcasted_iota(jnp.int32, (count, wide), 1)
    rows = 16 * result[0] + result[1]
    rows_ref[...] = jnp.where(lane < cands, rows, found).astype(jnp.int32)
    listed = jnp.where(lane.astype(jnp.float32) < found, result[2] + result[3] + result[4], -1.0)
    stacked = jnp.concatenate(split3(listed), axis=0)
    steps = cands // GROUP
    source = lax.broadcasted_iota(jnp.int32, (wide, wide), 0)
    block = lax.broadcasted_iota(jnp.int32, (wide, wide), 1) // (wide // GROUP)
    for t in range(steps):
        pick = jnp.where(source == block + t * GROUP, 1.0, 0.0).astype(jnp.bfloat16)
        spread = dot(stacked, pick)
        target_ref[pl.ds(t, count, stride=steps), :] = (
            spread[:count] + spread[count : 2 * count] + spread[2 * count :]
        )


def prep(me, meta, shard, cands):
    count = meta.shape[0]
    wide = 128
    return pl.pallas_call(
        functools.partial(prep_kernel, shard=shard, cands=cands),
        in_specs=[
            pl.BlockSpec(memory_space=pltpu.SMEM),
            pl.BlockSpec(memory_space=pltpu.VMEM),
        ],
        out_specs=[pl.BlockSpec(memory_space=pltpu.VMEM)] * 2,
        out_shape=[
            jax.ShapeDtypeStruct((count, wide), jnp.int32),
            jax.ShapeDtypeStruct((count * (cands // GROUP), wide), jnp.float32),
        ],
        scratch_shapes=[
            pltpu.VMEM((count * 8, wide), jnp.float32),
            pltpu.VMEM((count, wide), jnp.float32),
            pltpu.VMEM((count * 8, wide), jnp.float32),
        ],
        compiler_params=pltpu.CompilerParams(vmem_limit_bytes=VMEM_LIMIT),
        cost_estimate=pl.CostEstimate(flops=count * wide, bytes_accessed=count * wide, transcendentals=0),
        name="prep",
    )(me, meta)


def pair_kernel(source_ref, rows_ref, target_ref, queries_ref, inverse_ref, index_ref, turned_ref, *refs, cands, sources):
    out_refs = refs[:sources]
    (units_ref, unit_ref, acc_ref, total_ref, left_ref, right_ref, back_ref, raw_ref) = refs[sources:]
    count, tokens, dim = unit_ref.shape
    wide = rows_ref.shape[1]
    per_query = cands // GROUP
    slots = count * per_query
    bits = per_query.bit_length() - 1
    total = jnp.int32(0)
    for q in range(count):
        for t in range(per_query):
            units_ref[total + t] = jnp.int32(q * per_query + t)
        total = total + lax.div(rows_ref[q, cands] + (GROUP - 1), GROUP)
    for t in range(2 * UNITS):
        units_ref[total + t] = jnp.int32(slots)
    steps = lax.div(total + (UNITS - 1), UNITS)

    def entry(number):
        slot = units_ref[number]
        q = jnp.minimum(lax.shift_right_logical(slot, bits), count - 1)
        return slot, q, jnp.bitwise_and(slot, per_query - 1) * GROUP

    for q in range(count):
        unit_ref[q] = rounded_queries(queries_ref[0, q])
    acc_ref[...] = jnp.zeros_like(acc_ref)
    ones = jnp.ones((8, wide), jnp.bfloat16)

    def tiles_of(number, ref):
        _, q, base = entry(number)
        return q, [ref[rows_ref[q, base + g]] for g in range(GROUP)]

    def multiply(step):
        found = []
        for u in range(UNITS):
            q, tiles = tiles_of(step * UNITS + u, turned_ref)
            found.append(dot(unit_ref[q], jnp.concatenate(tiles, axis=1)))
        return found

    def forward(step, carry):
        expos, weights = [], []
        for u in range(UNITS):
            _, q, base = entry(step * UNITS + u)
            for g in range(GROUP):
                inverse = inverse_ref[pl.ds(rows_ref[q, base + g], 1), :]
                raw = raw_ref[u, :, g * wide : (g + 1) * wide]
                expo = jnp.exp2(raw * (inverse * (LOG2E / inner_temp)))
                expos.append(expo.astype(jnp.bfloat16))
                weights.append((expo * inverse).astype(jnp.bfloat16))
        following = multiply(step + 1)
        backs = []
        for u in range(UNITS):
            _, tiles = tiles_of(step * UNITS + u, index_ref)
            for g in range(0, GROUP, 2):
                k = u * GROUP + g
                part = dot(
                    jnp.concatenate(weights[k : k + 2], axis=0),
                    jnp.concatenate(tiles[g : g + 2], axis=1),
                )
                backs += [part[:tokens, :dim], part[tokens:, dim:]]
        totals = []
        for u in range(0, UNITS, 2):
            part = dot_last(ones, jnp.concatenate(expos[u * GROUP : (u + 2) * GROUP], axis=0))
            totals += [part[0:1, :wide], part[0:1, wide:]]
        for u in range(UNITS):
            back_ref[step * UNITS + u] = jnp.concatenate(
                backs[u * GROUP : (u + 1) * GROUP], axis=0
            ).astype(jnp.bfloat16)
            total_ref[pl.ds(units_ref[step * UNITS + u], 1), :] = totals[u]
        for u in range(UNITS):
            raw_ref[u] = following[u]
        return carry

    for u, raw in enumerate(multiply(0)):
        raw_ref[u] = raw
    lax.fori_loop(0, steps, forward, 0)

    target = target_ref[...]
    held = target >= 0.0
    totals = jnp.where(held, total_ref[0:slots, :], 1.0)
    target = jnp.where(held, target, 0.0)
    same = lax.broadcasted_iota(jnp.int32, (wide, wide), 0) // tokens == lax.broadcasted_iota(
        jnp.int32, (wide, wide), 1
    ) // tokens
    same = jnp.where(same, 1.0, 0.0).astype(jnp.bfloat16)
    parts = [dot(part, same) for part in split3(jnp.log(totals))]
    score = inner_temp * (parts[0] + parts[1] + parts[2])
    lift = jnp.where(held, jnp.exp(score), 0.0)
    recip = 1.0 / totals
    left_ref[0:slots, :] = lift * recip
    right_ref[0:slots, :] = target * recip
    left_ref[slots:, :] = jnp.zeros_like(left_ref[slots:, :])
    right_ref[slots:, :] = jnp.zeros_like(right_ref[slots:, :])

    def per_source(values):
        rows = jnp.sum(values.reshape(count, per_query, wide), axis=1)
        return jnp.sum(rows, axis=-1, keepdims=True) * (1.0 / tokens)

    lane = lax.broadcasted_iota(jnp.int32, (count, wide), 1)
    sums = jnp.where(lane < wide // 2, per_source(lift), per_source(target * score))
    diagonal = lax.broadcasted_iota(jnp.int32, (tokens, wide), 0) == lax.broadcasted_iota(
        jnp.int32, (tokens, wide), 1
    ) % tokens

    def backward(step, carry):
        owners, sides = [], []
        for u in range(UNITS):
            slot, q, _ = entry(step * UNITS + u)
            left = jnp.where(diagonal, left_ref[pl.ds(slot, 1), :], 0.0)
            right = jnp.where(diagonal, right_ref[pl.ds(slot, 1), :], 0.0)
            both = jnp.concatenate([left, right], axis=0)
            high = both.astype(jnp.bfloat16)
            sides += [high, (both - high.astype(jnp.float32)).astype(jnp.bfloat16)]
            owners.append(q)
        parts = []
        for u in range(0, UNITS, 2):
            pulled = dot(
                jnp.concatenate(sides[2 * u : 2 * u + 4], axis=0),
                jnp.concatenate([back_ref[step * UNITS + u], back_ref[step * UNITS + u + 1]], axis=1),
            )
            height = 2 * tokens
            parts += [
                pulled[:height, :dim] + pulled[height : 2 * height, :dim],
                pulled[2 * height : 3 * height, dim:] + pulled[3 * height :, dim:],
            ]
        for q, part in zip(owners, parts):
            acc_ref[q] += part
        return carry

    lax.fori_loop(0, steps, backward, 0)
    for k, out_ref in enumerate(out_refs):
        @pl.when(pl.program_id(0) == k)
        def _():
            for q in range(count):
                out_ref[pl.ds(q * 2 * tokens, 2 * tokens), :] = acc_ref[q].astype(jnp.bfloat16)
            for j, part in enumerate(split3(sums)):
                out_ref[pl.ds(count * 2 * tokens + j * count, count), :] = part


def pairs(sources, rows, targets, queries, inverse, index, turned, cands, room):
    count, tokens, dim = queries.shape[1:]
    wide = rows.shape[1]
    per_query = cands // GROUP
    slots = count * per_query
    most = (room + (GROUP - 1) * count) // GROUP + UNITS
    height = count * 2 * tokens + 3 * count
    return pl.pallas_call(
        functools.partial(pair_kernel, cands=cands, sources=len(sources)),
        grid_spec=pltpu.PrefetchScalarGridSpec(
            num_scalar_prefetch=1,
            grid=(len(sources),),
            in_specs=[
                pl.BlockSpec((count, wide), lambda i, s: (s[i], 0), memory_space=pltpu.SMEM),
                pl.BlockSpec((slots, wide), lambda i, s: (s[i], 0)),
                pl.BlockSpec((1, count, tokens, dim), lambda i, s: (s[i], 0, 0, 0)),
                pl.BlockSpec(memory_space=pltpu.VMEM),
                pl.BlockSpec(memory_space=pltpu.VMEM),
                pl.BlockSpec(memory_space=pltpu.VMEM),
            ],
            out_specs=[pl.BlockSpec((height, dim), lambda i, s: (0, 0))] * len(sources),
            scratch_shapes=[
                pltpu.SMEM((slots + per_query + 2 * UNITS,), jnp.int32),
                pltpu.VMEM((count, tokens, dim), jnp.bfloat16),
                pltpu.VMEM((count, 2 * tokens, dim), jnp.float32),
                pltpu.VMEM((slots + 8, wide), jnp.float32),
                pltpu.VMEM((slots + 8, wide), jnp.float32),
                pltpu.VMEM((slots + 8, wide), jnp.float32),
                pltpu.VMEM((most, GROUP * tokens, dim), jnp.bfloat16),
                pltpu.VMEM((UNITS, tokens, GROUP * wide), jnp.float32),
            ],
        ),
        out_shape=[jax.ShapeDtypeStruct((height, dim), jnp.bfloat16)] * len(sources),
        compiler_params=pltpu.CompilerParams(vmem_limit_bytes=VMEM_LIMIT),
        cost_estimate=pl.CostEstimate(
            flops=6 * len(sources) * room * tokens * wide * dim,
            bytes_accessed=2 * len(sources) * room * wide * dim,
            transcendentals=len(sources) * room * tokens * wide,
        ),
        name="pairs",
    )(jnp.stack(sources), rows, targets, queries, inverse, index, turned)


def neg_kernel(rows_ref, queries_ref, shard_ref, index_ref, turned_ref, inverse_ref, acc_ref, sums_ref,
               sems, unit_ref, expo_ref, total_ref, left_ref, back_ref, *, tokens):
    total = rows_ref.shape[0]
    chunk = expo_ref.shape[0]
    height, dim = queries_ref.shape
    wide = index_ref.shape[1]
    lanes = 128
    half = min(height, 256)
    for c in range(height // lanes):
        part = slice(c * lanes, (c + 1) * lanes)
        unit_ref[:, part] = rounded_queries(queries_ref[part]).T
    load_shard(shard_ref, index_ref, turned_ref, inverse_ref, sems)
    back_ref[...] = jnp.zeros_like(back_ref)
    sums_ref[...] = jnp.zeros_like(sums_ref)
    same = lax.broadcasted_iota(jnp.int32, (lanes, lanes), 0) // tokens == lax.broadcasted_iota(
        jnp.int32, (lanes, lanes), 1
    ) // tokens
    same = jnp.where(same, 1.0, 0.0).astype(jnp.bfloat16)

    def block(number, carry):
        def forward(step, carry):
            first = step * NEG_STEP
            tiles = jnp.concatenate(
                [index_ref[rows_ref[number * chunk + first + g]] for g in range(NEG_STEP)], axis=0
            )
            raw = dot(tiles, unit_ref[...])
            broad = tiles.astype(jnp.float32)
            inverse = lax.rsqrt(jnp.sum(broad * broad, axis=-1, keepdims=True) + epsilon)
            expo = jnp.exp2(raw * (inverse * (LOG2E / inner_temp)))
            for g in range(NEG_STEP):
                part = slice(g * wide, (g + 1) * wide)
                expo_ref[first + g] = (expo[part] * inverse[part]).astype(jnp.bfloat16)
                total_ref[pl.ds(first + g, 1), :] = jnp.sum(expo[part], axis=0, keepdims=True)
            return carry

        lax.fori_loop(0, chunk // NEG_STEP, forward, 0)
        for c in range(height // lanes):
            part = slice(c * lanes, (c + 1) * lanes)
            totals = total_ref[:, part]
            pieces = [dot(piece, same) for piece in split3(jnp.log(totals))]
            lift = jnp.exp(inner_temp * (pieces[0] + pieces[1] + pieces[2]))
            left_ref[:, part] = lift / totals
            sums_ref[:, part] += jnp.broadcast_to(jnp.sum(lift, axis=0, keepdims=True), (8, lanes))
        for c in range(height // half):
            part = slice(c * half, (c + 1) * half)

            def backward(step, acc):
                for g in range(NEG_STEP):
                    k = step * NEG_STEP + g
                    tile = turned_ref[rows_ref[number * chunk + k]]
                    acc = acc + dot(tile, expo_ref[k, :, part]) * left_ref[pl.ds(k, 1), part]
                return acc

            back_ref[:, part] = lax.fori_loop(0, chunk // NEG_STEP, backward, back_ref[:, part])
        return carry

    lax.fori_loop(0, total // chunk, block, 0)
    for c in range(height // lanes):
        part = slice(c * lanes, (c + 1) * lanes)
        acc_ref[part, :] = back_ref[:, part].T


def negatives(rows, queries, index):
    total = rows.shape[0]
    count, tokens, dim = queries.shape
    wide = index.shape[1]
    height = count * tokens
    chunk = math.gcd(total, NEG_CHUNK)
    return pl.pallas_call(
        functools.partial(neg_kernel, tokens=tokens),
        in_specs=[
            pl.BlockSpec(memory_space=pltpu.SMEM),
            pl.BlockSpec(memory_space=pltpu.VMEM),
            pl.BlockSpec(memory_space=pltpu.HBM),
        ],
        out_specs=[pl.BlockSpec(memory_space=pltpu.VMEM)] * 5,
        out_shape=[
            pltpu.VMEM(index.shape, jnp.bfloat16),
            pltpu.VMEM((index.shape[0], dim, wide), jnp.bfloat16),
            pltpu.VMEM((index.shape[0], wide), jnp.float32),
            jax.ShapeDtypeStruct((height, dim), jnp.float32),
            jax.ShapeDtypeStruct((8, height), jnp.float32),
        ],
        scratch_shapes=[
            pltpu.SemaphoreType.DMA((LOADS,)),
            pltpu.VMEM((dim, height), jnp.bfloat16),
            pltpu.VMEM((chunk, wide, height), jnp.bfloat16),
            pltpu.VMEM((chunk, height), jnp.float32),
            pltpu.VMEM((chunk, height), jnp.float32),
            pltpu.VMEM((dim, height), jnp.float32),
        ],
        compiler_params=pltpu.CompilerParams(vmem_limit_bytes=VMEM_LIMIT),
        cost_estimate=pl.CostEstimate(
            flops=4 * total * height * wide * dim,
            bytes_accessed=2 * total * wide * dim,
            transcendentals=total * height * wide,
        ),
        name="negatives",
    )(rows, queries.reshape(height, dim), pltpu.with_memory_space_constraint(index, pltpu.HBM))


def finish_kernel(queries_ref, teacher_ref, back_ref, sums_ref, *refs, owners):
    messages, (loss_ref, grad_ref) = refs[:owners], refs[owners:]
    count, tokens, dim = grad_ref.shape
    cut = count * 2 * tokens
    scores = jnp.zeros((count, dim), jnp.float32)
    for message in messages:
        for k in range(3):
            scores = scores + message[cut + k * count : cut + (k + 1) * count, :].astype(jnp.float32)
    totals = []
    for q in range(count):
        total = scores[q : q + 1, 0:1] + sums_ref[0:1, q * tokens : q * tokens + 1]
        totals.append(total)
        pulled = back_ref[q * tokens : (q + 1) * tokens, :]
        right = jnp.zeros((tokens, dim), jnp.float32)
        for message in messages:
            pulled = pulled + message[q * 2 * tokens : (q * 2 + 1) * tokens, :].astype(jnp.float32)
            right = right + message[(q * 2 + 1) * tokens : (q + 1) * 2 * tokens, :].astype(jnp.float32)
        pulled = pulled / total - right
        wide = queries_ref[q].astype(jnp.float32)
        radius = jnp.sqrt(jnp.sum(wide * wide, axis=-1, keepdims=True) + epsilon)
        unit = wide / radius
        grad_ref[q] = (pulled - unit * jnp.sum(unit * pulled, axis=-1, keepdims=True)) / radius
    spread = jnp.log(jnp.concatenate(totals, axis=0))
    teacher = teacher_ref[...]
    log_target = teacher - jnp.log(jnp.sum(jnp.exp(teacher), axis=-1, keepdims=True))
    gain = jnp.sum(jnp.exp(log_target) * (log_target + spread), axis=-1, keepdims=True)
    loss_ref[...] = gain - scores[:, dim // 2 : dim // 2 + 1] + jnp.zeros_like(loss_ref)


def finish(queries, teacher, back, sums, messages):
    count, tokens, dim = queries.shape
    owners = len(messages)
    return pl.pallas_call(
        functools.partial(finish_kernel, owners=owners),
        in_specs=[pl.BlockSpec(memory_space=pltpu.VMEM)] * (4 + owners),
        out_specs=[pl.BlockSpec(memory_space=pltpu.VMEM)] * 2,
        out_shape=[
            jax.ShapeDtypeStruct((count, dim), jnp.float32),
            jax.ShapeDtypeStruct((count, tokens, dim), jnp.float32),
        ],
        compiler_params=pltpu.CompilerParams(vmem_limit_bytes=VMEM_LIMIT),
        name="finish",
    )(queries, teacher, back, sums, *messages)


def on_device(queries, index, cand_owner, cand_row, neg_row, teacher):
    count, tokens, dim = queries.shape
    cands = cand_row.shape[1]
    shard = index.shape[0]
    owners = lax.axis_size("corpus")
    room = (2 * count * cands + owners - 1) // owners
    me = lax.axis_index("corpus").astype(jnp.int32)
    group = lax.axis_size("blk")

    def from_step(value, axis, size, step):
        return lax.ppermute(value, axis, [((i + step) % size, i) for i in range(size)])

    def gathered(value, axis, size):
        return [value] + [from_step(value, axis, size, step) for step in range(1, size)]

    code = (cand_owner[..., 0] * shard + cand_row).astype(jnp.float32)
    meta = jnp.concatenate([code, teacher], axis=1)
    all_neg = jnp.concatenate(gathered(neg_row, "blk", group), axis=0).reshape(-1)
    def told(value):
        copies = jnp.broadcast_to(value[None], (owners,) + value.shape)
        return lax.all_to_all(copies, "corpus", split_axis=0, concat_axis=0, tiled=True)

    all_meta = told(meta).reshape(owners * count, -1)
    all_queries = told(queries)
    rows, targets = prep(me.reshape(1), all_meta, shard, cands)
    rows, all_neg = lax.optimization_barrier((rows, all_neg))
    index, turned, inverse, neg_acc, neg_sum = negatives(all_neg, queries, index)
    messages = []
    order = list(range(1, owners)) + [0]
    groups = [order[first : first + SOURCES] for first in range(0, owners, SOURCES)]
    groups = groups[:-1] + [groups[-1][:-1], groups[-1][-1:]]
    for steps in groups:
        sources = [lax.rem(me + step, owners) for step in steps]
        found = pairs(
            sources, rows, targets, all_queries, inverse, index, turned, cands, room
        )
        for step, message in zip(steps, found):
            if step:
                message = lax.ppermute(
                    message, "corpus", [(i, (i + step) % owners) for i in range(owners)]
                )
            messages.append(message)
    losses, query_grads = finish(queries, teacher, neg_acc, neg_sum, messages)
    return (losses[:, 0], query_grads)


def solution(mesh):
    placed = (
        P(("corpus", "blk"), None, None),
        P("corpus", None, None),
        P(("corpus", "blk"), None, None),
        P(("corpus", "blk"), None),
        P(("corpus", "blk"), None),
        P(("corpus", "blk"), None),
    )
    return jax.shard_map(
        on_device,
        mesh=mesh,
        in_specs=placed,
        out_specs=(P(("corpus", "blk")), P(("corpus", "blk"), None, None)),
        check_vma=False,
    )
```

```python
import functools
import math

import jax
import jax.numpy as jnp
from jax import lax
from jax.experimental import pallas as pl
from jax.experimental.pallas import tpu as pltpu
from jax.sharding import PartitionSpec as P

inner_temp = 0.1
epsilon = 1e-06
LOG2E = 1.4426950408889634
GROUP = 4
UNITS = 12
LOADS = 8
LOAD_STEP = 16
NEG_STEP = 8
NEG_CHUNK = 24
SOURCES = 2
VMEM_LIMIT = 12 * 1024 * 1024
LAST = (((1,), (1,)), ((), ()))


def dot_last(a, b):
    return lax.dot_general(a, b, LAST, preferred_element_type=jnp.float32)


def dot(a, b):
    return jnp.dot(a, b, preferred_element_type=jnp.float32)


def split3(x):
    high = x.astype(jnp.bfloat16)
    rest = x - high.astype(jnp.float32)
    mid = rest.astype(jnp.bfloat16)
    low = (rest - mid.astype(jnp.float32)).astype(jnp.bfloat16)
    return high, mid, low


def rounded_queries(raw):
    wide = raw.astype(jnp.float32)
    radius = jnp.sqrt(jnp.sum(wide * wide, axis=-1, keepdims=True) + epsilon)
    return (wide / radius).astype(jnp.bfloat16)


def load_shard(index_ref, tiles_ref, turned_ref, inverse_ref, sems):
    count = index_ref.shape[0]
    chunk = count // LOADS

    def copy(part):
        at = pl.ds(part * chunk, chunk)
        return pltpu.make_async_copy(index_ref.at[at], tiles_ref.at[at], sems.at[part])

    for part in range(LOADS):
        copy(part).start()

    for part in range(LOADS):
        copy(part).wait()

        def body(step, carry):
            first = part * chunk + step * LOAD_STEP
            squares = []
            turned = []
            for k in range(LOAD_STEP):
                tile = tiles_ref[first + k].T
                turned.append(tile)
                wide = tile.astype(jnp.float32)
                squares.append(jnp.sum(wide * wide, axis=0, keepdims=True))
            for k in range(LOAD_STEP):
                turned_ref[first + k] = turned[k]
            at = pl.ds(pl.multiple_of(first, LOAD_STEP), LOAD_STEP)
            inverse_ref[at, :] = lax.rsqrt(jnp.concatenate(squares, axis=0) + epsilon)
            return carry

        lax.fori_loop(0, chunk // LOAD_STEP, body, 0)


def prep_kernel(me_ref, meta_ref, rows_ref, target_ref, value_ref, place_ref, result_ref, *, shard, cands):
    count = meta_ref.shape[0]
    code = meta_ref[:, :cands]
    owner = jnp.floor((code + 0.5) * (1.0 / shard))
    row = code - owner * shard
    teacher = meta_ref[:, cands:]
    log_target = teacher - jnp.log(jnp.sum(jnp.exp(teacher), axis=-1, keepdims=True))
    target = jnp.exp(log_target)
    mine = (owner == me_ref[0].astype(jnp.float32)).astype(jnp.float32)
    before = lax.broadcasted_iota(jnp.int32, (cands, cands), 0) < lax.broadcasted_iota(
        jnp.int32, (cands, cands), 1
    )
    place = dot(mine.astype(jnp.bfloat16), before.astype(jnp.float32).astype(jnp.bfloat16))
    wide = value_ref.shape[1]
    pad = jnp.zeros((count, wide - cands), jnp.float32)
    place_ref[...] = jnp.concatenate([jnp.where(mine > 0, place, -1.0), pad - 1.0], axis=1)
    row_high = jnp.floor(row * (1.0 / 16))
    first, second, third = split3(target)
    values = [row_high, row - 16 * row_high, first, second, third]
    for v in range(8):
        value = values[v].astype(jnp.float32) if v < len(values) else jnp.zeros_like(row)
        value_ref[pl.ds(v, count, stride=8), :] = jnp.concatenate([value, pad], axis=1)
    spots = lax.broadcasted_iota(jnp.int32, (wide, wide), 0).astype(jnp.float32)

    def body(step, carry):
        for k in range(8):
            q = step * 8 + k
            hot = jnp.where(place_ref[pl.ds(q, 1), :] == spots, 1.0, 0.0).astype(jnp.bfloat16)
            at = pl.ds(pl.multiple_of(q * 8, 8), 8)
            result_ref[at, :] = dot_last(value_ref[at, :].astype(jnp.bfloat16), hot)
        return carry

    lax.fori_loop(0, count // 8, body, 0)
    result = [result_ref[pl.ds(v, count, stride=8), :] for v in range(5)]
    found = jnp.sum(mine, axis=-1, keepdims=True)
    lane = lax.broadcasted_iota(jnp.int32, (count, wide), 1)
    rows = 16 * result[0] + result[1]
    rows_ref[...] = jnp.where(lane < cands, rows, found).astype(jnp.int32)
    listed = jnp.where(lane.astype(jnp.float32) < found, result[2] + result[3] + result[4], -1.0)
    stacked = jnp.concatenate(split3(listed), axis=0)
    steps = cands // GROUP
    source = lax.broadcasted_iota(jnp.int32, (wide, wide), 0)
    block = lax.broadcasted_iota(jnp.int32, (wide, wide), 1) // (wide // GROUP)
    for t in range(steps):
        pick = jnp.where(source == block + t * GROUP, 1.0, 0.0).astype(jnp.bfloat16)
        spread = dot(stacked, pick)
        target_ref[pl.ds(t, count, stride=steps), :] = (
            spread[:count] + spread[count : 2 * count] + spread[2 * count :]
        )


def prep(me, meta, shard, cands):
    count = meta.shape[0]
    wide = 128
    return pl.pallas_call(
        functools.partial(prep_kernel, shard=shard, cands=cands),
        in_specs=[
            pl.BlockSpec(memory_space=pltpu.SMEM),
            pl.BlockSpec(memory_space=pltpu.VMEM),
        ],
        out_specs=[pl.BlockSpec(memory_space=pltpu.VMEM)] * 2,
        out_shape=[
            jax.ShapeDtypeStruct((count, wide), jnp.int32),
            jax.ShapeDtypeStruct((count * (cands // GROUP), wide), jnp.float32),
        ],
        scratch_shapes=[
            pltpu.VMEM((count * 8, wide), jnp.float32),
            pltpu.VMEM((count, wide), jnp.float32),
            pltpu.VMEM((count * 8, wide), jnp.float32),
        ],
        compiler_params=pltpu.CompilerParams(vmem_limit_bytes=VMEM_LIMIT),
        cost_estimate=pl.CostEstimate(flops=count * wide, bytes_accessed=count * wide, transcendentals=0),
        name="prep",
    )(me, meta)


def pair_kernel(source_ref, rows_ref, target_ref, queries_ref, inverse_ref, index_ref, turned_ref, *refs, cands, sources):
    out_refs = refs[:sources]
    (units_ref, unit_ref, acc_ref, total_ref, left_ref, right_ref, back_ref, raw_ref) = refs[sources:]
    count, tokens, dim = unit_ref.shape
    wide = rows_ref.shape[1]
    per_query = cands // GROUP
    slots = count * per_query
    bits = per_query.bit_length() - 1
    total = jnp.int32(0)
    for q in range(count):
        for t in range(per_query):
            units_ref[total + t] = jnp.int32(q * per_query + t)
        total = total + lax.div(rows_ref[q, cands] + (GROUP - 1), GROUP)
    for t in range(2 * UNITS):
        units_ref[total + t] = jnp.int32(slots)
    steps = lax.div(total + (UNITS - 1), UNITS)

    def entry(number):
        slot = units_ref[number]
        q = jnp.minimum(lax.shift_right_logical(slot, bits), count - 1)
        return slot, q, jnp.bitwise_and(slot, per_query - 1) * GROUP

    for q in range(count):
        unit_ref[q] = rounded_queries(queries_ref[0, q])
    acc_ref[...] = jnp.zeros_like(acc_ref)
    ones = jnp.ones((8, wide), jnp.bfloat16)

    def tiles_of(number, ref):
        _, q, base = entry(number)
        return q, [ref[rows_ref[q, base + g]] for g in range(GROUP)]

    def multiply(step):
        found = []
        for u in range(UNITS):
            q, tiles = tiles_of(step * UNITS + u, turned_ref)
            found.append(dot(unit_ref[q], jnp.concatenate(tiles, axis=1)))
        return found

    def forward(step, carry):
        expos, weights, rows = [], [], []
        for u in range(UNITS):
            _, q, base = entry(step * UNITS + u)
            for g in range(GROUP):
                rows.append(rows_ref[q, base + g])
                inverse = inverse_ref[pl.ds(rows[-1], 1), :]
                raw = raw_ref[u, :, g * wide : (g + 1) * wide]
                expo = jnp.exp2(raw * (inverse * (LOG2E / inner_temp)))
                expos.append(expo.astype(jnp.bfloat16))
                weights.append((expo * inverse).astype(jnp.bfloat16))
        following = multiply(step + 1)
        backs = []
        for u in range(UNITS):
            for k in range(u * GROUP, (u + 1) * GROUP, 2):
                part = dot(
                    jnp.concatenate(weights[k : k + 2], axis=0),
                    jnp.concatenate([index_ref[row] for row in rows[k : k + 2]], axis=1),
                )
                backs += [part[:tokens, :dim], part[tokens:, dim:]]
        totals = []
        for u in range(0, UNITS, 2):
            part = dot_last(ones, jnp.concatenate(expos[u * GROUP : (u + 2) * GROUP], axis=0))
            totals += [part[0:1, :wide], part[0:1, wide:]]
        for u in range(UNITS):
            back_ref[step * UNITS + u] = jnp.concatenate(
                backs[u * GROUP : (u + 1) * GROUP], axis=0
            ).astype(jnp.bfloat16)
            total_ref[pl.ds(units_ref[step * UNITS + u], 1), :] = totals[u]
        for u in range(UNITS):
            raw_ref[u] = following[u]
        return carry

    for u, raw in enumerate(multiply(0)):
        raw_ref[u] = raw
    lax.fori_loop(0, steps, forward, 0)

    target = target_ref[...]
    held = target >= 0.0
    totals = jnp.where(held, total_ref[0:slots, :], 1.0)
    target = jnp.where(held, target, 0.0)
    same = lax.broadcasted_iota(jnp.int32, (wide, wide), 0) // tokens == lax.broadcasted_iota(
        jnp.int32, (wide, wide), 1
    ) // tokens
    same = jnp.where(same, 1.0, 0.0).astype(jnp.bfloat16)
    parts = [dot(part, same) for part in split3(jnp.log(totals))]
    score = inner_temp * (parts[0] + parts[1] + parts[2])
    lift = jnp.where(held, jnp.exp(score), 0.0)
    recip = 1.0 / totals
    left_ref[0:slots, :] = lift * recip
    right_ref[0:slots, :] = target * recip
    left_ref[slots:, :] = jnp.zeros_like(left_ref[slots:, :])
    right_ref[slots:, :] = jnp.zeros_like(right_ref[slots:, :])

    def per_source(values):
        rows = jnp.sum(values.reshape(count, per_query, wide), axis=1)
        return jnp.sum(rows, axis=-1, keepdims=True) * (1.0 / tokens)

    lane = lax.broadcasted_iota(jnp.int32, (count, wide), 1)
    sums = jnp.where(lane < wide // 2, per_source(lift), per_source(target * score))
    diagonal = lax.broadcasted_iota(jnp.int32, (tokens, wide), 0) == lax.broadcasted_iota(
        jnp.int32, (tokens, wide), 1
    ) % tokens

    def backward(step, carry):
        owners, sides = [], []
        for u in range(UNITS):
            slot, q, _ = entry(step * UNITS + u)
            left = jnp.where(diagonal, left_ref[pl.ds(slot, 1), :], 0.0)
            right = jnp.where(diagonal, right_ref[pl.ds(slot, 1), :], 0.0)
            both = jnp.concatenate([left, right], axis=0)
            high = both.astype(jnp.bfloat16)
            sides += [high, (both - high.astype(jnp.float32)).astype(jnp.bfloat16)]
            owners.append(q)
        parts = []
        for u in range(0, UNITS, 2):
            pulled = dot(
                jnp.concatenate(sides[2 * u : 2 * u + 4], axis=0),
                jnp.concatenate([back_ref[step * UNITS + u], back_ref[step * UNITS + u + 1]], axis=1),
            )
            height = 2 * tokens
            parts += [
                pulled[:height, :dim] + pulled[height : 2 * height, :dim],
                pulled[2 * height : 3 * height, dim:] + pulled[3 * height :, dim:],
            ]
        for q, part in zip(owners, parts):
            acc_ref[q] += part
        return carry

    lax.fori_loop(0, steps, backward, 0)
    for k, out_ref in enumerate(out_refs):
        @pl.when(pl.program_id(0) == k)
        def _():
            for q in range(count):
                out_ref[pl.ds(q * 2 * tokens, 2 * tokens), :] = acc_ref[q].astype(jnp.bfloat16)
            for j, part in enumerate(split3(sums)):
                out_ref[pl.ds(count * 2 * tokens + j * count, count), :] = part


def pairs(sources, rows, targets, queries, inverse, index, turned, cands, room):
    count, tokens, dim = queries.shape[1:]
    wide = rows.shape[1]
    per_query = cands // GROUP
    slots = count * per_query
    most = (room + (GROUP - 1) * count) // GROUP + UNITS
    height = count * 2 * tokens + 3 * count
    return pl.pallas_call(
        functools.partial(pair_kernel, cands=cands, sources=len(sources)),
        grid_spec=pltpu.PrefetchScalarGridSpec(
            num_scalar_prefetch=1,
            grid=(len(sources),),
            in_specs=[
                pl.BlockSpec((count, wide), lambda i, s: (s[i], 0), memory_space=pltpu.SMEM),
                pl.BlockSpec((slots, wide), lambda i, s: (s[i], 0)),
                pl.BlockSpec((1, count, tokens, dim), lambda i, s: (s[i], 0, 0, 0)),
                pl.BlockSpec(memory_space=pltpu.VMEM),
                pl.BlockSpec(memory_space=pltpu.VMEM),
                pl.BlockSpec(memory_space=pltpu.VMEM),
            ],
            out_specs=[pl.BlockSpec((height, dim), lambda i, s: (0, 0))] * len(sources),
            scratch_shapes=[
                pltpu.SMEM((slots + per_query + 2 * UNITS,), jnp.int32),
                pltpu.VMEM((count, tokens, dim), jnp.bfloat16),
                pltpu.VMEM((count, 2 * tokens, dim), jnp.float32),
                pltpu.VMEM((slots + 8, wide), jnp.float32),
                pltpu.VMEM((slots + 8, wide), jnp.float32),
                pltpu.VMEM((slots + 8, wide), jnp.float32),
                pltpu.VMEM((most, GROUP * tokens, dim), jnp.bfloat16),
                pltpu.VMEM((UNITS, tokens, GROUP * wide), jnp.float32),
            ],
        ),
        out_shape=[jax.ShapeDtypeStruct((height, dim), jnp.bfloat16)] * len(sources),
        compiler_params=pltpu.CompilerParams(vmem_limit_bytes=VMEM_LIMIT),
        cost_estimate=pl.CostEstimate(
            flops=6 * len(sources) * room * tokens * wide * dim,
            bytes_accessed=2 * len(sources) * room * wide * dim,
            transcendentals=len(sources) * room * tokens * wide,
        ),
        name="pairs",
    )(jnp.stack(sources), rows, targets, queries, inverse, index, turned)


def neg_kernel(rows_ref, queries_ref, shard_ref, index_ref, turned_ref, inverse_ref, acc_ref, sums_ref,
               sems, unit_ref, expo_ref, total_ref, left_ref, back_ref, raw_ref, *, tokens):
    total = rows_ref.shape[0]
    chunk = expo_ref.shape[0]
    height, dim = queries_ref.shape
    wide = index_ref.shape[1]
    lanes = 128
    half = min(height, 256)
    for c in range(height // lanes):
        part = slice(c * lanes, (c + 1) * lanes)
        unit_ref[:, part] = rounded_queries(queries_ref[part]).T
    load_shard(shard_ref, index_ref, turned_ref, inverse_ref, sems)
    back_ref[...] = jnp.zeros_like(back_ref)
    sums_ref[...] = jnp.zeros_like(sums_ref)
    same = lax.broadcasted_iota(jnp.int32, (lanes, lanes), 0) // tokens == lax.broadcasted_iota(
        jnp.int32, (lanes, lanes), 1
    ) // tokens
    same = jnp.where(same, 1.0, 0.0).astype(jnp.bfloat16)

    def block(number, carry):
        def tiles_of(step):
            first = number * chunk + jnp.minimum(step, chunk // NEG_STEP - 1) * NEG_STEP
            return jnp.concatenate([index_ref[rows_ref[first + g]] for g in range(NEG_STEP)], axis=0)

        def forward(step, carry):
            first = step * NEG_STEP
            broad = tiles_of(step).astype(jnp.float32)
            inverse = lax.rsqrt(jnp.sum(broad * broad, axis=-1, keepdims=True) + epsilon)
            expo = jnp.exp2(raw_ref[...] * (inverse * (LOG2E / inner_temp)))
            following = dot(tiles_of(step + 1), unit_ref[...])
            for g in range(NEG_STEP):
                part = slice(g * wide, (g + 1) * wide)
                expo_ref[first + g] = (expo[part] * inverse[part]).astype(jnp.bfloat16)
                total_ref[pl.ds(first + g, 1), :] = jnp.sum(expo[part], axis=0, keepdims=True)
            raw_ref[...] = following
            return carry

        raw_ref[...] = dot(tiles_of(0), unit_ref[...])
        lax.fori_loop(0, chunk // NEG_STEP, forward, 0)
        for c in range(height // lanes):
            part = slice(c * lanes, (c + 1) * lanes)
            totals = total_ref[:, part]
            pieces = [dot(piece, same) for piece in split3(jnp.log(totals))]
            lift = jnp.exp(inner_temp * (pieces[0] + pieces[1] + pieces[2]))
            left_ref[:, part] = lift / totals
            sums_ref[:, part] += jnp.broadcast_to(jnp.sum(lift, axis=0, keepdims=True), (8, lanes))
        for c in range(height // half):
            part = slice(c * half, (c + 1) * half)

            def backward(step, acc):
                for g in range(NEG_STEP):
                    k = step * NEG_STEP + g
                    tile = turned_ref[rows_ref[number * chunk + k]]
                    acc = acc + dot(tile, expo_ref[k, :, part]) * left_ref[pl.ds(k, 1), part]
                return acc

            back_ref[:, part] = lax.fori_loop(0, chunk // NEG_STEP, backward, back_ref[:, part])
        return carry

    lax.fori_loop(0, total // chunk, block, 0)
    for c in range(height // lanes):
        part = slice(c * lanes, (c + 1) * lanes)
        acc_ref[part, :] = back_ref[:, part].T


def negatives(rows, queries, index):
    total = rows.shape[0]
    count, tokens, dim = queries.shape
    wide = index.shape[1]
    height = count * tokens
    chunk = math.gcd(total, NEG_CHUNK)
    return pl.pallas_call(
        functools.partial(neg_kernel, tokens=tokens),
        in_specs=[
            pl.BlockSpec(memory_space=pltpu.SMEM),
            pl.BlockSpec(memory_space=pltpu.VMEM),
            pl.BlockSpec(memory_space=pltpu.HBM),
        ],
        out_specs=[pl.BlockSpec(memory_space=pltpu.VMEM)] * 5,
        out_shape=[
            pltpu.VMEM(index.shape, jnp.bfloat16),
            pltpu.VMEM((index.shape[0], dim, wide), jnp.bfloat16),
            pltpu.VMEM((index.shape[0], wide), jnp.float32),
            jax.ShapeDtypeStruct((height, dim), jnp.float32),
            jax.ShapeDtypeStruct((8, height), jnp.float32),
        ],
        scratch_shapes=[
            pltpu.SemaphoreType.DMA((LOADS,)),
            pltpu.VMEM((dim, height), jnp.bfloat16),
            pltpu.VMEM((chunk, wide, height), jnp.bfloat16),
            pltpu.VMEM((chunk, height), jnp.float32),
            pltpu.VMEM((chunk, height), jnp.float32),
            pltpu.VMEM((dim, height), jnp.float32),
            pltpu.VMEM((NEG_STEP * wide, height), jnp.float32),
        ],
        compiler_params=pltpu.CompilerParams(vmem_limit_bytes=VMEM_LIMIT),
        cost_estimate=pl.CostEstimate(
            flops=4 * total * height * wide * dim,
            bytes_accessed=2 * total * wide * dim,
            transcendentals=total * height * wide,
        ),
        name="negatives",
    )(rows, queries.reshape(height, dim), pltpu.with_memory_space_constraint(index, pltpu.HBM))


def finish_kernel(queries_ref, teacher_ref, back_ref, sums_ref, *refs, owners):
    messages, (loss_ref, grad_ref) = refs[:owners], refs[owners:]
    count, tokens, dim = grad_ref.shape
    cut = count * 2 * tokens
    scores = jnp.zeros((count, dim), jnp.float32)
    for message in messages:
        for k in range(3):
            scores = scores + message[cut + k * count : cut + (k + 1) * count, :].astype(jnp.float32)
    totals = []
    for q in range(count):
        total = scores[q : q + 1, 0:1] + sums_ref[0:1, q * tokens : q * tokens + 1]
        totals.append(total)
        pulled = back_ref[q * tokens : (q + 1) * tokens, :]
        right = jnp.zeros((tokens, dim), jnp.float32)
        for message in messages:
            pulled = pulled + message[q * 2 * tokens : (q * 2 + 1) * tokens, :].astype(jnp.float32)
            right = right + message[(q * 2 + 1) * tokens : (q + 1) * 2 * tokens, :].astype(jnp.float32)
        pulled = pulled / total - right
        wide = queries_ref[q].astype(jnp.float32)
        radius = jnp.sqrt(jnp.sum(wide * wide, axis=-1, keepdims=True) + epsilon)
        unit = wide / radius
        grad_ref[q] = (pulled - unit * jnp.sum(unit * pulled, axis=-1, keepdims=True)) / radius
    spread = jnp.log(jnp.concatenate(totals, axis=0))
    teacher = teacher_ref[...]
    log_target = teacher - jnp.log(jnp.sum(jnp.exp(teacher), axis=-1, keepdims=True))
    gain = jnp.sum(jnp.exp(log_target) * (log_target + spread), axis=-1, keepdims=True)
    loss_ref[...] = gain - scores[:, dim // 2 : dim // 2 + 1] + jnp.zeros_like(loss_ref)


def finish(queries, teacher, back, sums, messages):
    count, tokens, dim = queries.shape
    owners = len(messages)
    return pl.pallas_call(
        functools.partial(finish_kernel, owners=owners),
        in_specs=[pl.BlockSpec(memory_space=pltpu.VMEM)] * (4 + owners),
        out_specs=[pl.BlockSpec(memory_space=pltpu.VMEM)] * 2,
        out_shape=[
            jax.ShapeDtypeStruct((count, dim), jnp.float32),
            jax.ShapeDtypeStruct((count, tokens, dim), jnp.float32),
        ],
        compiler_params=pltpu.CompilerParams(vmem_limit_bytes=VMEM_LIMIT),
        name="finish",
    )(queries, teacher, back, sums, *messages)


def on_device(queries, index, cand_owner, cand_row, neg_row, teacher):
    count, tokens, dim = queries.shape
    cands = cand_row.shape[1]
    shard = index.shape[0]
    owners = lax.axis_size("corpus")
    room = (2 * count * cands + owners - 1) // owners
    me = lax.axis_index("corpus").astype(jnp.int32)
    group = lax.axis_size("blk")

    def from_step(value, axis, size, step):
        return lax.ppermute(value, axis, [((i + step) % size, i) for i in range(size)])

    def gathered(value, axis, size):
        return [value] + [from_step(value, axis, size, step) for step in range(1, size)]

    code = (cand_owner[..., 0] * shard + cand_row).astype(jnp.float32)
    meta = jnp.concatenate([code, teacher], axis=1)
    all_neg = jnp.concatenate(gathered(neg_row, "blk", group), axis=0).reshape(-1)
    def told(value):
        copies = jnp.broadcast_to(value[None], (owners,) + value.shape)
        return lax.all_to_all(copies, "corpus", split_axis=0, concat_axis=0, tiled=True)

    all_meta = told(meta).reshape(owners * count, -1)
    all_queries = told(queries)
    rows, targets = prep(me.reshape(1), all_meta, shard, cands)
    rows, all_neg = lax.optimization_barrier((rows, all_neg))
    index, turned, inverse, neg_acc, neg_sum = negatives(all_neg, queries, index)
    messages = []
    order = list(range(1, owners)) + [0]
    groups = [order[first : first + SOURCES] for first in range(0, owners, SOURCES)]
    for steps in groups:
        sources = [lax.rem(me + step, owners) for step in steps]
        found = pairs(
            sources, rows, targets, all_queries, inverse, index, turned, cands, room
        )
        for step, message in zip(steps, found):
            if step:
                message = lax.ppermute(
                    message, "corpus", [(i, (i + step) % owners) for i in range(owners)]
                )
            messages.append(message)
    losses, query_grads = finish(queries, teacher, neg_acc, neg_sum, messages)
    return (losses[:, 0], query_grads)


def solution(mesh):
    placed = (
        P(("corpus", "blk"), None, None),
        P("corpus", None, None),
        P(("corpus", "blk"), None, None),
        P(("corpus", "blk"), None),
        P(("corpus", "blk"), None),
        P(("corpus", "blk"), None),
    )
    return jax.shard_map(
        on_device,
        mesh=mesh,
        in_specs=placed,
        out_specs=(P(("corpus", "blk")), P(("corpus", "blk"), None, None)),
        check_vma=False,
    )
```

```python
import functools
import math

import jax
import jax.numpy as jnp
from jax import lax
from jax.experimental import pallas as pl
from jax.experimental.pallas import tpu as pltpu
from jax.sharding import PartitionSpec as P

inner_temp = 0.1
epsilon = 1e-06
LOG2E = 1.4426950408889634
GROUP = 4
UNITS = 24
LOADS = 8
LOAD_STEP = 16
NEG_STEP = 8
NEG_CHUNK = 24
SOURCES = 2
VMEM_LIMIT = 14 * 1024 * 1024
LAST = (((1,), (1,)), ((), ()))


def dot_last(a, b):
    return lax.dot_general(a, b, LAST, preferred_element_type=jnp.float32)


def dot(a, b):
    return jnp.dot(a, b, preferred_element_type=jnp.float32)


def split3(x):
    high = x.astype(jnp.bfloat16)
    rest = x - high.astype(jnp.float32)
    mid = rest.astype(jnp.bfloat16)
    low = (rest - mid.astype(jnp.float32)).astype(jnp.bfloat16)
    return high, mid, low


def rounded_queries(raw):
    wide = raw.astype(jnp.float32)
    radius = jnp.sqrt(jnp.sum(wide * wide, axis=-1, keepdims=True) + epsilon)
    return (wide / radius).astype(jnp.bfloat16)


def load_shard(index_ref, tiles_ref, turned_ref, inverse_ref, sems):
    count = index_ref.shape[0]
    chunk = count // LOADS

    def copy(part):
        at = pl.ds(part * chunk, chunk)
        return pltpu.make_async_copy(index_ref.at[at], tiles_ref.at[at], sems.at[part])

    for part in range(LOADS):
        copy(part).start()

    for part in range(LOADS):
        copy(part).wait()

        def body(step, carry):
            first = part * chunk + step * LOAD_STEP
            squares = []
            turned = []
            for k in range(LOAD_STEP):
                tile = tiles_ref[first + k].T
                turned.append(tile)
                wide = tile.astype(jnp.float32)
                squares.append(jnp.sum(wide * wide, axis=0, keepdims=True))
            for k in range(LOAD_STEP):
                turned_ref[first + k] = turned[k]
            at = pl.ds(pl.multiple_of(first, LOAD_STEP), LOAD_STEP)
            inverse_ref[at, :] = lax.rsqrt(jnp.concatenate(squares, axis=0) + epsilon)
            return carry

        lax.fori_loop(0, chunk // LOAD_STEP, body, 0)


def load(index):
    count, tokens, dim = index.shape
    return pl.pallas_call(
        load_shard,
        in_specs=[pl.BlockSpec(memory_space=pltpu.HBM)],
        out_specs=[pl.BlockSpec(memory_space=pltpu.VMEM)] * 3,
        out_shape=[
            pltpu.VMEM((count, tokens, dim), jnp.bfloat16),
            pltpu.VMEM((count, dim, tokens), jnp.bfloat16),
            pltpu.VMEM((count, tokens), jnp.float32),
        ],
        scratch_shapes=[pltpu.SemaphoreType.DMA((LOADS,))],
        compiler_params=pltpu.CompilerParams(vmem_limit_bytes=VMEM_LIMIT),
        cost_estimate=pl.CostEstimate(
            flops=2 * count * tokens * dim,
            bytes_accessed=2 * count * tokens * dim,
            transcendentals=count * tokens,
        ),
        name="load",
    )(pltpu.with_memory_space_constraint(index, pltpu.HBM))


def prep_kernel(me_ref, meta_ref, rows_ref, target_ref, value_ref, place_ref, result_ref, *, shard, cands):
    count = meta_ref.shape[0]
    code = meta_ref[:, :cands]
    owner = jnp.floor((code + 0.5) * (1.0 / shard))
    row = code - owner * shard
    teacher = meta_ref[:, cands:]
    log_target = teacher - jnp.log(jnp.sum(jnp.exp(teacher), axis=-1, keepdims=True))
    target = jnp.exp(log_target)
    mine = (owner == me_ref[0].astype(jnp.float32)).astype(jnp.float32)
    before = lax.broadcasted_iota(jnp.int32, (cands, cands), 0) < lax.broadcasted_iota(
        jnp.int32, (cands, cands), 1
    )
    place = dot(mine.astype(jnp.bfloat16), before.astype(jnp.float32).astype(jnp.bfloat16))
    wide = value_ref.shape[1]
    pad = jnp.zeros((count, wide - cands), jnp.float32)
    place_ref[...] = jnp.concatenate([jnp.where(mine > 0, place, -1.0), pad - 1.0], axis=1)
    row_high = jnp.floor(row * (1.0 / 16))
    first, second, third = split3(target)
    values = [row_high, row - 16 * row_high, first, second, third]
    for v in range(8):
        value = values[v].astype(jnp.float32) if v < len(values) else jnp.zeros_like(row)
        value_ref[pl.ds(v, count, stride=8), :] = jnp.concatenate([value, pad], axis=1)
    spots = lax.broadcasted_iota(jnp.int32, (wide, wide), 0).astype(jnp.float32)

    def body(step, carry):
        for k in range(8):
            q = step * 8 + k
            hot = jnp.where(place_ref[pl.ds(q, 1), :] == spots, 1.0, 0.0).astype(jnp.bfloat16)
            at = pl.ds(pl.multiple_of(q * 8, 8), 8)
            result_ref[at, :] = dot_last(value_ref[at, :].astype(jnp.bfloat16), hot)
        return carry

    lax.fori_loop(0, count // 8, body, 0)
    result = [result_ref[pl.ds(v, count, stride=8), :] for v in range(5)]
    found = jnp.sum(mine, axis=-1, keepdims=True)
    lane = lax.broadcasted_iota(jnp.int32, (count, wide), 1)
    rows = 16 * result[0] + result[1]
    rows_ref[...] = jnp.where(lane < cands, rows, found).astype(jnp.int32)
    listed = jnp.where(lane.astype(jnp.float32) < found, result[2] + result[3] + result[4], -1.0)
    stacked = jnp.concatenate(split3(listed), axis=0)
    steps = cands // GROUP
    source = lax.broadcasted_iota(jnp.int32, (wide, wide), 0)
    block = lax.broadcasted_iota(jnp.int32, (wide, wide), 1) // (wide // GROUP)
    for t in range(steps):
        pick = jnp.where(source == block + t * GROUP, 1.0, 0.0).astype(jnp.bfloat16)
        spread = dot(stacked, pick)
        target_ref[pl.ds(t, count, stride=steps), :] = (
            spread[:count] + spread[count : 2 * count] + spread[2 * count :]
        )


def prep(me, meta, shard, cands):
    count = meta.shape[0]
    wide = 128
    return pl.pallas_call(
        functools.partial(prep_kernel, shard=shard, cands=cands),
        in_specs=[
            pl.BlockSpec(memory_space=pltpu.SMEM),
            pl.BlockSpec(memory_space=pltpu.VMEM),
        ],
        out_specs=[pl.BlockSpec(memory_space=pltpu.VMEM)] * 2,
        out_shape=[
            jax.ShapeDtypeStruct((count, wide), jnp.int32),
            jax.ShapeDtypeStruct((count * (cands // GROUP), wide), jnp.float32),
        ],
        scratch_shapes=[
            pltpu.VMEM((count * 8, wide), jnp.float32),
            pltpu.VMEM((count, wide), jnp.float32),
            pltpu.VMEM((count * 8, wide), jnp.float32),
        ],
        compiler_params=pltpu.CompilerParams(vmem_limit_bytes=VMEM_LIMIT),
        cost_estimate=pl.CostEstimate(flops=count * wide, bytes_accessed=count * wide, transcendentals=0),
        name="prep",
    )(me, meta)


def pair_kernel(source_ref, rows_ref, target_ref, queries_ref, inverse_ref, index_ref, turned_ref, *refs, cands, sources):
    out_refs = refs[:sources]
    (units_ref, unit_ref, acc_ref, total_ref, left_ref, right_ref, back_ref, raw_ref) = refs[sources:]
    count, tokens, dim = unit_ref.shape
    wide = rows_ref.shape[1]
    per_query = cands // GROUP
    slots = count * per_query
    bits = per_query.bit_length() - 1
    total = jnp.int32(0)
    for q in range(count):
        for t in range(per_query):
            units_ref[total + t] = jnp.int32(q * per_query + t)
        total = total + lax.div(rows_ref[q, cands] + (GROUP - 1), GROUP)
    for t in range(2 * UNITS):
        units_ref[total + t] = jnp.int32(slots)
    steps = lax.div(total + (UNITS - 1), UNITS)

    def entry(number):
        slot = units_ref[number]
        q = jnp.minimum(lax.shift_right_logical(slot, bits), count - 1)
        return slot, q, jnp.bitwise_and(slot, per_query - 1) * GROUP

    for q in range(count):
        unit_ref[q] = rounded_queries(queries_ref[0, q])
    acc_ref[...] = jnp.zeros_like(acc_ref)
    ones = jnp.ones((8, wide), jnp.bfloat16)

    def tiles_of(number, ref):
        _, q, base = entry(number)
        return q, [ref[rows_ref[q, base + g]] for g in range(GROUP)]

    def multiply(step):
        found = []
        for u in range(UNITS):
            q, tiles = tiles_of(step * UNITS + u, turned_ref)
            found.append(dot(unit_ref[q], jnp.concatenate(tiles, axis=1)))
        return found

    def forward(step, carry):
        expos, weights, rows = [], [], []
        for u in range(UNITS):
            _, q, base = entry(step * UNITS + u)
            for g in range(GROUP):
                rows.append(rows_ref[q, base + g])
                inverse = inverse_ref[pl.ds(rows[-1], 1), :]
                raw = raw_ref[u, :, g * wide : (g + 1) * wide]
                expo = jnp.exp2(raw * (inverse * (LOG2E / inner_temp)))
                expos.append(expo.astype(jnp.bfloat16))
                weights.append((expo * inverse).astype(jnp.bfloat16))
        following = multiply(step + 1)
        backs = []
        for u in range(UNITS):
            for k in range(u * GROUP, (u + 1) * GROUP, 2):
                part = dot(
                    jnp.concatenate(weights[k : k + 2], axis=0),
                    jnp.concatenate([index_ref[row] for row in rows[k : k + 2]], axis=1),
                )
                backs += [part[:tokens, :dim], part[tokens:, dim:]]
        totals = []
        for u in range(0, UNITS, 2):
            part = dot_last(ones, jnp.concatenate(expos[u * GROUP : (u + 2) * GROUP], axis=0))
            totals += [part[0:1, :wide], part[0:1, wide:]]
        for u in range(UNITS):
            back_ref[step * UNITS + u] = jnp.concatenate(
                backs[u * GROUP : (u + 1) * GROUP], axis=0
            ).astype(jnp.bfloat16)
            total_ref[pl.ds(units_ref[step * UNITS + u], 1), :] = totals[u]
        for u in range(UNITS):
            raw_ref[u] = following[u]
        return carry

    for u, raw in enumerate(multiply(0)):
        raw_ref[u] = raw
    lax.fori_loop(0, steps, forward, 0)

    target = target_ref[...]
    held = target >= 0.0
    totals = jnp.where(held, total_ref[0:slots, :], 1.0)
    target = jnp.where(held, target, 0.0)
    same = lax.broadcasted_iota(jnp.int32, (wide, wide), 0) // tokens == lax.broadcasted_iota(
        jnp.int32, (wide, wide), 1
    ) // tokens
    same = jnp.where(same, 1.0, 0.0).astype(jnp.bfloat16)
    parts = [dot(part, same) for part in split3(jnp.log(totals))]
    score = inner_temp * (parts[0] + parts[1] + parts[2])
    lift = jnp.where(held, jnp.exp(score), 0.0)
    recip = 1.0 / totals
    left_ref[0:slots, :] = lift * recip
    right_ref[0:slots, :] = target * recip
    left_ref[slots:, :] = jnp.zeros_like(left_ref[slots:, :])
    right_ref[slots:, :] = jnp.zeros_like(right_ref[slots:, :])

    def per_source(values):
        rows = jnp.sum(values.reshape(count, per_query, wide), axis=1)
        return jnp.sum(rows, axis=-1, keepdims=True) * (1.0 / tokens)

    lane = lax.broadcasted_iota(jnp.int32, (count, wide), 1)
    sums = jnp.where(lane < wide // 2, per_source(lift), per_source(target * score))
    diagonal = lax.broadcasted_iota(jnp.int32, (tokens, wide), 0) == lax.broadcasted_iota(
        jnp.int32, (tokens, wide), 1
    ) % tokens

    def backward(step, carry):
        owners, sides = [], []
        for u in range(UNITS):
            slot, q, _ = entry(step * UNITS + u)
            left = jnp.where(diagonal, left_ref[pl.ds(slot, 1), :], 0.0)
            right = jnp.where(diagonal, right_ref[pl.ds(slot, 1), :], 0.0)
            both = jnp.concatenate([left, right], axis=0)
            high = both.astype(jnp.bfloat16)
            sides += [high, (both - high.astype(jnp.float32)).astype(jnp.bfloat16)]
            owners.append(q)
        parts = []
        for u in range(0, UNITS, 2):
            pulled = dot(
                jnp.concatenate(sides[2 * u : 2 * u + 4], axis=0),
                jnp.concatenate([back_ref[step * UNITS + u], back_ref[step * UNITS + u + 1]], axis=1),
            )
            height = 2 * tokens
            parts += [
                pulled[:height, :dim] + pulled[height : 2 * height, :dim],
                pulled[2 * height : 3 * height, dim:] + pulled[3 * height :, dim:],
            ]
        for q, part in zip(owners, parts):
            acc_ref[q] += part
        return carry

    lax.fori_loop(0, steps, backward, 0)
    for k, out_ref in enumerate(out_refs):
        @pl.when(pl.program_id(0) == k)
        def _():
            for q in range(count):
                out_ref[pl.ds(q * 2 * tokens, 2 * tokens), :] = acc_ref[q].astype(jnp.bfloat16)
            for j, part in enumerate(split3(sums)):
                out_ref[pl.ds(count * 2 * tokens + j * count, count), :] = part


def pairs(sources, rows, targets, queries, inverse, index, turned, cands, room):
    count, tokens, dim = queries.shape[1:]
    wide = rows.shape[1]
    per_query = cands // GROUP
    slots = count * per_query
    most = (room + (GROUP - 1) * count) // GROUP + UNITS
    height = count * 2 * tokens + 3 * count
    return pl.pallas_call(
        functools.partial(pair_kernel, cands=cands, sources=len(sources)),
        grid_spec=pltpu.PrefetchScalarGridSpec(
            num_scalar_prefetch=1,
            grid=(len(sources),),
            in_specs=[
                pl.BlockSpec((count, wide), lambda i, s: (s[i], 0), memory_space=pltpu.SMEM),
                pl.BlockSpec((slots, wide), lambda i, s: (s[i], 0)),
                pl.BlockSpec((1, count, tokens, dim), lambda i, s: (s[i], 0, 0, 0)),
                pl.BlockSpec(memory_space=pltpu.VMEM),
                pl.BlockSpec(memory_space=pltpu.VMEM),
                pl.BlockSpec(memory_space=pltpu.VMEM),
            ],
            out_specs=[pl.BlockSpec((height, dim), lambda i, s: (0, 0))] * len(sources),
            scratch_shapes=[
                pltpu.SMEM((slots + per_query + 2 * UNITS,), jnp.int32),
                pltpu.VMEM((count, tokens, dim), jnp.bfloat16),
                pltpu.VMEM((count, 2 * tokens, dim), jnp.float32),
                pltpu.VMEM((slots + 8, wide), jnp.float32),
                pltpu.VMEM((slots + 8, wide), jnp.float32),
                pltpu.VMEM((slots + 8, wide), jnp.float32),
                pltpu.VMEM((most, GROUP * tokens, dim), jnp.bfloat16),
                pltpu.VMEM((UNITS, tokens, GROUP * wide), jnp.float32),
            ],
        ),
        out_shape=[jax.ShapeDtypeStruct((height, dim), jnp.bfloat16)] * len(sources),
        compiler_params=pltpu.CompilerParams(vmem_limit_bytes=VMEM_LIMIT),
        cost_estimate=pl.CostEstimate(
            flops=6 * len(sources) * room * tokens * wide * dim,
            bytes_accessed=2 * len(sources) * room * wide * dim,
            transcendentals=len(sources) * room * tokens * wide,
        ),
        name="pairs",
    )(jnp.stack(sources), rows, targets, queries, inverse, index, turned)


def neg_kernel(rows_ref, queries_ref, shard_ref, acc_ref, sums_ref,
               unit_ref, expo_ref, total_ref, left_ref, back_ref, raw_ref, tiles_ref, turned_ref, sems,
               *, tokens):
    total = rows_ref.shape[0]
    chunk = expo_ref.shape[0]
    height, dim = queries_ref.shape
    wide = shard_ref.shape[1]
    lanes = 128
    half = min(height, 256)
    def fetch(number):
        place = jnp.bitwise_and(number, 1)
        for k in range(chunk):
            pltpu.make_async_copy(
                shard_ref.at[rows_ref[number * chunk + k]], tiles_ref.at[place, k], sems.at[place]
            ).start()

    fetch(jnp.int32(0))
    for c in range(height // lanes):
        part = slice(c * lanes, (c + 1) * lanes)
        unit_ref[:, part] = rounded_queries(queries_ref[part]).T
    back_ref[...] = jnp.zeros_like(back_ref)
    sums_ref[...] = jnp.zeros_like(sums_ref)

    same = lax.broadcasted_iota(jnp.int32, (lanes, lanes), 0) // tokens == lax.broadcasted_iota(
        jnp.int32, (lanes, lanes), 1
    ) // tokens
    same = jnp.where(same, 1.0, 0.0).astype(jnp.bfloat16)

    def block(number, carry):
        @pl.when(number + 1 < total // chunk)
        def _():
            fetch(number + 1)

        place = jnp.bitwise_and(number, 1)
        pltpu.make_async_copy(shard_ref.at[pl.ds(0, chunk)], tiles_ref.at[place], sems.at[place]).wait()

        def tiles_of(step):
            first = jnp.minimum(step, chunk // NEG_STEP - 1) * NEG_STEP
            return tiles_ref[place, pl.ds(first, NEG_STEP)].reshape(NEG_STEP * wide, dim)

        def forward(step, carry):
            first = step * NEG_STEP
            tiles = tiles_of(step)
            broad = tiles.astype(jnp.float32)
            inverse = lax.rsqrt(jnp.sum(broad * broad, axis=-1, keepdims=True) + epsilon)
            expo = jnp.exp2(raw_ref[...] * (inverse * (LOG2E / inner_temp)))
            following = dot(tiles_of(step + 1), unit_ref[...])
            for g in range(NEG_STEP):
                part = slice(g * wide, (g + 1) * wide)
                turned_ref[first + g] = tiles[part].T
                expo_ref[first + g] = (expo[part] * inverse[part]).astype(jnp.bfloat16)
                total_ref[pl.ds(first + g, 1), :] = jnp.sum(expo[part], axis=0, keepdims=True)
            raw_ref[...] = following
            return carry

        raw_ref[...] = dot(tiles_of(0), unit_ref[...])
        lax.fori_loop(0, chunk // NEG_STEP, forward, 0)
        for c in range(height // lanes):
            part = slice(c * lanes, (c + 1) * lanes)
            totals = total_ref[:, part]
            pieces = [dot(piece, same) for piece in split3(jnp.log(totals))]
            lift = jnp.exp(inner_temp * (pieces[0] + pieces[1] + pieces[2]))
            left_ref[:, part] = lift / totals
            sums_ref[:, part] += jnp.broadcast_to(jnp.sum(lift, axis=0, keepdims=True), (8, lanes))
        for c in range(height // half):
            part = slice(c * half, (c + 1) * half)

            def backward(step, acc):
                for g in range(NEG_STEP):
                    k = step * NEG_STEP + g
                    acc = acc + dot(turned_ref[k], expo_ref[k, :, part]) * left_ref[pl.ds(k, 1), part]
                return acc

            back_ref[:, part] = lax.fori_loop(0, chunk // NEG_STEP, backward, back_ref[:, part])
        return carry

    lax.fori_loop(0, total // chunk, block, 0)
    for c in range(height // lanes):
        part = slice(c * lanes, (c + 1) * lanes)
        acc_ref[part, :] = back_ref[:, part].T


def negatives(rows, queries, index):
    total = rows.shape[0]
    count, tokens, dim = queries.shape
    wide = index.shape[1]
    height = count * tokens
    chunk = math.gcd(total, NEG_CHUNK)
    return pl.pallas_call(
        functools.partial(neg_kernel, tokens=tokens),
        in_specs=[
            pl.BlockSpec(memory_space=pltpu.SMEM),
            pl.BlockSpec(memory_space=pltpu.VMEM),
            pl.BlockSpec(memory_space=pltpu.HBM),
        ],
        out_specs=[pl.BlockSpec(memory_space=pltpu.VMEM)] * 2,
        out_shape=[
            jax.ShapeDtypeStruct((height, dim), jnp.float32),
            jax.ShapeDtypeStruct((8, height), jnp.float32),
        ],
        scratch_shapes=[
            pltpu.VMEM((dim, height), jnp.bfloat16),
            pltpu.VMEM((chunk, wide, height), jnp.bfloat16),
            pltpu.VMEM((chunk, height), jnp.float32),
            pltpu.VMEM((chunk, height), jnp.float32),
            pltpu.VMEM((dim, height), jnp.float32),
            pltpu.VMEM((NEG_STEP * wide, height), jnp.float32),
            pltpu.VMEM((2, chunk, wide, dim), jnp.bfloat16),
            pltpu.VMEM((chunk, dim, wide), jnp.bfloat16),
            pltpu.SemaphoreType.DMA((2,)),
        ],
        compiler_params=pltpu.CompilerParams(vmem_limit_bytes=2 * VMEM_LIMIT),
        cost_estimate=pl.CostEstimate(
            flops=4 * total * height * wide * dim,
            bytes_accessed=2 * total * wide * dim,
            transcendentals=total * height * wide,
        ),
        name="negatives",
    )(rows, queries.reshape(height, dim), pltpu.with_memory_space_constraint(index, pltpu.HBM))


def finish_kernel(queries_ref, teacher_ref, back_ref, sums_ref, *refs, owners):
    messages, (loss_ref, grad_ref) = refs[:owners], refs[owners:]
    count, tokens, dim = grad_ref.shape
    cut = count * 2 * tokens
    scores = jnp.zeros((count, dim), jnp.float32)
    for message in messages:
        for k in range(3):
            scores = scores + message[cut + k * count : cut + (k + 1) * count, :].astype(jnp.float32)
    totals = []
    for q in range(count):
        total = scores[q : q + 1, 0:1] + sums_ref[0:1, q * tokens : q * tokens + 1]
        totals.append(total)
        pulled = back_ref[q * tokens : (q + 1) * tokens, :]
        right = jnp.zeros((tokens, dim), jnp.float32)
        for message in messages:
            pulled = pulled + message[q * 2 * tokens : (q * 2 + 1) * tokens, :].astype(jnp.float32)
            right = right + message[(q * 2 + 1) * tokens : (q + 1) * 2 * tokens, :].astype(jnp.float32)
        pulled = pulled / total - right
        wide = queries_ref[q].astype(jnp.float32)
        radius = jnp.sqrt(jnp.sum(wide * wide, axis=-1, keepdims=True) + epsilon)
        unit = wide / radius
        grad_ref[q] = (pulled - unit * jnp.sum(unit * pulled, axis=-1, keepdims=True)) / radius
    spread = jnp.log(jnp.concatenate(totals, axis=0))
    teacher = teacher_ref[...]
    log_target = teacher - jnp.log(jnp.sum(jnp.exp(teacher), axis=-1, keepdims=True))
    gain = jnp.sum(jnp.exp(log_target) * (log_target + spread), axis=-1, keepdims=True)
    loss_ref[...] = gain - scores[:, dim // 2 : dim // 2 + 1] + jnp.zeros_like(loss_ref)


def finish(queries, teacher, back, sums, messages):
    count, tokens, dim = queries.shape
    owners = len(messages)
    return pl.pallas_call(
        functools.partial(finish_kernel, owners=owners),
        in_specs=[pl.BlockSpec(memory_space=pltpu.VMEM)] * (4 + owners),
        out_specs=[pl.BlockSpec(memory_space=pltpu.VMEM)] * 2,
        out_shape=[
            jax.ShapeDtypeStruct((count, dim), jnp.float32),
            jax.ShapeDtypeStruct((count, tokens, dim), jnp.float32),
        ],
        compiler_params=pltpu.CompilerParams(vmem_limit_bytes=VMEM_LIMIT),
        name="finish",
    )(queries, teacher, back, sums, *messages)


def on_device(queries, index, cand_owner, cand_row, neg_row, teacher):
    count, tokens, dim = queries.shape
    cands = cand_row.shape[1]
    shard = index.shape[0]
    owners = lax.axis_size("corpus")
    room = (2 * count * cands + owners - 1) // owners
    me = lax.axis_index("corpus").astype(jnp.int32)
    group = lax.axis_size("blk")

    def from_step(value, axis, size, step):
        return lax.ppermute(value, axis, [((i + step) % size, i) for i in range(size)])

    def gathered(value, axis, size):
        return [value] + [from_step(value, axis, size, step) for step in range(1, size)]

    code = (cand_owner[..., 0] * shard + cand_row).astype(jnp.float32)
    meta = jnp.concatenate([code, teacher], axis=1)
    all_neg = jnp.concatenate(gathered(neg_row, "blk", group), axis=0).reshape(-1)
    def told(value):
        copies = jnp.broadcast_to(value[None], (owners,) + value.shape)
        return lax.all_to_all(copies, "corpus", split_axis=0, concat_axis=0, tiled=True)

    all_meta = told(meta).reshape(owners * count, -1)
    all_queries = told(queries)
    rows, targets = prep(me.reshape(1), all_meta, shard, cands)
    rows, all_neg = lax.optimization_barrier((rows, all_neg))
    neg_acc, neg_sum = negatives(all_neg, queries, index)
    index, all_queries, rows, neg_acc = lax.optimization_barrier((index, all_queries, rows, neg_acc))
    index, turned, inverse = load(index)
    messages = []
    order = list(range(1, owners)) + [0]
    groups = [order[first : first + SOURCES] for first in range(0, owners, SOURCES)]
    for steps in groups:
        sources = [lax.rem(me + step, owners) for step in steps]
        found = pairs(
            sources, rows, targets, all_queries, inverse, index, turned, cands, room
        )
        for step, message in zip(steps, found):
            if step:
                message = lax.ppermute(
                    message, "corpus", [(i, (i + step) % owners) for i in range(owners)]
                )
            messages.append(message)
    losses, query_grads = finish(queries, teacher, neg_acc, neg_sum, messages)
    return (losses[:, 0], query_grads)


def solution(mesh):
    placed = (
        P(("corpus", "blk"), None, None),
        P("corpus", None, None),
        P(("corpus", "blk"), None, None),
        P(("corpus", "blk"), None),
        P(("corpus", "blk"), None),
        P(("corpus", "blk"), None),
    )
    return jax.shard_map(
        on_device,
        mesh=mesh,
        in_specs=placed,
        out_specs=(P(("corpus", "blk")), P(("corpus", "blk"), None, None)),
        check_vma=False,
    )
```

```python
import functools
import math

import jax
import jax.numpy as jnp
from jax import lax
from jax.experimental import pallas as pl
from jax.experimental.pallas import tpu as pltpu
from jax.sharding import PartitionSpec as P

inner_temp = 0.1
epsilon = 1e-06
LOG2E = 1.4426950408889634
GROUP = 4
UNITS = 12
LOADS = 8
LOAD_STEP = 16
NEG_STEP = 8
NEG_CHUNK = 24
SOURCES = 2
VMEM_LIMIT = 8 * 1024 * 1024
LAST = (((1,), (1,)), ((), ()))


def dot_last(a, b):
    return lax.dot_general(a, b, LAST, preferred_element_type=jnp.float32)


def dot(a, b):
    return jnp.dot(a, b, preferred_element_type=jnp.float32)


def split3(x):
    high = x.astype(jnp.bfloat16)
    rest = x - high.astype(jnp.float32)
    mid = rest.astype(jnp.bfloat16)
    low = (rest - mid.astype(jnp.float32)).astype(jnp.bfloat16)
    return high, mid, low


def rounded_queries(raw):
    wide = raw.astype(jnp.float32)
    radius = jnp.sqrt(jnp.sum(wide * wide, axis=-1, keepdims=True) + epsilon)
    return (wide / radius).astype(jnp.bfloat16)


def load_shard(index_ref, tiles_ref, turned_ref, inverse_ref, sems):
    count = index_ref.shape[0]
    chunk = count // LOADS

    def copy(part):
        at = pl.ds(part * chunk, chunk)
        return pltpu.make_async_copy(index_ref.at[at], tiles_ref.at[at], sems.at[part])

    for part in range(LOADS):
        copy(part).start()

    for part in range(LOADS):
        copy(part).wait()

        def body(step, carry):
            first = part * chunk + step * LOAD_STEP
            squares = []
            turned = []
            for k in range(LOAD_STEP):
                tile = tiles_ref[first + k].T
                turned.append(tile)
                wide = tile.astype(jnp.float32)
                squares.append(jnp.sum(wide * wide, axis=0, keepdims=True))
            for k in range(LOAD_STEP):
                turned_ref[first + k] = turned[k]
            at = pl.ds(pl.multiple_of(first, LOAD_STEP), LOAD_STEP)
            inverse_ref[at, :] = lax.rsqrt(jnp.concatenate(squares, axis=0) + epsilon)
            return carry

        lax.fori_loop(0, chunk // LOAD_STEP, body, 0)


def load(index):
    count, tokens, dim = index.shape
    return pl.pallas_call(
        load_shard,
        in_specs=[pl.BlockSpec(memory_space=pltpu.HBM)],
        out_specs=[pl.BlockSpec(memory_space=pltpu.VMEM)] * 3,
        out_shape=[
            pltpu.VMEM((count, tokens, dim), jnp.bfloat16),
            pltpu.VMEM((count, dim, tokens), jnp.bfloat16),
            pltpu.VMEM((count, tokens), jnp.float32),
        ],
        scratch_shapes=[pltpu.SemaphoreType.DMA((LOADS,))],
        compiler_params=pltpu.CompilerParams(vmem_limit_bytes=VMEM_LIMIT),
        cost_estimate=pl.CostEstimate(
            flops=2 * count * tokens * dim,
            bytes_accessed=2 * count * tokens * dim,
            transcendentals=count * tokens,
        ),
        name="load",
    )(pltpu.with_memory_space_constraint(index, pltpu.HBM))


def prep_kernel(me_ref, meta_ref, rows_ref, target_ref, value_ref, place_ref, result_ref, *, shard, cands):
    count = meta_ref.shape[0]
    code = meta_ref[:, :cands]
    owner = jnp.floor((code + 0.5) * (1.0 / shard))
    row = code - owner * shard
    teacher = meta_ref[:, cands:]
    log_target = teacher - jnp.log(jnp.sum(jnp.exp(teacher), axis=-1, keepdims=True))
    target = jnp.exp(log_target)
    mine = (owner == me_ref[0].astype(jnp.float32)).astype(jnp.float32)
    before = lax.broadcasted_iota(jnp.int32, (cands, cands), 0) < lax.broadcasted_iota(
        jnp.int32, (cands, cands), 1
    )
    place = dot(mine.astype(jnp.bfloat16), before.astype(jnp.float32).astype(jnp.bfloat16))
    wide = value_ref.shape[1]
    pad = jnp.zeros((count, wide - cands), jnp.float32)
    place_ref[...] = jnp.concatenate([jnp.where(mine > 0, place, -1.0), pad - 1.0], axis=1)
    row_high = jnp.floor(row * (1.0 / 16))
    first, second, third = split3(target)
    values = [row_high, row - 16 * row_high, first, second, third]
    for v in range(8):
        value = values[v].astype(jnp.float32) if v < len(values) else jnp.zeros_like(row)
        value_ref[pl.ds(v, count, stride=8), :] = jnp.concatenate([value, pad], axis=1)
    spots = lax.broadcasted_iota(jnp.int32, (wide, wide), 0).astype(jnp.float32)

    def body(step, carry):
        for k in range(8):
            q = step * 8 + k
            hot = jnp.where(place_ref[pl.ds(q, 1), :] == spots, 1.0, 0.0).astype(jnp.bfloat16)
            at = pl.ds(pl.multiple_of(q * 8, 8), 8)
            result_ref[at, :] = dot_last(value_ref[at, :].astype(jnp.bfloat16), hot)
        return carry

    lax.fori_loop(0, count // 8, body, 0)
    result = [result_ref[pl.ds(v, count, stride=8), :] for v in range(5)]
    found = jnp.sum(mine, axis=-1, keepdims=True)
    lane = lax.broadcasted_iota(jnp.int32, (count, wide), 1)
    rows = 16 * result[0] + result[1]
    rows_ref[...] = jnp.where(lane < cands, rows, found).astype(jnp.int32)
    listed = jnp.where(lane.astype(jnp.float32) < found, result[2] + result[3] + result[4], -1.0)
    stacked = jnp.concatenate(split3(listed), axis=0)
    steps = cands // GROUP
    source = lax.broadcasted_iota(jnp.int32, (wide, wide), 0)
    block = lax.broadcasted_iota(jnp.int32, (wide, wide), 1) // (wide // GROUP)
    for t in range(steps):
        pick = jnp.where(source == block + t * GROUP, 1.0, 0.0).astype(jnp.bfloat16)
        spread = dot(stacked, pick)
        target_ref[pl.ds(t, count, stride=steps), :] = (
            spread[:count] + spread[count : 2 * count] + spread[2 * count :]
        )


def prep(me, meta, shard, cands):
    count = meta.shape[0]
    wide = 128
    return pl.pallas_call(
        functools.partial(prep_kernel, shard=shard, cands=cands),
        in_specs=[
            pl.BlockSpec(memory_space=pltpu.SMEM),
            pl.BlockSpec(memory_space=pltpu.VMEM),
        ],
        out_specs=[pl.BlockSpec(memory_space=pltpu.VMEM)] * 2,
        out_shape=[
            jax.ShapeDtypeStruct((count, wide), jnp.int32),
            jax.ShapeDtypeStruct((count * (cands // GROUP), wide), jnp.float32),
        ],
        scratch_shapes=[
            pltpu.VMEM((count * 8, wide), jnp.float32),
            pltpu.VMEM((count, wide), jnp.float32),
            pltpu.VMEM((count * 8, wide), jnp.float32),
        ],
        compiler_params=pltpu.CompilerParams(vmem_limit_bytes=VMEM_LIMIT),
        cost_estimate=pl.CostEstimate(flops=count * wide, bytes_accessed=count * wide, transcendentals=0),
        name="prep",
    )(me, meta)


def pair_kernel(source_ref, rows_ref, target_ref, queries_ref, inverse_ref, index_ref, turned_ref, *refs, cands, sources):
    out_refs = refs[:sources]
    (units_ref, unit_ref, acc_ref, total_ref, left_ref, right_ref, back_ref, raw_ref) = refs[sources:]
    count, tokens, dim = unit_ref.shape
    wide = rows_ref.shape[1]
    per_query = cands // GROUP
    slots = count * per_query
    bits = per_query.bit_length() - 1
    total = jnp.int32(0)
    for q in range(count):
        for t in range(per_query):
            units_ref[total + t] = jnp.int32(q * per_query + t)
        total = total + lax.div(rows_ref[q, cands] + (GROUP - 1), GROUP)
    for t in range(2 * UNITS):
        units_ref[total + t] = jnp.int32(slots)
    steps = lax.div(total + (UNITS - 1), UNITS)

    def entry(number):
        slot = units_ref[number]
        q = jnp.minimum(lax.shift_right_logical(slot, bits), count - 1)
        return slot, q, jnp.bitwise_and(slot, per_query - 1) * GROUP

    for q in range(count):
        unit_ref[q] = rounded_queries(queries_ref[0, q])
    acc_ref[...] = jnp.zeros_like(acc_ref)
    ones = jnp.ones((8, wide), jnp.bfloat16)

    def tiles_of(number, ref):
        _, q, base = entry(number)
        return q, [ref[rows_ref[q, base + g]] for g in range(GROUP)]

    def multiply(step):
        found = []
        for u in range(UNITS):
            q, tiles = tiles_of(step * UNITS + u, turned_ref)
            found.append(dot(unit_ref[q], jnp.concatenate(tiles, axis=1)))
        return found

    def forward(step, carry):
        expos, weights, rows = [], [], []
        for u in range(UNITS):
            _, q, base = entry(step * UNITS + u)
            for g in range(GROUP):
                rows.append(rows_ref[q, base + g])
                inverse = inverse_ref[pl.ds(rows[-1], 1), :]
                raw = raw_ref[u, :, g * wide : (g + 1) * wide]
                expo = jnp.exp2(raw * (inverse * (LOG2E / inner_temp)))
                expos.append(expo.astype(jnp.bfloat16))
                weights.append((expo * inverse).astype(jnp.bfloat16))
        following = multiply(step + 1)
        backs = []
        for u in range(UNITS):
            for k in range(u * GROUP, (u + 1) * GROUP, 2):
                part = dot(
                    jnp.concatenate(weights[k : k + 2], axis=0),
                    jnp.concatenate([index_ref[row] for row in rows[k : k + 2]], axis=1),
                )
                backs += [part[:tokens, :dim], part[tokens:, dim:]]
        totals = []
        for u in range(0, UNITS, 2):
            part = dot_last(ones, jnp.concatenate(expos[u * GROUP : (u + 2) * GROUP], axis=0))
            totals += [part[0:1, :wide], part[0:1, wide:]]
        for u in range(UNITS):
            back_ref[step * UNITS + u] = jnp.concatenate(
                backs[u * GROUP : (u + 1) * GROUP], axis=0
            ).astype(jnp.bfloat16)
            total_ref[pl.ds(units_ref[step * UNITS + u], 1), :] = totals[u]
        for u in range(UNITS):
            raw_ref[u] = following[u]
        return carry

    for u, raw in enumerate(multiply(0)):
        raw_ref[u] = raw
    lax.fori_loop(0, steps, forward, 0)

    target = target_ref[...]
    held = target >= 0.0
    totals = jnp.where(held, total_ref[0:slots, :], 1.0)
    target = jnp.where(held, target, 0.0)
    same = lax.broadcasted_iota(jnp.int32, (wide, wide), 0) // tokens == lax.broadcasted_iota(
        jnp.int32, (wide, wide), 1
    ) // tokens
    same = jnp.where(same, 1.0, 0.0).astype(jnp.bfloat16)
    parts = [dot(part, same) for part in split3(jnp.log(totals))]
    score = inner_temp * (parts[0] + parts[1] + parts[2])
    lift = jnp.where(held, jnp.exp(score), 0.0)
    recip = 1.0 / totals
    left_ref[0:slots, :] = lift * recip
    right_ref[0:slots, :] = target * recip
    left_ref[slots:, :] = jnp.zeros_like(left_ref[slots:, :])
    right_ref[slots:, :] = jnp.zeros_like(right_ref[slots:, :])

    def per_source(values):
        rows = jnp.sum(values.reshape(count, per_query, wide), axis=1)
        return jnp.sum(rows, axis=-1, keepdims=True) * (1.0 / tokens)

    lane = lax.broadcasted_iota(jnp.int32, (count, wide), 1)
    sums = jnp.where(lane < wide // 2, per_source(lift), per_source(target * score))
    diagonal = lax.broadcasted_iota(jnp.int32, (tokens, wide), 0) == lax.broadcasted_iota(
        jnp.int32, (tokens, wide), 1
    ) % tokens

    def backward(step, carry):
        owners, sides = [], []
        for u in range(UNITS):
            slot, q, _ = entry(step * UNITS + u)
            left = jnp.where(diagonal, left_ref[pl.ds(slot, 1), :], 0.0)
            right = jnp.where(diagonal, right_ref[pl.ds(slot, 1), :], 0.0)
            both = jnp.concatenate([left, right], axis=0)
            high = both.astype(jnp.bfloat16)
            sides += [high, (both - high.astype(jnp.float32)).astype(jnp.bfloat16)]
            owners.append(q)
        parts = []
        for u in range(0, UNITS, 2):
            pulled = dot(
                jnp.concatenate(sides[2 * u : 2 * u + 4], axis=0),
                jnp.concatenate([back_ref[step * UNITS + u], back_ref[step * UNITS + u + 1]], axis=1),
            )
            height = 2 * tokens
            parts += [
                pulled[:height, :dim] + pulled[height : 2 * height, :dim],
                pulled[2 * height : 3 * height, dim:] + pulled[3 * height :, dim:],
            ]
        for q, part in zip(owners, parts):
            acc_ref[q] += part
        return carry

    lax.fori_loop(0, steps, backward, 0)
    for k, out_ref in enumerate(out_refs):
        @pl.when(pl.program_id(0) == k)
        def _():
            for q in range(count):
                out_ref[pl.ds(q * 2 * tokens, 2 * tokens), :] = acc_ref[q].astype(jnp.bfloat16)
            for j, part in enumerate(split3(sums)):
                out_ref[pl.ds(count * 2 * tokens + j * count, count), :] = part


def pairs(sources, rows, targets, queries, inverse, index, turned, cands, room):
    count, tokens, dim = queries.shape[1:]
    wide = rows.shape[1]
    per_query = cands // GROUP
    slots = count * per_query
    most = (room + (GROUP - 1) * count) // GROUP + UNITS
    height = count * 2 * tokens + 3 * count
    return pl.pallas_call(
        functools.partial(pair_kernel, cands=cands, sources=len(sources)),
        grid_spec=pltpu.PrefetchScalarGridSpec(
            num_scalar_prefetch=1,
            grid=(len(sources),),
            in_specs=[
                pl.BlockSpec((count, wide), lambda i, s: (s[i], 0), memory_space=pltpu.SMEM),
                pl.BlockSpec((slots, wide), lambda i, s: (s[i], 0)),
                pl.BlockSpec((1, count, tokens, dim), lambda i, s: (s[i], 0, 0, 0)),
                pl.BlockSpec(memory_space=pltpu.VMEM),
                pl.BlockSpec(memory_space=pltpu.VMEM),
                pl.BlockSpec(memory_space=pltpu.VMEM),
            ],
            out_specs=[pl.BlockSpec((height, dim), lambda i, s: (0, 0))] * len(sources),
            scratch_shapes=[
                pltpu.SMEM((slots + per_query + 2 * UNITS,), jnp.int32),
                pltpu.VMEM((count, tokens, dim), jnp.bfloat16),
                pltpu.VMEM((count, 2 * tokens, dim), jnp.float32),
                pltpu.VMEM((slots + 8, wide), jnp.float32),
                pltpu.VMEM((slots + 8, wide), jnp.float32),
                pltpu.VMEM((slots + 8, wide), jnp.float32),
                pltpu.VMEM((most, GROUP * tokens, dim), jnp.bfloat16),
                pltpu.VMEM((UNITS, tokens, GROUP * wide), jnp.float32),
            ],
        ),
        out_shape=[jax.ShapeDtypeStruct((height, dim), jnp.bfloat16)] * len(sources),
        compiler_params=pltpu.CompilerParams(vmem_limit_bytes=VMEM_LIMIT),
        cost_estimate=pl.CostEstimate(
            flops=6 * len(sources) * room * tokens * wide * dim,
            bytes_accessed=2 * len(sources) * room * wide * dim,
            transcendentals=len(sources) * room * tokens * wide,
        ),
        name="pairs",
    )(jnp.stack(sources), rows, targets, queries, inverse, index, turned)


def neg_kernel(rows_ref, queries_ref, shard_ref, acc_ref, sums_ref,
               unit_ref, expo_ref, total_ref, left_ref, back_ref, raw_ref, tiles_ref, turned_ref, sems,
               *, tokens):
    total = rows_ref.shape[0]
    chunk = expo_ref.shape[0]
    height, dim = queries_ref.shape
    wide = shard_ref.shape[1]
    lanes = 128
    half = min(height, 256)
    def fetch(number):
        place = jnp.bitwise_and(number, 1)
        for k in range(chunk):
            pltpu.make_async_copy(
                shard_ref.at[rows_ref[number * chunk + k]], tiles_ref.at[place, k], sems.at[place]
            ).start()

    fetch(jnp.int32(0))
    for c in range(height // lanes):
        part = slice(c * lanes, (c + 1) * lanes)
        unit_ref[:, part] = rounded_queries(queries_ref[part]).T
    back_ref[...] = jnp.zeros_like(back_ref)
    sums_ref[...] = jnp.zeros_like(sums_ref)

    same = lax.broadcasted_iota(jnp.int32, (lanes, lanes), 0) // tokens == lax.broadcasted_iota(
        jnp.int32, (lanes, lanes), 1
    ) // tokens
    same = jnp.where(same, 1.0, 0.0).astype(jnp.bfloat16)

    def block(number, carry):
        @pl.when(number + 1 < total // chunk)
        def _():
            fetch(number + 1)

        place = jnp.bitwise_and(number, 1)
        pltpu.make_async_copy(shard_ref.at[pl.ds(0, chunk)], tiles_ref.at[place], sems.at[place]).wait()

        def tiles_of(step):
            first = jnp.minimum(step, chunk // NEG_STEP - 1) * NEG_STEP
            return tiles_ref[place, pl.ds(first, NEG_STEP)].reshape(NEG_STEP * wide, dim)

        def forward(step, carry):
            first = step * NEG_STEP
            tiles = tiles_of(step)
            broad = tiles.astype(jnp.float32)
            inverse = lax.rsqrt(jnp.sum(broad * broad, axis=-1, keepdims=True) + epsilon)
            expo = jnp.exp2(raw_ref[...] * (inverse * (LOG2E / inner_temp)))
            following = dot(tiles_of(step + 1), unit_ref[...])
            for g in range(NEG_STEP):
                part = slice(g * wide, (g + 1) * wide)
                turned_ref[first + g] = tiles[part].T
                expo_ref[first + g] = (expo[part] * inverse[part]).astype(jnp.bfloat16)
                total_ref[pl.ds(first + g, 1), :] = jnp.sum(expo[part], axis=0, keepdims=True)
            raw_ref[...] = following
            return carry

        raw_ref[...] = dot(tiles_of(0), unit_ref[...])
        lax.fori_loop(0, chunk // NEG_STEP, forward, 0)
        for c in range(height // lanes):
            part = slice(c * lanes, (c + 1) * lanes)
            totals = total_ref[:, part]
            pieces = [dot(piece, same) for piece in split3(jnp.log(totals))]
            lift = jnp.exp(inner_temp * (pieces[0] + pieces[1] + pieces[2]))
            left_ref[:, part] = lift / totals
            sums_ref[:, part] += jnp.broadcast_to(jnp.sum(lift, axis=0, keepdims=True), (8, lanes))
        for c in range(height // half):
            part = slice(c * half, (c + 1) * half)

            def backward(step, acc):
                for g in range(NEG_STEP):
                    k = step * NEG_STEP + g
                    acc = acc + dot(turned_ref[k], expo_ref[k, :, part]) * left_ref[pl.ds(k, 1), part]
                return acc

            back_ref[:, part] = lax.fori_loop(0, chunk // NEG_STEP, backward, back_ref[:, part])
        return carry

    lax.fori_loop(0, total // chunk, block, 0)
    for c in range(height // lanes):
        part = slice(c * lanes, (c + 1) * lanes)
        acc_ref[part, :] = back_ref[:, part].T


def negatives(rows, queries, index):
    total = rows.shape[0]
    count, tokens, dim = queries.shape
    wide = index.shape[1]
    height = count * tokens
    chunk = math.gcd(total, NEG_CHUNK)
    return pl.pallas_call(
        functools.partial(neg_kernel, tokens=tokens),
        in_specs=[
            pl.BlockSpec(memory_space=pltpu.SMEM),
            pl.BlockSpec(memory_space=pltpu.VMEM),
            pl.BlockSpec(memory_space=pltpu.HBM),
        ],
        out_specs=[pl.BlockSpec(memory_space=pltpu.VMEM)] * 2,
        out_shape=[
            jax.ShapeDtypeStruct((height, dim), jnp.float32),
            jax.ShapeDtypeStruct((8, height), jnp.float32),
        ],
        scratch_shapes=[
            pltpu.VMEM((dim, height), jnp.bfloat16),
            pltpu.VMEM((chunk, wide, height), jnp.bfloat16),
            pltpu.VMEM((chunk, height), jnp.float32),
            pltpu.VMEM((chunk, height), jnp.float32),
            pltpu.VMEM((dim, height), jnp.float32),
            pltpu.VMEM((NEG_STEP * wide, height), jnp.float32),
            pltpu.VMEM((2, chunk, wide, dim), jnp.bfloat16),
            pltpu.VMEM((chunk, dim, wide), jnp.bfloat16),
            pltpu.SemaphoreType.DMA((2,)),
        ],
        compiler_params=pltpu.CompilerParams(vmem_limit_bytes=3 * VMEM_LIMIT),
        cost_estimate=pl.CostEstimate(
            flops=4 * total * height * wide * dim,
            bytes_accessed=2 * total * wide * dim,
            transcendentals=total * height * wide,
        ),
        name="negatives",
    )(rows, queries.reshape(height, dim), pltpu.with_memory_space_constraint(index, pltpu.HBM))


def finish_kernel(queries_ref, teacher_ref, back_ref, sums_ref, *refs, owners):
    messages, (loss_ref, grad_ref) = refs[:owners], refs[owners:]
    count, tokens, dim = grad_ref.shape
    cut = count * 2 * tokens
    scores = jnp.zeros((count, dim), jnp.float32)
    for message in messages:
        for k in range(3):
            scores = scores + message[cut + k * count : cut + (k + 1) * count, :].astype(jnp.float32)
    totals = []
    for q in range(count):
        total = scores[q : q + 1, 0:1] + sums_ref[0:1, q * tokens : q * tokens + 1]
        totals.append(total)
        pulled = back_ref[q * tokens : (q + 1) * tokens, :]
        right = jnp.zeros((tokens, dim), jnp.float32)
        for message in messages:
            pulled = pulled + message[q * 2 * tokens : (q * 2 + 1) * tokens, :].astype(jnp.float32)
            right = right + message[(q * 2 + 1) * tokens : (q + 1) * 2 * tokens, :].astype(jnp.float32)
        pulled = pulled / total - right
        wide = queries_ref[q].astype(jnp.float32)
        radius = jnp.sqrt(jnp.sum(wide * wide, axis=-1, keepdims=True) + epsilon)
        unit = wide / radius
        grad_ref[q] = (pulled - unit * jnp.sum(unit * pulled, axis=-1, keepdims=True)) / radius
    spread = jnp.log(jnp.concatenate(totals, axis=0))
    teacher = teacher_ref[...]
    log_target = teacher - jnp.log(jnp.sum(jnp.exp(teacher), axis=-1, keepdims=True))
    gain = jnp.sum(jnp.exp(log_target) * (log_target + spread), axis=-1, keepdims=True)
    loss_ref[...] = gain - scores[:, dim // 2 : dim // 2 + 1] + jnp.zeros_like(loss_ref)


def finish(queries, teacher, back, sums, messages):
    count, tokens, dim = queries.shape
    owners = len(messages)
    return pl.pallas_call(
        functools.partial(finish_kernel, owners=owners),
        in_specs=[pl.BlockSpec(memory_space=pltpu.VMEM)] * (4 + owners),
        out_specs=[pl.BlockSpec(memory_space=pltpu.VMEM)] * 2,
        out_shape=[
            jax.ShapeDtypeStruct((count, dim), jnp.float32),
            jax.ShapeDtypeStruct((count, tokens, dim), jnp.float32),
        ],
        compiler_params=pltpu.CompilerParams(vmem_limit_bytes=VMEM_LIMIT),
        name="finish",
    )(queries, teacher, back, sums, *messages)


def on_device(queries, index, cand_owner, cand_row, neg_row, teacher):
    count, tokens, dim = queries.shape
    cands = cand_row.shape[1]
    shard = index.shape[0]
    owners = lax.axis_size("corpus")
    room = (2 * count * cands + owners - 1) // owners
    me = lax.axis_index("corpus").astype(jnp.int32)
    group = lax.axis_size("blk")

    def from_step(value, axis, size, step):
        return lax.ppermute(value, axis, [((i + step) % size, i) for i in range(size)])

    def gathered(value, axis, size):
        return [value] + [from_step(value, axis, size, step) for step in range(1, size)]

    code = (cand_owner[..., 0] * shard + cand_row).astype(jnp.float32)
    meta = jnp.concatenate([code, teacher], axis=1)
    all_neg = jnp.concatenate(gathered(neg_row, "blk", group), axis=0).reshape(-1)
    def told(value):
        copies = jnp.broadcast_to(value[None], (owners,) + value.shape)
        return lax.all_to_all(copies, "corpus", split_axis=0, concat_axis=0, tiled=True)

    all_meta = told(meta).reshape(owners * count, -1)
    all_queries = told(queries)
    rows, targets = prep(me.reshape(1), all_meta, shard, cands)
    rows, all_neg = lax.optimization_barrier((rows, all_neg))
    neg_acc, neg_sum = negatives(all_neg, queries, index)
    index, all_queries, rows, neg_acc = lax.optimization_barrier((index, all_queries, rows, neg_acc))
    index, turned, inverse = load(index)
    messages = []
    order = list(range(1, owners)) + [0]
    groups = [order[first : first + SOURCES] for first in range(0, owners, SOURCES)]
    for steps in groups:
        sources = [lax.rem(me + step, owners) for step in steps]
        found = pairs(
            sources, rows, targets, all_queries, inverse, index, turned, cands, room
        )
        for step, message in zip(steps, found):
            if step:
                message = lax.ppermute(
                    message, "corpus", [(i, (i + step) % owners) for i in range(owners)]
                )
            messages.append(message)
    losses, query_grads = finish(queries, teacher, neg_acc, neg_sum, messages)
    return (losses[:, 0], query_grads)


def solution(mesh):
    placed = (
        P(("corpus", "blk"), None, None),
        P("corpus", None, None),
        P(("corpus", "blk"), None, None),
        P(("corpus", "blk"), None),
        P(("corpus", "blk"), None),
        P(("corpus", "blk"), None),
    )
    return jax.shard_map(
        on_device,
        mesh=mesh,
        in_specs=placed,
        out_specs=(P(("corpus", "blk")), P(("corpus", "blk"), None, None)),
        check_vma=False,
    )
```

```python
import functools
import math

import jax
import jax.numpy as jnp
from jax import lax
from jax.experimental import pallas as pl
from jax.experimental.pallas import tpu as pltpu
from jax.sharding import PartitionSpec as P

inner_temp = 0.1
epsilon = 1e-06
LOG2E = 1.4426950408889634
GROUP = 4
UNITS = 12
LOADS = 8
LOAD_STEP = 16
NEG_STEP = 8
NEG_CHUNK = 24
SOURCES = 2
CODE = 64
VMEM_LIMIT = 8 * 1024 * 1024
LAST = (((1,), (1,)), ((), ()))


def dot_last(a, b):
    return lax.dot_general(a, b, LAST, preferred_element_type=jnp.float32)


def dot(a, b):
    return jnp.dot(a, b, preferred_element_type=jnp.float32)


def split3(x):
    high = x.astype(jnp.bfloat16)
    rest = x - high.astype(jnp.float32)
    mid = rest.astype(jnp.bfloat16)
    low = (rest - mid.astype(jnp.float32)).astype(jnp.bfloat16)
    return high, mid, low


def rounded_queries(raw):
    wide = raw.astype(jnp.float32)
    radius = jnp.sqrt(jnp.sum(wide * wide, axis=-1, keepdims=True) + epsilon)
    return (wide / radius).astype(jnp.bfloat16)


def load_shard(index_ref, tiles_ref, turned_ref, inverse_ref, sems):
    count = index_ref.shape[0]
    chunk = count // LOADS

    def copy(part):
        at = pl.ds(part * chunk, chunk)
        return pltpu.make_async_copy(index_ref.at[at], tiles_ref.at[at], sems.at[part])

    for part in range(LOADS):
        copy(part).start()

    for part in range(LOADS):
        copy(part).wait()

        def body(step, carry):
            first = part * chunk + step * LOAD_STEP
            squares = []
            turned = []
            for k in range(LOAD_STEP):
                tile = tiles_ref[first + k].T
                turned.append(tile)
                wide = tile.astype(jnp.float32)
                squares.append(jnp.sum(wide * wide, axis=0, keepdims=True))
            for k in range(LOAD_STEP):
                turned_ref[first + k] = turned[k]
            at = pl.ds(pl.multiple_of(first, LOAD_STEP), LOAD_STEP)
            inverse_ref[at, :] = lax.rsqrt(jnp.concatenate(squares, axis=0) + epsilon)
            return carry

        lax.fori_loop(0, chunk // LOAD_STEP, body, 0)


def load(index):
    count, tokens, dim = index.shape
    return pl.pallas_call(
        load_shard,
        in_specs=[pl.BlockSpec(memory_space=pltpu.HBM)],
        out_specs=[pl.BlockSpec(memory_space=pltpu.VMEM)] * 3,
        out_shape=[
            pltpu.VMEM((count, tokens, dim), jnp.bfloat16),
            pltpu.VMEM((count, dim, tokens), jnp.bfloat16),
            pltpu.VMEM((count, tokens), jnp.float32),
        ],
        scratch_shapes=[pltpu.SemaphoreType.DMA((LOADS,))],
        compiler_params=pltpu.CompilerParams(vmem_limit_bytes=VMEM_LIMIT),
        cost_estimate=pl.CostEstimate(
            flops=2 * count * tokens * dim,
            bytes_accessed=2 * count * tokens * dim,
            transcendentals=count * tokens,
        ),
        name="load",
    )(pltpu.with_memory_space_constraint(index, pltpu.HBM))


def prep_kernel(me_ref, told_ref, rows_ref, target_ref, value_ref, place_ref, result_ref, *, shard, cands):
    sources, height = told_ref.shape[:2]
    each = rows_ref.shape[0] // sources
    count = rows_ref.shape[0]
    base = height - 3 * each

    def part(k):
        rows = [told_ref[s, base + k * each : base + (k + 1) * each, :] for s in range(sources)]
        return jnp.concatenate(rows, axis=0).astype(jnp.float32)

    codes, upper, lower = part(0), part(1), part(2)
    code = CODE * codes[:, :cands] + codes[:, cands:]
    owner = jnp.floor((code + 0.5) * (1.0 / shard))
    row = code - owner * shard
    teacher = upper[:, :cands] + upper[:, cands:] + lower[:, :cands]
    log_target = teacher - jnp.log(jnp.sum(jnp.exp(teacher), axis=-1, keepdims=True))
    target = jnp.exp(log_target)
    mine = (owner == me_ref[0].astype(jnp.float32)).astype(jnp.float32)
    before = lax.broadcasted_iota(jnp.int32, (cands, cands), 0) < lax.broadcasted_iota(
        jnp.int32, (cands, cands), 1
    )
    place = dot(mine.astype(jnp.bfloat16), before.astype(jnp.float32).astype(jnp.bfloat16))
    wide = value_ref.shape[1]
    pad = jnp.zeros((count, wide - cands), jnp.float32)
    place_ref[...] = jnp.concatenate([jnp.where(mine > 0, place, -1.0), pad - 1.0], axis=1)
    row_high = jnp.floor(row * (1.0 / 16))
    first, second, third = split3(target)
    values = [row_high, row - 16 * row_high, first, second, third]
    for v in range(8):
        value = values[v].astype(jnp.float32) if v < len(values) else jnp.zeros_like(row)
        value_ref[pl.ds(v, count, stride=8), :] = jnp.concatenate([value, pad], axis=1)
    spots = lax.broadcasted_iota(jnp.int32, (wide, wide), 0).astype(jnp.float32)

    def body(step, carry):
        for k in range(8):
            q = step * 8 + k
            hot = jnp.where(place_ref[pl.ds(q, 1), :] == spots, 1.0, 0.0).astype(jnp.bfloat16)
            at = pl.ds(pl.multiple_of(q * 8, 8), 8)
            result_ref[at, :] = dot_last(value_ref[at, :].astype(jnp.bfloat16), hot)
        return carry

    lax.fori_loop(0, count // 8, body, 0)
    result = [result_ref[pl.ds(v, count, stride=8), :] for v in range(5)]
    found = jnp.sum(mine, axis=-1, keepdims=True)
    lane = lax.broadcasted_iota(jnp.int32, (count, wide), 1)
    rows = 16 * result[0] + result[1]
    rows_ref[...] = jnp.where(lane < cands, rows, found).astype(jnp.int32)
    listed = jnp.where(lane.astype(jnp.float32) < found, result[2] + result[3] + result[4], -1.0)
    stacked = jnp.concatenate(split3(listed), axis=0)
    steps = cands // GROUP
    source = lax.broadcasted_iota(jnp.int32, (wide, wide), 0)
    block = lax.broadcasted_iota(jnp.int32, (wide, wide), 1) // (wide // GROUP)
    for t in range(steps):
        pick = jnp.where(source == block + t * GROUP, 1.0, 0.0).astype(jnp.bfloat16)
        spread = dot(stacked, pick)
        target_ref[pl.ds(t, count, stride=steps), :] = (
            spread[:count] + spread[count : 2 * count] + spread[2 * count :]
        )


def prep(me, told, count, shard, cands):
    wide = 128
    return pl.pallas_call(
        functools.partial(prep_kernel, shard=shard, cands=cands),
        in_specs=[
            pl.BlockSpec(memory_space=pltpu.SMEM),
            pl.BlockSpec(memory_space=pltpu.VMEM),
        ],
        out_specs=[pl.BlockSpec(memory_space=pltpu.VMEM)] * 2,
        out_shape=[
            jax.ShapeDtypeStruct((count, wide), jnp.int32),
            jax.ShapeDtypeStruct((count * (cands // GROUP), wide), jnp.float32),
        ],
        scratch_shapes=[
            pltpu.VMEM((count * 8, wide), jnp.float32),
            pltpu.VMEM((count, wide), jnp.float32),
            pltpu.VMEM((count * 8, wide), jnp.float32),
        ],
        compiler_params=pltpu.CompilerParams(vmem_limit_bytes=VMEM_LIMIT),
        cost_estimate=pl.CostEstimate(flops=count * wide, bytes_accessed=count * wide, transcendentals=0),
        name="prep",
    )(me, told)


def pair_kernel(source_ref, rows_ref, target_ref, queries_ref, inverse_ref, index_ref, turned_ref, *refs, cands, sources):
    out_refs = refs[:sources]
    (units_ref, unit_ref, acc_ref, total_ref, left_ref, right_ref, back_ref, raw_ref) = refs[sources:]
    count, tokens, dim = unit_ref.shape
    wide = rows_ref.shape[1]
    per_query = cands // GROUP
    slots = count * per_query
    bits = per_query.bit_length() - 1
    total = jnp.int32(0)
    for q in range(count):
        for t in range(per_query):
            units_ref[total + t] = jnp.int32(q * per_query + t)
        total = total + lax.div(rows_ref[q, cands] + (GROUP - 1), GROUP)
    for t in range(2 * UNITS):
        units_ref[total + t] = jnp.int32(slots)
    steps = lax.div(total + (UNITS - 1), UNITS)

    def entry(number):
        slot = units_ref[number]
        q = jnp.minimum(lax.shift_right_logical(slot, bits), count - 1)
        return slot, q, jnp.bitwise_and(slot, per_query - 1) * GROUP

    for q in range(count):
        unit_ref[q] = rounded_queries(queries_ref[0, q * tokens : (q + 1) * tokens, :])
    acc_ref[...] = jnp.zeros_like(acc_ref)
    ones = jnp.ones((8, wide), jnp.bfloat16)

    def tiles_of(number, ref):
        _, q, base = entry(number)
        return q, [ref[rows_ref[q, base + g]] for g in range(GROUP)]

    def multiply(step):
        found = []
        for u in range(UNITS):
            q, tiles = tiles_of(step * UNITS + u, turned_ref)
            found.append(dot(unit_ref[q], jnp.concatenate(tiles, axis=1)))
        return found

    def forward(step, carry):
        expos, weights, rows = [], [], []
        for u in range(UNITS):
            _, q, base = entry(step * UNITS + u)
            for g in range(GROUP):
                rows.append(rows_ref[q, base + g])
                inverse = inverse_ref[pl.ds(rows[-1], 1), :]
                raw = raw_ref[u, :, g * wide : (g + 1) * wide]
                expo = jnp.exp2(raw * (inverse * (LOG2E / inner_temp)))
                expos.append(expo.astype(jnp.bfloat16))
                weights.append((expo * inverse).astype(jnp.bfloat16))
        following = multiply(step + 1)
        backs = []
        for u in range(UNITS):
            for k in range(u * GROUP, (u + 1) * GROUP, 2):
                part = dot(
                    jnp.concatenate(weights[k : k + 2], axis=0),
                    jnp.concatenate([index_ref[row] for row in rows[k : k + 2]], axis=1),
                )
                backs += [part[:tokens, :dim], part[tokens:, dim:]]
        totals = []
        for u in range(0, UNITS, 2):
            part = dot_last(ones, jnp.concatenate(expos[u * GROUP : (u + 2) * GROUP], axis=0))
            totals += [part[0:1, :wide], part[0:1, wide:]]
        for u in range(UNITS):
            back_ref[step * UNITS + u] = jnp.concatenate(
                backs[u * GROUP : (u + 1) * GROUP], axis=0
            ).astype(jnp.bfloat16)
            total_ref[pl.ds(units_ref[step * UNITS + u], 1), :] = totals[u]
        for u in range(UNITS):
            raw_ref[u] = following[u]
        return carry

    for u, raw in enumerate(multiply(0)):
        raw_ref[u] = raw
    lax.fori_loop(0, steps, forward, 0)

    target = target_ref[...]
    held = target >= 0.0
    totals = jnp.where(held, total_ref[0:slots, :], 1.0)
    target = jnp.where(held, target, 0.0)
    same = lax.broadcasted_iota(jnp.int32, (wide, wide), 0) // tokens == lax.broadcasted_iota(
        jnp.int32, (wide, wide), 1
    ) // tokens
    same = jnp.where(same, 1.0, 0.0).astype(jnp.bfloat16)
    parts = [dot(part, same) for part in split3(jnp.log(totals))]
    score = inner_temp * (parts[0] + parts[1] + parts[2])
    lift = jnp.where(held, jnp.exp(score), 0.0)
    recip = 1.0 / totals
    left_ref[0:slots, :] = lift * recip
    right_ref[0:slots, :] = target * recip
    left_ref[slots:, :] = jnp.zeros_like(left_ref[slots:, :])
    right_ref[slots:, :] = jnp.zeros_like(right_ref[slots:, :])

    def per_source(values):
        rows = jnp.sum(values.reshape(count, per_query, wide), axis=1)
        return jnp.sum(rows, axis=-1, keepdims=True) * (1.0 / tokens)

    lane = lax.broadcasted_iota(jnp.int32, (count, wide), 1)
    sums = jnp.where(lane < wide // 2, per_source(lift), per_source(target * score))
    diagonal = lax.broadcasted_iota(jnp.int32, (tokens, wide), 0) == lax.broadcasted_iota(
        jnp.int32, (tokens, wide), 1
    ) % tokens

    def backward(step, carry):
        owners, sides = [], []
        for u in range(UNITS):
            slot, q, _ = entry(step * UNITS + u)
            left = jnp.where(diagonal, left_ref[pl.ds(slot, 1), :], 0.0)
            right = jnp.where(diagonal, right_ref[pl.ds(slot, 1), :], 0.0)
            both = jnp.concatenate([left, right], axis=0)
            high = both.astype(jnp.bfloat16)
            sides += [high, (both - high.astype(jnp.float32)).astype(jnp.bfloat16)]
            owners.append(q)
        parts = []
        for u in range(0, UNITS, 2):
            pulled = dot(
                jnp.concatenate(sides[2 * u : 2 * u + 4], axis=0),
                jnp.concatenate([back_ref[step * UNITS + u], back_ref[step * UNITS + u + 1]], axis=1),
            )
            height = 2 * tokens
            parts += [
                pulled[:height, :dim] + pulled[height : 2 * height, :dim],
                pulled[2 * height : 3 * height, dim:] + pulled[3 * height :, dim:],
            ]
        for q, part in zip(owners, parts):
            acc_ref[q] += part
        return carry

    lax.fori_loop(0, steps, backward, 0)
    for k, out_ref in enumerate(out_refs):
        @pl.when(pl.program_id(0) == k)
        def _():
            for q in range(count):
                out_ref[pl.ds(q * 2 * tokens, 2 * tokens), :] = acc_ref[q].astype(jnp.bfloat16)
            for j, part in enumerate(split3(sums)):
                out_ref[pl.ds(count * 2 * tokens + j * count, count), :] = part


def pairs(sources, rows, targets, told, count, tokens, inverse, index, turned, cands, room):
    dim = told.shape[2]
    wide = rows.shape[1]
    per_query = cands // GROUP
    slots = count * per_query
    most = (room + (GROUP - 1) * count) // GROUP + UNITS
    height = count * 2 * tokens + 3 * count
    return pl.pallas_call(
        functools.partial(pair_kernel, cands=cands, sources=len(sources)),
        grid_spec=pltpu.PrefetchScalarGridSpec(
            num_scalar_prefetch=1,
            grid=(len(sources),),
            in_specs=[
                pl.BlockSpec((count, wide), lambda i, s: (s[i], 0), memory_space=pltpu.SMEM),
                pl.BlockSpec((slots, wide), lambda i, s: (s[i], 0)),
                pl.BlockSpec((1,) + told.shape[1:], lambda i, s: (s[i], 0, 0)),
                pl.BlockSpec(memory_space=pltpu.VMEM),
                pl.BlockSpec(memory_space=pltpu.VMEM),
                pl.BlockSpec(memory_space=pltpu.VMEM),
            ],
            out_specs=[pl.BlockSpec((height, dim), lambda i, s: (0, 0))] * len(sources),
            scratch_shapes=[
                pltpu.SMEM((slots + per_query + 2 * UNITS,), jnp.int32),
                pltpu.VMEM((count, tokens, dim), jnp.bfloat16),
                pltpu.VMEM((count, 2 * tokens, dim), jnp.float32),
                pltpu.VMEM((slots + 8, wide), jnp.float32),
                pltpu.VMEM((slots + 8, wide), jnp.float32),
                pltpu.VMEM((slots + 8, wide), jnp.float32),
                pltpu.VMEM((most, GROUP * tokens, dim), jnp.bfloat16),
                pltpu.VMEM((UNITS, tokens, GROUP * wide), jnp.float32),
            ],
        ),
        out_shape=[jax.ShapeDtypeStruct((height, dim), jnp.bfloat16)] * len(sources),
        compiler_params=pltpu.CompilerParams(vmem_limit_bytes=VMEM_LIMIT),
        cost_estimate=pl.CostEstimate(
            flops=6 * len(sources) * room * tokens * wide * dim,
            bytes_accessed=2 * len(sources) * room * wide * dim,
            transcendentals=len(sources) * room * tokens * wide,
        ),
        name="pairs",
    )(jnp.stack(sources), rows, targets, told, inverse, index, turned)


def neg_kernel(rows_ref, queries_ref, shard_ref, acc_ref, sums_ref,
               unit_ref, expo_ref, total_ref, left_ref, back_ref, raw_ref, tiles_ref, turned_ref, sems,
               *, tokens):
    total = rows_ref.shape[0]
    chunk = expo_ref.shape[0]
    height, dim = queries_ref.shape
    wide = shard_ref.shape[1]
    lanes = 128
    half = min(height, 256)
    def fetch(number):
        place = jnp.bitwise_and(number, 1)
        for k in range(chunk):
            pltpu.make_async_copy(
                shard_ref.at[rows_ref[number * chunk + k]], tiles_ref.at[place, k], sems.at[place]
            ).start()

    fetch(jnp.int32(0))
    for c in range(height // lanes):
        part = slice(c * lanes, (c + 1) * lanes)
        unit_ref[:, part] = rounded_queries(queries_ref[part]).T
    back_ref[...] = jnp.zeros_like(back_ref)
    sums_ref[...] = jnp.zeros_like(sums_ref)

    same = lax.broadcasted_iota(jnp.int32, (lanes, lanes), 0) // tokens == lax.broadcasted_iota(
        jnp.int32, (lanes, lanes), 1
    ) // tokens
    same = jnp.where(same, 1.0, 0.0).astype(jnp.bfloat16)

    def block(number, carry):
        @pl.when(number + 1 < total // chunk)
        def _():
            fetch(number + 1)

        place = jnp.bitwise_and(number, 1)
        pltpu.make_async_copy(shard_ref.at[pl.ds(0, chunk)], tiles_ref.at[place], sems.at[place]).wait()

        def tiles_of(step):
            first = jnp.minimum(step, chunk // NEG_STEP - 1) * NEG_STEP
            return tiles_ref[place, pl.ds(first, NEG_STEP)].reshape(NEG_STEP * wide, dim)

        def forward(step, carry):
            first = step * NEG_STEP
            tiles = tiles_of(step)
            broad = tiles.astype(jnp.float32)
            inverse = lax.rsqrt(jnp.sum(broad * broad, axis=-1, keepdims=True) + epsilon)
            expo = jnp.exp2(raw_ref[...] * (inverse * (LOG2E / inner_temp)))
            following = dot(tiles_of(step + 1), unit_ref[...])
            for g in range(NEG_STEP):
                part = slice(g * wide, (g + 1) * wide)
                turned_ref[first + g] = tiles[part].T
                expo_ref[first + g] = (expo[part] * inverse[part]).astype(jnp.bfloat16)
                total_ref[pl.ds(first + g, 1), :] = jnp.sum(expo[part], axis=0, keepdims=True)
            raw_ref[...] = following
            return carry

        raw_ref[...] = dot(tiles_of(0), unit_ref[...])
        lax.fori_loop(0, chunk // NEG_STEP, forward, 0)
        for c in range(height // lanes):
            part = slice(c * lanes, (c + 1) * lanes)
            totals = total_ref[:, part]
            pieces = [dot(piece, same) for piece in split3(jnp.log(totals))]
            lift = jnp.exp(inner_temp * (pieces[0] + pieces[1] + pieces[2]))
            left_ref[:, part] = lift / totals
            sums_ref[:, part] += jnp.broadcast_to(jnp.sum(lift, axis=0, keepdims=True), (8, lanes))
        for c in range(height // half):
            part = slice(c * half, (c + 1) * half)

            def backward(step, acc):
                for g in range(NEG_STEP):
                    k = step * NEG_STEP + g
                    acc = acc + dot(turned_ref[k], expo_ref[k, :, part]) * left_ref[pl.ds(k, 1), part]
                return acc

            back_ref[:, part] = lax.fori_loop(0, chunk // NEG_STEP, backward, back_ref[:, part])
        return carry

    lax.fori_loop(0, total // chunk, block, 0)
    for c in range(height // lanes):
        part = slice(c * lanes, (c + 1) * lanes)
        acc_ref[part, :] = back_ref[:, part].T


def negatives(rows, queries, index):
    total = rows.shape[0]
    count, tokens, dim = queries.shape
    wide = index.shape[1]
    height = count * tokens
    chunk = math.gcd(total, NEG_CHUNK)
    return pl.pallas_call(
        functools.partial(neg_kernel, tokens=tokens),
        in_specs=[
            pl.BlockSpec(memory_space=pltpu.SMEM),
            pl.BlockSpec(memory_space=pltpu.VMEM),
            pl.BlockSpec(memory_space=pltpu.HBM),
        ],
        out_specs=[pl.BlockSpec(memory_space=pltpu.VMEM)] * 2,
        out_shape=[
            jax.ShapeDtypeStruct((height, dim), jnp.float32),
            jax.ShapeDtypeStruct((8, height), jnp.float32),
        ],
        scratch_shapes=[
            pltpu.VMEM((dim, height), jnp.bfloat16),
            pltpu.VMEM((chunk, wide, height), jnp.bfloat16),
            pltpu.VMEM((chunk, height), jnp.float32),
            pltpu.VMEM((chunk, height), jnp.float32),
            pltpu.VMEM((dim, height), jnp.float32),
            pltpu.VMEM((NEG_STEP * wide, height), jnp.float32),
            pltpu.VMEM((2, chunk, wide, dim), jnp.bfloat16),
            pltpu.VMEM((chunk, dim, wide), jnp.bfloat16),
            pltpu.SemaphoreType.DMA((2,)),
        ],
        compiler_params=pltpu.CompilerParams(vmem_limit_bytes=3 * VMEM_LIMIT),
        cost_estimate=pl.CostEstimate(
            flops=4 * total * height * wide * dim,
            bytes_accessed=2 * total * wide * dim,
            transcendentals=total * height * wide,
        ),
        name="negatives",
    )(rows, queries.reshape(height, dim), pltpu.with_memory_space_constraint(index, pltpu.HBM))


def finish_kernel(queries_ref, teacher_ref, back_ref, sums_ref, *refs, owners):
    messages, (loss_ref, grad_ref) = refs[:owners], refs[owners:]
    count, tokens, dim = grad_ref.shape
    cut = count * 2 * tokens
    scores = jnp.zeros((count, dim), jnp.float32)
    for message in messages:
        for k in range(3):
            scores = scores + message[cut + k * count : cut + (k + 1) * count, :].astype(jnp.float32)
    totals = []
    for q in range(count):
        total = scores[q : q + 1, 0:1] + sums_ref[0:1, q * tokens : q * tokens + 1]
        totals.append(total)
        pulled = back_ref[q * tokens : (q + 1) * tokens, :]
        right = jnp.zeros((tokens, dim), jnp.float32)
        for message in messages:
            pulled = pulled + message[q * 2 * tokens : (q * 2 + 1) * tokens, :].astype(jnp.float32)
            right = right + message[(q * 2 + 1) * tokens : (q + 1) * 2 * tokens, :].astype(jnp.float32)
        pulled = pulled / total - right
        wide = queries_ref[q].astype(jnp.float32)
        radius = jnp.sqrt(jnp.sum(wide * wide, axis=-1, keepdims=True) + epsilon)
        unit = wide / radius
        grad_ref[q] = (pulled - unit * jnp.sum(unit * pulled, axis=-1, keepdims=True)) / radius
    spread = jnp.log(jnp.concatenate(totals, axis=0))
    teacher = teacher_ref[...]
    log_target = teacher - jnp.log(jnp.sum(jnp.exp(teacher), axis=-1, keepdims=True))
    gain = jnp.sum(jnp.exp(log_target) * (log_target + spread), axis=-1, keepdims=True)
    loss_ref[...] = gain - scores[:, dim // 2 : dim // 2 + 1] + jnp.zeros_like(loss_ref)


def finish(queries, teacher, back, sums, messages):
    count, tokens, dim = queries.shape
    owners = len(messages)
    return pl.pallas_call(
        functools.partial(finish_kernel, owners=owners),
        in_specs=[pl.BlockSpec(memory_space=pltpu.VMEM)] * (4 + owners),
        out_specs=[pl.BlockSpec(memory_space=pltpu.VMEM)] * 2,
        out_shape=[
            jax.ShapeDtypeStruct((count, dim), jnp.float32),
            jax.ShapeDtypeStruct((count, tokens, dim), jnp.float32),
        ],
        compiler_params=pltpu.CompilerParams(vmem_limit_bytes=VMEM_LIMIT),
        name="finish",
    )(queries, teacher, back, sums, *messages)


def on_device(queries, index, cand_owner, cand_row, neg_row, teacher):
    count, tokens, dim = queries.shape
    cands = cand_row.shape[1]
    shard = index.shape[0]
    owners = lax.axis_size("corpus")
    room = (2 * count * cands + owners - 1) // owners
    me = lax.axis_index("corpus").astype(jnp.int32)
    group = lax.axis_size("blk")

    def from_step(value, axis, size, step):
        return lax.ppermute(value, axis, [((i + step) % size, i) for i in range(size)])

    def gathered(value, axis, size):
        return [value] + [from_step(value, axis, size, step) for step in range(1, size)]

    code = cand_owner[..., 0] * shard + cand_row
    high = lax.reduce_precision(teacher, 8, 7)
    mid = lax.reduce_precision(teacher - high, 8, 7)
    low = lax.reduce_precision(teacher - high - mid, 8, 7)
    meta = [code // CODE, code % CODE, high, mid, low, jnp.zeros_like(low)]
    meta = [value.astype(jnp.bfloat16) for value in meta]
    meta = [jnp.concatenate(meta[k : k + 2], axis=1) for k in range(0, 6, 2)]
    message = jnp.concatenate([queries.reshape(count * tokens, dim)] + meta, axis=0)
    all_neg = jnp.concatenate(gathered(neg_row, "blk", group), axis=0).reshape(-1)
    told = jnp.broadcast_to(message[None], (owners,) + message.shape)
    told = lax.all_to_all(told, "corpus", split_axis=0, concat_axis=0, tiled=True)
    neg_acc, neg_sum = negatives(all_neg, queries, index)
    told, neg_acc = lax.optimization_barrier((told, neg_acc))
    rows, targets = prep(me.reshape(1), told, owners * count, shard, cands)
    index, told, rows = lax.optimization_barrier((index, told, rows))
    index, turned, inverse = load(index)
    messages = []
    order = list(range(1, owners)) + [0]
    groups = [order[first : first + SOURCES] for first in range(0, owners, SOURCES)]
    for steps in groups:
        sources = [lax.rem(me + step, owners) for step in steps]
        found = pairs(
            sources, rows, targets, told, count, tokens, inverse, index, turned, cands, room
        )
        for step, message in zip(steps, found):
            if step:
                message = lax.ppermute(
                    message, "corpus", [(i, (i + step) % owners) for i in range(owners)]
                )
            messages.append(message)
    losses, query_grads = finish(queries, teacher, neg_acc, neg_sum, messages)
    return (losses[:, 0], query_grads)


def solution(mesh):
    placed = (
        P(("corpus", "blk"), None, None),
        P("corpus", None, None),
        P(("corpus", "blk"), None, None),
        P(("corpus", "blk"), None),
        P(("corpus", "blk"), None),
        P(("corpus", "blk"), None),
    )
    return jax.shard_map(
        on_device,
        mesh=mesh,
        in_specs=placed,
        out_specs=(P(("corpus", "blk")), P(("corpus", "blk"), None, None)),
        check_vma=False,
    )
```

```python
import functools
import math

import jax
import jax.numpy as jnp
from jax import lax
from jax.experimental import pallas as pl
from jax.experimental.pallas import tpu as pltpu
from jax.sharding import PartitionSpec as P

inner_temp = 0.1
epsilon = 1e-06
LOG2E = 1.4426950408889634
GROUP = 4
UNITS = 12
LOADS = 8
LOAD_STEP = 16
NEG_STEP = 8
NEG_CHUNK = 24
SOURCES = 2
CODE = 64
VMEM_LIMIT = 8 * 1024 * 1024
LAST = (((1,), (1,)), ((), ()))


def dot_last(a, b):
    return lax.dot_general(a, b, LAST, preferred_element_type=jnp.float32)


def dot(a, b):
    return jnp.dot(a, b, preferred_element_type=jnp.float32)


def split3(x):
    high = x.astype(jnp.bfloat16)
    rest = x - high.astype(jnp.float32)
    mid = rest.astype(jnp.bfloat16)
    low = (rest - mid.astype(jnp.float32)).astype(jnp.bfloat16)
    return high, mid, low


def rounded_queries(raw):
    wide = raw.astype(jnp.float32)
    radius = jnp.sqrt(jnp.sum(wide * wide, axis=-1, keepdims=True) + epsilon)
    return (wide / radius).astype(jnp.bfloat16)


def load_shard(index_ref, tiles_ref, turned_ref, inverse_ref, sems):
    count = index_ref.shape[0]
    chunk = count // LOADS

    def copy(part):
        at = pl.ds(part * chunk, chunk)
        return pltpu.make_async_copy(index_ref.at[at], tiles_ref.at[at], sems.at[part])

    for part in range(LOADS):
        copy(part).start()

    for part in range(LOADS):
        copy(part).wait()

        def body(step, carry):
            first = part * chunk + step * LOAD_STEP
            squares = []
            turned = []
            for k in range(LOAD_STEP):
                tile = tiles_ref[first + k].T
                turned.append(tile)
                wide = tile.astype(jnp.float32)
                squares.append(jnp.sum(wide * wide, axis=0, keepdims=True))
            for k in range(LOAD_STEP):
                turned_ref[first + k] = turned[k]
            at = pl.ds(pl.multiple_of(first, LOAD_STEP), LOAD_STEP)
            inverse_ref[at, :] = lax.rsqrt(jnp.concatenate(squares, axis=0) + epsilon)
            return carry

        lax.fori_loop(0, chunk // LOAD_STEP, body, 0)


def load(index):
    count, tokens, dim = index.shape
    return pl.pallas_call(
        load_shard,
        in_specs=[pl.BlockSpec(memory_space=pltpu.HBM)],
        out_specs=[pl.BlockSpec(memory_space=pltpu.VMEM)] * 3,
        out_shape=[
            pltpu.VMEM((count, tokens, dim), jnp.bfloat16),
            pltpu.VMEM((count, dim, tokens), jnp.bfloat16),
            pltpu.VMEM((count, tokens), jnp.float32),
        ],
        scratch_shapes=[pltpu.SemaphoreType.DMA((LOADS,))],
        compiler_params=pltpu.CompilerParams(vmem_limit_bytes=VMEM_LIMIT),
        cost_estimate=pl.CostEstimate(
            flops=2 * count * tokens * dim,
            bytes_accessed=2 * count * tokens * dim,
            transcendentals=count * tokens,
        ),
        name="load",
    )(pltpu.with_memory_space_constraint(index, pltpu.HBM))


def prep_kernel(me_ref, told_ref, rows_ref, target_ref, value_ref, place_ref, result_ref, *, shard, cands):
    sources, height = told_ref.shape[:2]
    each = rows_ref.shape[0] // sources
    count = rows_ref.shape[0]
    base = height - 3 * each

    def part(k):
        rows = [told_ref[s, base + k * each : base + (k + 1) * each, :] for s in range(sources)]
        return jnp.concatenate(rows, axis=0).astype(jnp.float32)

    codes, upper, lower = part(0), part(1), part(2)
    code = CODE * codes[:, :cands] + codes[:, cands:]
    owner = jnp.floor((code + 0.5) * (1.0 / shard))
    row = code - owner * shard
    teacher = upper[:, :cands] + upper[:, cands:] + lower[:, :cands]
    log_target = teacher - jnp.log(jnp.sum(jnp.exp(teacher), axis=-1, keepdims=True))
    target = jnp.exp(log_target)
    mine = (owner == me_ref[0].astype(jnp.float32)).astype(jnp.float32)
    before = lax.broadcasted_iota(jnp.int32, (cands, cands), 0) < lax.broadcasted_iota(
        jnp.int32, (cands, cands), 1
    )
    place = dot(mine.astype(jnp.bfloat16), before.astype(jnp.float32).astype(jnp.bfloat16))
    wide = value_ref.shape[1]
    pad = jnp.zeros((count, wide - cands), jnp.float32)
    place_ref[...] = jnp.concatenate([jnp.where(mine > 0, place, -1.0), pad - 1.0], axis=1)
    row_high = jnp.floor(row * (1.0 / 16))
    first, second, third = split3(target)
    values = [row_high, row - 16 * row_high, first, second, third]
    for v in range(8):
        value = values[v].astype(jnp.float32) if v < len(values) else jnp.zeros_like(row)
        value_ref[pl.ds(v, count, stride=8), :] = jnp.concatenate([value, pad], axis=1)
    spots = lax.broadcasted_iota(jnp.int32, (wide, wide), 0).astype(jnp.float32)

    def body(step, carry):
        for k in range(8):
            q = step * 8 + k
            hot = jnp.where(place_ref[pl.ds(q, 1), :] == spots, 1.0, 0.0).astype(jnp.bfloat16)
            at = pl.ds(pl.multiple_of(q * 8, 8), 8)
            result_ref[at, :] = dot_last(value_ref[at, :].astype(jnp.bfloat16), hot)
        return carry

    lax.fori_loop(0, count // 8, body, 0)
    result = [result_ref[pl.ds(v, count, stride=8), :] for v in range(5)]
    found = jnp.sum(mine, axis=-1, keepdims=True)
    lane = lax.broadcasted_iota(jnp.int32, (count, wide), 1)
    rows = 16 * result[0] + result[1]
    rows_ref[...] = jnp.where(lane < cands, rows, found).astype(jnp.int32)
    listed = jnp.where(lane.astype(jnp.float32) < found, result[2] + result[3] + result[4], -1.0)
    stacked = jnp.concatenate(split3(listed), axis=0)
    steps = cands // GROUP
    source = lax.broadcasted_iota(jnp.int32, (wide, wide), 0)
    block = lax.broadcasted_iota(jnp.int32, (wide, wide), 1) // (wide // GROUP)
    for t in range(steps):
        pick = jnp.where(source == block + t * GROUP, 1.0, 0.0).astype(jnp.bfloat16)
        spread = dot(stacked, pick)
        target_ref[pl.ds(t, count, stride=steps), :] = (
            spread[:count] + spread[count : 2 * count] + spread[2 * count :]
        )


def prep(me, told, count, shard, cands):
    wide = 128
    return pl.pallas_call(
        functools.partial(prep_kernel, shard=shard, cands=cands),
        in_specs=[
            pl.BlockSpec(memory_space=pltpu.SMEM),
            pl.BlockSpec(memory_space=pltpu.VMEM),
        ],
        out_specs=[pl.BlockSpec(memory_space=pltpu.VMEM)] * 2,
        out_shape=[
            jax.ShapeDtypeStruct((count, wide), jnp.int32),
            jax.ShapeDtypeStruct((count * (cands // GROUP), wide), jnp.float32),
        ],
        scratch_shapes=[
            pltpu.VMEM((count * 8, wide), jnp.float32),
            pltpu.VMEM((count, wide), jnp.float32),
            pltpu.VMEM((count * 8, wide), jnp.float32),
        ],
        compiler_params=pltpu.CompilerParams(vmem_limit_bytes=VMEM_LIMIT),
        cost_estimate=pl.CostEstimate(flops=count * wide, bytes_accessed=count * wide, transcendentals=0),
        name="prep",
    )(me, told)


def pair_kernel(source_ref, rows_ref, target_ref, queries_ref, inverse_ref, index_ref, turned_ref, *refs, cands, sources):
    out_refs = refs[:sources]
    (units_ref, unit_ref, acc_ref, total_ref, left_ref, right_ref, back_ref, raw_ref) = refs[sources:]
    count, tokens, dim = unit_ref.shape
    wide = rows_ref.shape[1]
    per_query = cands // GROUP
    slots = count * per_query
    bits = per_query.bit_length() - 1
    total = jnp.int32(0)
    for q in range(count):
        for t in range(per_query):
            units_ref[total + t] = jnp.int32(q * per_query + t)
        total = total + lax.div(rows_ref[q, cands] + (GROUP - 1), GROUP)
    for t in range(2 * UNITS):
        units_ref[total + t] = jnp.int32(slots)
    steps = lax.div(total + (UNITS - 1), UNITS)

    def entry(number):
        slot = units_ref[number]
        q = jnp.minimum(lax.shift_right_logical(slot, bits), count - 1)
        return slot, q, jnp.bitwise_and(slot, per_query - 1) * GROUP

    for q in range(count):
        unit_ref[q] = rounded_queries(queries_ref[0, q * tokens : (q + 1) * tokens, :])
    acc_ref[...] = jnp.zeros_like(acc_ref)
    ones = jnp.ones((8, wide), jnp.bfloat16)

    def tiles_of(number, ref):
        _, q, base = entry(number)
        return q, [ref[rows_ref[q, base + g]] for g in range(GROUP)]

    def multiply(step):
        found = []
        for u in range(UNITS):
            q, tiles = tiles_of(step * UNITS + u, turned_ref)
            found.append(dot(unit_ref[q], jnp.concatenate(tiles, axis=1)))
        return found

    def forward(step, carry):
        expos, weights, rows = [], [], []
        for u in range(UNITS):
            _, q, base = entry(step * UNITS + u)
            for g in range(GROUP):
                rows.append(rows_ref[q, base + g])
                inverse = inverse_ref[pl.ds(rows[-1], 1), :]
                raw = raw_ref[u, :, g * wide : (g + 1) * wide]
                expo = jnp.exp2(raw * (inverse * (LOG2E / inner_temp)))
                expos.append(expo.astype(jnp.bfloat16))
                weights.append((expo * inverse).astype(jnp.bfloat16))
        following = multiply(step + 1)
        backs = []
        for u in range(UNITS):
            for k in range(u * GROUP, (u + 1) * GROUP, 2):
                part = dot(
                    jnp.concatenate(weights[k : k + 2], axis=0),
                    jnp.concatenate([index_ref[row] for row in rows[k : k + 2]], axis=1),
                )
                backs += [part[:tokens, :dim], part[tokens:, dim:]]
        totals = []
        for u in range(0, UNITS, 2):
            part = dot_last(ones, jnp.concatenate(expos[u * GROUP : (u + 2) * GROUP], axis=0))
            totals += [part[0:1, :wide], part[0:1, wide:]]
        for u in range(UNITS):
            back_ref[step * UNITS + u] = jnp.concatenate(
                backs[u * GROUP : (u + 1) * GROUP], axis=0
            ).astype(jnp.bfloat16)
            total_ref[pl.ds(units_ref[step * UNITS + u], 1), :] = totals[u]
        for u in range(UNITS):
            raw_ref[u] = following[u]
        return carry

    for u, raw in enumerate(multiply(0)):
        raw_ref[u] = raw
    lax.fori_loop(0, steps, forward, 0)

    target = target_ref[...]
    held = target >= 0.0
    totals = jnp.where(held, total_ref[0:slots, :], 1.0)
    target = jnp.where(held, target, 0.0)
    same = lax.broadcasted_iota(jnp.int32, (wide, wide), 0) // tokens == lax.broadcasted_iota(
        jnp.int32, (wide, wide), 1
    ) // tokens
    same = jnp.where(same, 1.0, 0.0).astype(jnp.bfloat16)
    parts = [dot(part, same) for part in split3(jnp.log(totals))]
    score = inner_temp * (parts[0] + parts[1] + parts[2])
    lift = jnp.where(held, jnp.exp(score), 0.0)
    recip = 1.0 / totals
    left_ref[0:slots, :] = lift * recip
    right_ref[0:slots, :] = target * recip
    left_ref[slots:, :] = jnp.zeros_like(left_ref[slots:, :])
    right_ref[slots:, :] = jnp.zeros_like(right_ref[slots:, :])

    def per_source(values):
        rows = jnp.sum(values.reshape(count, per_query, wide), axis=1)
        return jnp.sum(rows, axis=-1, keepdims=True) * (1.0 / tokens)

    lane = lax.broadcasted_iota(jnp.int32, (count, wide), 1)
    sums = jnp.where(lane < wide // 2, per_source(lift), per_source(target * score))
    diagonal = lax.broadcasted_iota(jnp.int32, (tokens, wide), 0) == lax.broadcasted_iota(
        jnp.int32, (tokens, wide), 1
    ) % tokens

    def backward(step, carry):
        owners, sides = [], []
        for u in range(UNITS):
            slot, q, _ = entry(step * UNITS + u)
            left = jnp.where(diagonal, left_ref[pl.ds(slot, 1), :], 0.0)
            right = jnp.where(diagonal, right_ref[pl.ds(slot, 1), :], 0.0)
            both = jnp.concatenate([left, right], axis=0)
            high = both.astype(jnp.bfloat16)
            sides += [high, (both - high.astype(jnp.float32)).astype(jnp.bfloat16)]
            owners.append(q)
        parts = []
        for u in range(0, UNITS, 2):
            pulled = dot(
                jnp.concatenate(sides[2 * u : 2 * u + 4], axis=0),
                jnp.concatenate([back_ref[step * UNITS + u], back_ref[step * UNITS + u + 1]], axis=1),
            )
            height = 2 * tokens
            parts += [
                pulled[:height, :dim] + pulled[height : 2 * height, :dim],
                pulled[2 * height : 3 * height, dim:] + pulled[3 * height :, dim:],
            ]
        for q, part in zip(owners, parts):
            acc_ref[q] += part
        return carry

    lax.fori_loop(0, steps, backward, 0)
    for k, out_ref in enumerate(out_refs):
        @pl.when(pl.program_id(0) == k)
        def _():
            for q in range(count):
                out_ref[pl.ds(q * 2 * tokens, 2 * tokens), :] = acc_ref[q].astype(jnp.bfloat16)
            for j, part in enumerate(split3(sums)):
                out_ref[pl.ds(count * 2 * tokens + j * count, count), :] = part


def pairs(sources, rows, targets, told, count, tokens, inverse, index, turned, cands, room):
    dim = told.shape[2]
    wide = rows.shape[1]
    per_query = cands // GROUP
    slots = count * per_query
    most = (room + (GROUP - 1) * count) // GROUP + UNITS
    height = count * 2 * tokens + 3 * count
    return pl.pallas_call(
        functools.partial(pair_kernel, cands=cands, sources=len(sources)),
        grid_spec=pltpu.PrefetchScalarGridSpec(
            num_scalar_prefetch=1,
            grid=(len(sources),),
            in_specs=[
                pl.BlockSpec((count, wide), lambda i, s: (s[i], 0), memory_space=pltpu.SMEM),
                pl.BlockSpec((slots, wide), lambda i, s: (s[i], 0)),
                pl.BlockSpec((1,) + told.shape[1:], lambda i, s: (s[i], 0, 0)),
                pl.BlockSpec(memory_space=pltpu.VMEM),
                pl.BlockSpec(memory_space=pltpu.VMEM),
                pl.BlockSpec(memory_space=pltpu.VMEM),
            ],
            out_specs=[pl.BlockSpec((height, dim), lambda i, s: (0, 0))] * len(sources),
            scratch_shapes=[
                pltpu.SMEM((slots + per_query + 2 * UNITS,), jnp.int32),
                pltpu.VMEM((count, tokens, dim), jnp.bfloat16),
                pltpu.VMEM((count, 2 * tokens, dim), jnp.float32),
                pltpu.VMEM((slots + 8, wide), jnp.float32),
                pltpu.VMEM((slots + 8, wide), jnp.float32),
                pltpu.VMEM((slots + 8, wide), jnp.float32),
                pltpu.VMEM((most, GROUP * tokens, dim), jnp.bfloat16),
                pltpu.VMEM((UNITS, tokens, GROUP * wide), jnp.float32),
            ],
        ),
        out_shape=[jax.ShapeDtypeStruct((height, dim), jnp.bfloat16)] * len(sources),
        compiler_params=pltpu.CompilerParams(vmem_limit_bytes=VMEM_LIMIT),
        cost_estimate=pl.CostEstimate(
            flops=6 * len(sources) * room * tokens * wide * dim,
            bytes_accessed=2 * len(sources) * room * wide * dim,
            transcendentals=len(sources) * room * tokens * wide,
        ),
        name="pairs",
    )(jnp.stack(sources), rows, targets, told, inverse, index, turned)


def neg_kernel(rows_ref, queries_ref, shard_ref, acc_ref, sums_ref,
               unit_ref, expo_ref, total_ref, left_ref, back_ref, raw_ref, tiles_ref, turned_ref, sems,
               *, tokens):
    total = rows_ref.shape[0]
    chunk = expo_ref.shape[0]
    height, dim = queries_ref.shape
    wide = shard_ref.shape[1]
    lanes = 128
    half = min(height, 256)
    def fetch(number):
        place = jnp.bitwise_and(number, 1)
        for k in range(chunk):
            pltpu.make_async_copy(
                shard_ref.at[rows_ref[number * chunk + k]], tiles_ref.at[place, k], sems.at[place]
            ).start()

    fetch(jnp.int32(0))
    for c in range(height // lanes):
        part = slice(c * lanes, (c + 1) * lanes)
        unit_ref[:, part] = rounded_queries(queries_ref[part]).T
    back_ref[...] = jnp.zeros_like(back_ref)
    sums_ref[...] = jnp.zeros_like(sums_ref)

    same = lax.broadcasted_iota(jnp.int32, (lanes, lanes), 0) // tokens == lax.broadcasted_iota(
        jnp.int32, (lanes, lanes), 1
    ) // tokens
    same = jnp.where(same, 1.0, 0.0).astype(jnp.bfloat16)

    def block(number, carry):
        @pl.when(number + 1 < total // chunk)
        def _():
            fetch(number + 1)

        place = jnp.bitwise_and(number, 1)
        pltpu.make_async_copy(shard_ref.at[pl.ds(0, chunk)], tiles_ref.at[place], sems.at[place]).wait()

        def tiles_of(step):
            first = jnp.minimum(step, chunk // NEG_STEP - 1) * NEG_STEP
            return tiles_ref[place, pl.ds(first, NEG_STEP)].reshape(NEG_STEP * wide, dim)

        def forward(step, carry):
            first = step * NEG_STEP
            tiles = tiles_of(step)
            broad = tiles.astype(jnp.float32)
            inverse = lax.rsqrt(jnp.sum(broad * broad, axis=-1, keepdims=True) + epsilon)
            expo = jnp.exp2(raw_ref[...] * (inverse * (LOG2E / inner_temp)))
            following = dot(tiles_of(step + 1), unit_ref[...])
            for g in range(NEG_STEP):
                part = slice(g * wide, (g + 1) * wide)
                turned_ref[first + g] = tiles[part].T
                expo_ref[first + g] = (expo[part] * inverse[part]).astype(jnp.bfloat16)
                total_ref[pl.ds(first + g, 1), :] = jnp.sum(expo[part], axis=0, keepdims=True)
            raw_ref[...] = following
            return carry

        raw_ref[...] = dot(tiles_of(0), unit_ref[...])
        lax.fori_loop(0, chunk // NEG_STEP, forward, 0)
        for c in range(height // lanes):
            part = slice(c * lanes, (c + 1) * lanes)
            totals = total_ref[:, part]
            pieces = [dot(piece, same) for piece in split3(jnp.log(totals))]
            lift = jnp.exp(inner_temp * (pieces[0] + pieces[1] + pieces[2]))
            left_ref[:, part] = lift / totals
            sums_ref[:, part] += jnp.broadcast_to(jnp.sum(lift, axis=0, keepdims=True), (8, lanes))
        for c in range(height // half):
            part = slice(c * half, (c + 1) * half)

            def backward(step, acc):
                for g in range(NEG_STEP):
                    k = step * NEG_STEP + g
                    acc = acc + dot(turned_ref[k], expo_ref[k, :, part]) * left_ref[pl.ds(k, 1), part]
                return acc

            back_ref[:, part] = lax.fori_loop(0, chunk // NEG_STEP, backward, back_ref[:, part])
        return carry

    lax.fori_loop(0, total // chunk, block, 0)
    for c in range(height // lanes):
        part = slice(c * lanes, (c + 1) * lanes)
        acc_ref[part, :] = back_ref[:, part].T


def negatives(rows, queries, index):
    total = rows.shape[0]
    count, tokens, dim = queries.shape
    wide = index.shape[1]
    height = count * tokens
    chunk = math.gcd(total, NEG_CHUNK)
    return pl.pallas_call(
        functools.partial(neg_kernel, tokens=tokens),
        in_specs=[
            pl.BlockSpec(memory_space=pltpu.SMEM),
            pl.BlockSpec(memory_space=pltpu.VMEM),
            pl.BlockSpec(memory_space=pltpu.HBM),
        ],
        out_specs=[pl.BlockSpec(memory_space=pltpu.VMEM)] * 2,
        out_shape=[
            jax.ShapeDtypeStruct((height, dim), jnp.float32),
            jax.ShapeDtypeStruct((8, height), jnp.float32),
        ],
        scratch_shapes=[
            pltpu.VMEM((dim, height), jnp.bfloat16),
            pltpu.VMEM((chunk, wide, height), jnp.bfloat16),
            pltpu.VMEM((chunk, height), jnp.float32),
            pltpu.VMEM((chunk, height), jnp.float32),
            pltpu.VMEM((dim, height), jnp.float32),
            pltpu.VMEM((NEG_STEP * wide, height), jnp.float32),
            pltpu.VMEM((2, chunk, wide, dim), jnp.bfloat16),
            pltpu.VMEM((chunk, dim, wide), jnp.bfloat16),
            pltpu.SemaphoreType.DMA((2,)),
        ],
        compiler_params=pltpu.CompilerParams(vmem_limit_bytes=3 * VMEM_LIMIT),
        cost_estimate=pl.CostEstimate(
            flops=4 * total * height * wide * dim,
            bytes_accessed=2 * total * wide * dim,
            transcendentals=total * height * wide,
        ),
        name="negatives",
    )(rows, queries.reshape(height, dim), pltpu.with_memory_space_constraint(index, pltpu.HBM))


def finish_kernel(queries_ref, teacher_ref, back_ref, sums_ref, *refs, owners):
    messages, (loss_ref, grad_ref) = refs[:owners], refs[owners:]
    count, tokens, dim = grad_ref.shape
    cut = count * 2 * tokens
    scores = jnp.zeros((count, dim), jnp.float32)
    for message in messages:
        for k in range(3):
            scores = scores + message[cut + k * count : cut + (k + 1) * count, :].astype(jnp.float32)
    totals = []
    for q in range(count):
        total = scores[q : q + 1, 0:1] + sums_ref[0:1, q * tokens : q * tokens + 1]
        totals.append(total)
        pulled = back_ref[q * tokens : (q + 1) * tokens, :]
        right = jnp.zeros((tokens, dim), jnp.float32)
        for message in messages:
            pulled = pulled + message[q * 2 * tokens : (q * 2 + 1) * tokens, :].astype(jnp.float32)
            right = right + message[(q * 2 + 1) * tokens : (q + 1) * 2 * tokens, :].astype(jnp.float32)
        pulled = pulled / total - right
        wide = queries_ref[q].astype(jnp.float32)
        radius = jnp.sqrt(jnp.sum(wide * wide, axis=-1, keepdims=True) + epsilon)
        unit = wide / radius
        grad_ref[q] = (pulled - unit * jnp.sum(unit * pulled, axis=-1, keepdims=True)) / radius
    spread = jnp.log(jnp.concatenate(totals, axis=0))
    teacher = teacher_ref[...]
    log_target = teacher - jnp.log(jnp.sum(jnp.exp(teacher), axis=-1, keepdims=True))
    gain = jnp.sum(jnp.exp(log_target) * (log_target + spread), axis=-1, keepdims=True)
    loss_ref[...] = gain - scores[:, dim // 2 : dim // 2 + 1] + jnp.zeros_like(loss_ref)


def finish(queries, teacher, back, sums, messages):
    count, tokens, dim = queries.shape
    owners = len(messages)
    return pl.pallas_call(
        functools.partial(finish_kernel, owners=owners),
        in_specs=[pl.BlockSpec(memory_space=pltpu.VMEM)] * (4 + owners),
        out_specs=[pl.BlockSpec(memory_space=pltpu.VMEM)] * 2,
        out_shape=[
            jax.ShapeDtypeStruct((count, dim), jnp.float32),
            jax.ShapeDtypeStruct((count, tokens, dim), jnp.float32),
        ],
        compiler_params=pltpu.CompilerParams(vmem_limit_bytes=VMEM_LIMIT),
        name="finish",
    )(queries, teacher, back, sums, *messages)


def on_device(queries, index, cand_owner, cand_row, neg_row, teacher):
    count, tokens, dim = queries.shape
    cands = cand_row.shape[1]
    shard = index.shape[0]
    owners = lax.axis_size("corpus")
    room = (2 * count * cands + owners - 1) // owners
    me = lax.axis_index("corpus").astype(jnp.int32)
    group = lax.axis_size("blk")

    def from_step(value, axis, size, step):
        return lax.ppermute(value, axis, [((i + step) % size, i) for i in range(size)])

    def gathered(value, axis, size):
        return [value] + [from_step(value, axis, size, step) for step in range(1, size)]

    code = cand_owner[..., 0] * shard + cand_row
    high = lax.reduce_precision(teacher, 8, 7)
    mid = lax.reduce_precision(teacher - high, 8, 7)
    low = lax.reduce_precision(teacher - high - mid, 8, 7)
    meta = [code // CODE, code % CODE, high, mid, low, jnp.zeros_like(low)]
    meta = [value.astype(jnp.bfloat16) for value in meta]
    meta = [jnp.concatenate(meta[k : k + 2], axis=1) for k in range(0, 6, 2)]
    message = jnp.concatenate([queries.reshape(count * tokens, dim)] + meta, axis=0)
    all_neg = jnp.concatenate(gathered(neg_row, "blk", group), axis=0).reshape(-1)
    told = jnp.broadcast_to(message[None], (owners,) + message.shape)
    told = lax.all_to_all(told, "corpus", split_axis=0, concat_axis=0, tiled=True)
    neg_acc, neg_sum = negatives(all_neg, queries, index)
    told, neg_acc = lax.optimization_barrier((told, neg_acc))
    rows, targets = prep(me.reshape(1), told, owners * count, shard, cands)
    index, told, rows = lax.optimization_barrier((index, told, rows))
    index, turned, inverse = load(index)
    messages = []
    order = list(reversed(range(owners)))
    groups = [order[first : first + SOURCES] for first in range(0, owners, SOURCES)]
    for steps in groups:
        sources = [jnp.bitwise_xor(me, step) for step in steps]
        found = pairs(
            sources, rows, targets, told, count, tokens, inverse, index, turned, cands, room
        )
        for step, message in zip(steps, found):
            if step:
                message = lax.ppermute(
                    message, "corpus", [(i, i ^ step) for i in range(owners)]
                )
            messages.append(message)
    losses, query_grads = finish(queries, teacher, neg_acc, neg_sum, messages)
    return (losses[:, 0], query_grads)


def solution(mesh):
    placed = (
        P(("corpus", "blk"), None, None),
        P("corpus", None, None),
        P(("corpus", "blk"), None, None),
        P(("corpus", "blk"), None),
        P(("corpus", "blk"), None),
        P(("corpus", "blk"), None),
    )
    return jax.shard_map(
        on_device,
        mesh=mesh,
        in_specs=placed,
        out_specs=(P(("corpus", "blk")), P(("corpus", "blk"), None, None)),
        check_vma=False,
    )
```
